256 devices in a mesh: ctx: 64 (over y, z, core), head: 4 (over x).
Axes of the slice: x: 4, y: 4, z: 8, core: 2. Of those that a mesh axis runs over, the one named last changes fastest.
Arguments:
- tokens: bfloat16 [32768, 2560], P('ctx', 'head'), may hold values from -6 to 6
- dt_decay: bfloat16 [32768, 2, 80], P('ctx', None, 'head'), may hold values from -0.8 to 0.06, as said below
- dest: int32 [32768], P('ctx'), may hold values from 0 to 32767, as said below
- lengths: int32 [128], replicated, may hold values from 1 to 16384, 32768 in all
- w_x: bfloat16 [2560, 5120], P(None, 'head'), may hold values from -0.125 to 0.125
- w_bc: bfloat16 [2560, 256], replicated, may hold values from -0.125 to 0.125
- conv_x: float32 [4, 5120], P(None, 'head'), may hold values from -3 to 3
- conv_bc: float32 [4, 256], replicated, may hold values from -3 to 3
- bias_x: float32 [5120], P('head'), may hold values from -0.5 to 0.5
- bias_bc: float32 [256], replicated, may hold values from -0.5 to 0.5
- skip: float32 [80], P('head'), may hold values from 0.5 to 1.5
Outputs:
- ssm_output: bfloat16 [32768, 5120], P('ctx', 'head')
The draws below stay inside these ranges and needn't reach their ends.
Inputs may be any that keep to these rules, and one draw needn't show every extreme that they name: dest is a permutation of the packed positions; loader row r lands on context shard dest[r] // 512. Of the 512 rows of one loader shard at most 16 land on one context shard, and exactly 16 land on one of them. Up to a relabelling of the context shards, every loader shard sends the same counts. The lengths sum to 32768; document d holds the positions from the sum of the first d lengths on. `dt_decay`: entry [r, 0, h] is a positive step size, entry [r, 1, h] a negative log decay.
All inputs are finite; a program needn't handle non-finite values.
Results may differ from the reference program's by a relative error of at most 0.0035.
Values may be sent and summed in bfloat16 or wider, within the bound.
No kernel may reach another device: no remote copies, remote signals or barrier semaphores. Data moves between devices by JAX's collectives and lax.ppermute only.
A program may use at most 128 MiB of HBM per device.

```python
import math
import jax
import jax.numpy as jnp
import numpy as np
from jax import lax

D = 2560
SSM_HEAD_TOTAL = 80
HEAD_DIM = 64
STATE = 128
CONV = 4
STRETCH = 256
TOK_DEV = 512
INNER = 5120
PACKED_TOKENS = 32768
DOCS = 128
N_CTX = 64


def draw_dest(key, part):
    key = jax.random.fold_in(key, 11)
    key_order, key_pairs, key_place, key_rows = jax.random.split(key, 4)
    groups = N_CTX
    mean_count = TOK_DEV // N_CTX
    shard_order = jax.random.permutation(key_order, groups).astype(jnp.int32)
    pair_sizes = jax.random.randint(key_pairs, ((groups - 2) // 2,), 0, mean_count + 1).astype(jnp.int32)
    offsets = jnp.concatenate([jnp.array([mean_count, -mean_count], jnp.int32), jnp.stack([pair_sizes, -pair_sizes], axis=1).reshape(groups - 2)])
    columns = jnp.arange(groups, dtype=jnp.int32)
    counts = mean_count + offsets[(columns[None, :] - shard_order[:, None]) % groups]
    count_ends = jnp.cumsum(counts, axis=1)
    sorted_rows = jnp.arange(TOK_DEV, dtype=jnp.int32)
    shard_of = jnp.sum((sorted_rows[None, :, None] >= count_ends[:, None, :]).astype(jnp.int32), axis=2)
    within = sorted_rows[None, :] - jnp.take_along_axis(count_ends - counts, shard_of, axis=1)
    before = jnp.cumsum(counts, axis=0) - counts
    slot_index = jnp.take_along_axis(before, shard_of, axis=1) + within

    def shuffle_rows(row_key):
        return jax.random.permutation(row_key, TOK_DEV).astype(jnp.int32)
    place_perm = jax.vmap(shuffle_rows)(jax.random.split(key_place, groups))
    local_place = place_perm[shard_of, slot_index]
    position = shard_of * TOK_DEV + local_place
    row_perm = jax.vmap(shuffle_rows)(jax.random.split(key_rows, groups))
    return jnp.take_along_axis(position, row_perm, axis=1).reshape(PACKED_TOKENS).astype(jnp.int32)


def draw_dt_decay(key, part):
    key = jax.random.fold_in(key, 23)
    selection_key, gradual_key, middle_key, quick_key, scale_key, stride_key, spike_key, depth_key = jax.random.split(key, 8)
    slow_share = 0.5
    fast_share = 0.25
    per_token_scale = jnp.exp(jax.random.uniform(scale_key, (PACKED_TOKENS, SSM_HEAD_TOTAL), minval=math.log(0.5), maxval=math.log(2.0)))
    step_scale = jnp.exp(jax.random.uniform(stride_key, (PACKED_TOKENS, SSM_HEAD_TOTAL), minval=math.log(0.5), maxval=math.log(2.0)))
    head_pick = jax.random.uniform(selection_key, (SSM_HEAD_TOTAL,))
    slow_rate = jnp.exp(jax.random.uniform(gradual_key, (SSM_HEAD_TOTAL,), minval=math.log(0.1 / PACKED_TOKENS), maxval=math.log(1.0 / PACKED_TOKENS)))
    medium_rate = jnp.exp(jax.random.uniform(middle_key, (SSM_HEAD_TOTAL,), minval=math.log(1.0 / 2000.0), maxval=math.log(1.0 / 200.0)))
    fast_rate = jnp.exp(jax.random.uniform(quick_key, (SSM_HEAD_TOTAL,), minval=math.log(1.0 / 50.0), maxval=math.log(1.0 / 30.0)))
    per_head_rate = jnp.where(head_pick < slow_share, slow_rate, jnp.where(head_pick < 1.0 - fast_share, medium_rate, fast_rate))
    spike_rows = jax.random.randint(spike_key, (3,), 0, PACKED_TOKENS)
    spike_mask = jnp.any(jnp.arange(PACKED_TOKENS)[:, None] == spike_rows[None, :], axis=1)
    spike_depth = jax.random.uniform(depth_key, (PACKED_TOKENS, SSM_HEAD_TOTAL), minval=0.22, maxval=0.69)
    logarithm_decay = -per_head_rate[None, :] * per_token_scale - jnp.where(spike_mask[:, None], spike_depth, 0.0)
    step_size = 0.15 * jnp.sqrt(per_head_rate)[None, :] * step_scale
    return jnp.stack([step_size, logarithm_decay], axis=1).astype(jnp.bfloat16)


def levels(key, extent, pieces, smallest, largest):
    loudness = 1.0
    for axis_at, parts in pieces:
        steps = jax.random.uniform(jax.random.fold_in(jax.random.fold_in(key, 6), axis_at), (parts,), jnp.float32, smallest / len(pieces), largest / len(pieces))
        loudness = loudness * jnp.repeat(jnp.exp(steps), extent[axis_at] // parts).reshape((-1,) + (1,) * (len(extent) - 1 - axis_at))
    return loudness


def length_profile(amount, total, limit, skew):
    loads = [(1 << 20) // math.isqrt(standing ** skew) + 1 for standing in range(2, amount + 1)]
    spare, given = total - limit - (amount - 1), [1] * (amount - 1)
    while spare > 0:
        free = [i for i in range(amount - 1) if given[i] < limit]
        mass, budget = sum([loads[i] for i in free]), spare
        for i in free:
            extra = min(limit - given[i], max(1, budget * loads[i] // mass), spare)
            given[i] = given[i] + extra
            spare = spare - extra
    return np.array([limit] + given)


def uneven_parts(own_key, number_of, total, reach, skew):
    if number_of == 2:
        one = jax.random.randint(own_key, (), max(1, total - reach), min(reach, total - 1) + 1)
        return jnp.stack([one, total - one])
    tallies = jnp.asarray(length_profile(number_of, total, reach, skew), jnp.int32)
    pairs = (number_of - 1) // 2
    giver, sink = tallies[1:1 + 2 * pairs:2], tallies[2:2 + 2 * pairs:2]
    margin = jnp.minimum(giver - 1, reach - sink)
    moved = jax.random.randint(jax.random.fold_in(own_key, 1), (pairs,), 0, 1 << 20) % (margin + 1)
    tallies = tallies.at[1:1 + 2 * pairs:2].set(giver - moved).at[2:2 + 2 * pairs:2].set(sink + moved)
    return tallies[jax.random.permutation(jax.random.fold_in(own_key, 2), number_of)]


def normal_values(own_key, dims, spread, most, shards=(), kind=jnp.bfloat16):
    drawn = spread * jax.random.normal(own_key, dims, jnp.float32)
    if shards:
        drawn = drawn * levels(own_key, dims, shards, -0.22, 0.18)
    return jnp.clip(drawn, -most, most).astype(kind)


def setup_inputs(seed: int = 0) -> dict:
    splits = jax.random.split(jax.random.key(seed), 12)
    tokens = normal_values(splits[0], (PACKED_TOKENS, D), 1.0, 6.0, ((0, 64), (1, 4)))
    dt_decay = draw_dt_decay(jax.random.fold_in(splits[11], 71), 0)
    dest = draw_dest(jax.random.fold_in(splits[11], 71), 0)
    lengths = uneven_parts(splits[3], DOCS, PACKED_TOKENS, PACKED_TOKENS // 2, 2).astype(jnp.int32)
    w_x = normal_values(splits[4], (D, INNER), D ** -0.5, 0.125, ((1, 4),))
    w_bc = normal_values(splits[5], (D, 2 * STATE), D ** -0.5, 0.125)
    conv_x = normal_values(splits[6], (CONV, INNER), CONV ** -0.5, 3.0, ((1, 4),), jnp.float32)
    conv_bc = normal_values(splits[7], (CONV, 2 * STATE), CONV ** -0.5, 3.0, (), jnp.float32)
    bias_x = jnp.clip(jax.random.uniform(splits[8], (INNER,), jnp.float32, -0.5, 0.5) * levels(splits[8], (INNER,), ((0, 4),), -0.4, 0.0), -0.5, 0.5)
    bias_bc = jnp.clip(jax.random.uniform(splits[9], (2 * STATE,), jnp.float32, -0.5, 0.5), -0.5, 0.5)
    skip = jnp.clip(0.5 + 1.0 * jax.random.uniform(splits[10], (SSM_HEAD_TOTAL,), jnp.float32) ** levels(splits[10], (SSM_HEAD_TOTAL,), ((0, 4),), -0.2, 0.2), 0.5, 1.5)
    return dict(tokens=tokens, dt_decay=dt_decay, dest=dest, lengths=lengths, w_x=w_x, w_bc=w_bc, conv_x=conv_x, conv_bc=conv_bc, bias_x=bias_x, bias_bc=bias_bc, skip=skip)


def causal_conv(extended, weight, bias, positions, doc_start):
    tap_count = weight.shape[0]
    row_count = positions.shape[0]
    running = jnp.zeros((row_count, extended.shape[1]), jnp.float32) + bias[None, :]
    for tap_index in range(tap_count):
        lag_rows = tap_count - 1 - tap_index
        shifted = extended[tap_index:tap_index + row_count]
        valid = (positions - lag_rows >= doc_start)[:, None]
        running = running + jnp.where(valid, weight[tap_index][None, :] * shifted, 0.0)
    return jax.nn.silu(running).astype(jnp.bfloat16)


def block_terms(inject, input_map, output_map, logarithm_decay, positions, doc_start):
    cumulative = jnp.cumsum(logarithm_decay, axis=0)
    first_pos = positions[0]
    scores = jnp.dot(output_map, input_map.T, preferred_element_type=jnp.float32)
    keep_mask = (positions[:, None] >= positions[None, :]) & (doc_start[:, None] <= positions[None, :])
    log_gap = jnp.where(keep_mask[:, :, None], cumulative[:, None, :] - cumulative[None, :, :], 0.0)
    weights = jnp.where(keep_mask[:, :, None], scores[:, :, None] * jnp.exp(log_gap), 0.0).astype(jnp.bfloat16)
    inner_part = jnp.einsum("tsh,shp->thp", weights.astype(jnp.float32), inject.astype(jnp.float32))
    tail_decay = jnp.where((doc_start[-1] <= positions)[:, None], jnp.exp(cumulative[-1][None, :] - cumulative), 0.0)
    decayed = (inject.astype(jnp.float32) * tail_decay[:, :, None]).astype(jnp.bfloat16)
    block_state = jnp.einsum("shp,sn->hpn", decayed.astype(jnp.float32), input_map.astype(jnp.float32))
    carry_decay = jnp.where(doc_start[-1] < first_pos, jnp.exp(cumulative[-1]), 0.0)
    enter_decay = jnp.where((doc_start < first_pos)[:, None], jnp.exp(cumulative), 0.0)
    return inner_part, enter_decay, block_state, carry_decay


def reference(tokens, dt_decay, dest, lengths, w_x, w_bc, conv_x, conv_bc, bias_x, bias_bc, skip):
    block_rows = min(STRETCH, TOK_DEV)
    block_count = PACKED_TOKENS // block_rows
    inner_proj = jnp.dot(tokens, w_x, preferred_element_type=jnp.float32).astype(jnp.bfloat16)
    state_proj = jnp.dot(tokens, w_bc, preferred_element_type=jnp.float32).astype(jnp.bfloat16)
    inner_packed = jnp.zeros_like(inner_proj).at[dest].set(inner_proj)
    state_packed = jnp.zeros_like(state_proj).at[dest].set(state_proj)
    step_packed = jnp.zeros_like(dt_decay).at[dest].set(dt_decay)
    starts = (jnp.cumsum(lengths) - lengths).astype(jnp.int32)
    positions = jnp.arange(PACKED_TOKENS, dtype=jnp.int32)
    doc_start = jnp.max(jnp.where(starts[None, :] <= positions[:, None], starts[None, :], 0), axis=1).astype(jnp.int32)
    lead_x = jnp.zeros((CONV - 1, inner_packed.shape[1]), jnp.bfloat16)
    lead_b = jnp.zeros((CONV - 1, state_packed.shape[1]), jnp.bfloat16)
    inner_conv = causal_conv(jnp.concatenate([lead_x, inner_packed], axis=0), conv_x, bias_x, positions, doc_start)
    state_conv = causal_conv(jnp.concatenate([lead_b, state_packed], axis=0), conv_bc, bias_bc, positions, doc_start)
    input_map = state_conv[:, :STATE]
    output_map = state_conv[:, STATE:]
    step_size = step_packed[:, 0, :].astype(jnp.float32)
    logarithm_decay = step_packed[:, 1, :].astype(jnp.float32)
    inner_heads = inner_conv.reshape(PACKED_TOKENS, SSM_HEAD_TOTAL, HEAD_DIM)
    inject = (inner_heads.astype(jnp.float32) * step_size[:, :, None]).astype(jnp.bfloat16)
    block_items = (
        inner_heads.reshape(block_count, block_rows, SSM_HEAD_TOTAL, HEAD_DIM),
        inject.reshape(block_count, block_rows, SSM_HEAD_TOTAL, HEAD_DIM),
        input_map.reshape(block_count, block_rows, STATE),
        output_map.reshape(block_count, block_rows, STATE),
        logarithm_decay.reshape(block_count, block_rows, SSM_HEAD_TOTAL),
        positions.reshape(block_count, block_rows),
        doc_start.reshape(block_count, block_rows),
    )

    def advance(carried, block_item):
        inner_rows, inject_rows, input_rows, output_rows, decay_rows, position_rows, start_rows = block_item
        inner_part, enter_decay, block_state, carry_decay = block_terms(inject_rows, input_rows, output_rows, decay_rows, position_rows, start_rows)
        outer_part = jnp.einsum("tn,hpn->thp", output_rows.astype(jnp.float32), carried, precision=lax.Precision.HIGHEST) * enter_decay[:, :, None]
        mixed_rows = (inner_part + outer_part + skip[None, :, None] * inner_rows).astype(jnp.bfloat16)
        return carry_decay[:, None, None] * carried + block_state, mixed_rows.reshape(block_rows, SSM_HEAD_TOTAL * HEAD_DIM)

    initial = jnp.zeros((SSM_HEAD_TOTAL, HEAD_DIM, STATE), jnp.float32)
    final_state, blocks_out = lax.scan(advance, initial, block_items)
    return blocks_out.reshape(PACKED_TOKENS, SSM_HEAD_TOTAL * HEAD_DIM)
```

```python
import functools

import jax
import jax.numpy as jnp
from jax import lax
from jax.experimental import pallas as pl
from jax.experimental.pallas import tpu as pltpu
from jax.sharding import PartitionSpec as P

BF = jnp.bfloat16
F32 = jnp.float32
CAP = 16
BLK = 256
HD = 64
TILE = 256
HALO = 16
VMEM_LIMIT = 48 * 1024 * 1024


def iota(shape, dim):
    return lax.broadcasted_iota(jnp.int32, shape, dim)


def mm(a, b):
    return jnp.dot(a, b, preferred_element_type=F32)


def mm_nt(a, b):
    return lax.dot_general(a, b, (((1,), (1,)), ((), ())), preferred_element_type=F32)


def mm_tn(a, b):
    return lax.dot_general(a, b, (((0,), (0,)), ((), ())), preferred_element_type=F32)


def as_bf(mask):
    return jnp.where(mask, 1.0, 0.0).astype(BF)


def lower_ones(n):
    return as_bf(iota((n, n), 0) >= iota((n, n), 1))


def params(flops=0, bytes_accessed=0):
    return dict(
        compiler_params=pltpu.CompilerParams(vmem_limit_bytes=VMEM_LIMIT),
        cost_estimate=pl.CostEstimate(
            flops=flops, bytes_accessed=bytes_accessed, transcendentals=0
        ),
    )


def pack_kernel(dest_ref, tok_ref, small_ref, out_ref, slot_ref):
    step = pl.program_id(0)
    rows = tok_ref.shape[0]
    groups = 64
    slots = out_ref.shape[0]

    @pl.when(step == 0)
    def _():
        dest = dest_ref[...]
        target = dest // rows
        onehot = iota((groups, rows), 0) == target
        upper = as_bf(iota((rows, rows), 0) <= iota((rows, rows), 1))
        ranks = mm(as_bf(onehot), upper)
        rank = jnp.sum(jnp.where(onehot, ranks, 0.0), axis=0, keepdims=True) - 1.0
        slot_ref[...] = target * CAP + rank.astype(jnp.int32)

    select = as_bf(iota((slots, rows), 0) + step * slots == slot_ref[...])
    width = tok_ref.shape[1]
    out_ref[:, :width] = mm(select, tok_ref[...]).astype(BF)
    out_ref[:, width:] = mm(select, small_ref[...]).astype(BF)


def pack(dest, tokens, small, groups):
    rows, width = tokens.shape
    steps = 8
    slots = groups * CAP // steps
    full = width + small.shape[1]
    return pl.pallas_call(
        pack_kernel,
        grid=(steps,),
        in_specs=[
            pl.BlockSpec((1, rows), lambda i: (0, 0)),
            pl.BlockSpec((rows, width), lambda i: (0, 0)),
            pl.BlockSpec((rows, small.shape[1]), lambda i: (0, 0)),
        ],
        out_specs=pl.BlockSpec((slots, full), lambda i: (i, 0)),
        out_shape=jax.ShapeDtypeStruct((groups * CAP, full), BF),
        scratch_shapes=[pltpu.VMEM((1, rows), jnp.int32)],
        name="pack",
        **params(2 * rows * groups * CAP * full, 4 * rows * full),
    )(dest, tokens, small)


def unpack_kernel(width, heads, recv_ref, tok_ref, small_ref, pos_ref):
    step = pl.program_id(0)
    rows = tok_ref.shape[0]
    slots = recv_ref.shape[0]

    @pl.when(step == 0)
    def _():
        lane = iota((8, 128), 1)
        pick = jnp.where(
            lane == 2 * heads, 256.0, jnp.where(lane == 2 * heads + 1, 1.0, 0.0)
        ).astype(BF)
        pos_ref[...] = mm_nt(pick, recv_ref[:, width:])[0:1].astype(jnp.int32)

    select = as_bf(iota((rows, slots), 0) + (step * rows + 1) == pos_ref[...])
    tok_ref[...] = mm(select, recv_ref[:, :width]).astype(BF)
    small_ref[...] = mm(select, recv_ref[:, width:]).astype(BF)


def unpack(recv, width, heads, rows):
    slots, full = recv.shape
    steps = 4
    return pl.pallas_call(
        functools.partial(unpack_kernel, width, heads),
        grid=(steps,),
        in_specs=[pl.BlockSpec((slots, full), lambda i: (0, 0))],
        out_specs=[
            pl.BlockSpec((rows // steps, width), lambda i: (i, 0)),
            pl.BlockSpec((rows // steps, full - width), lambda i: (i, 0)),
        ],
        out_shape=[
            jax.ShapeDtypeStruct((rows, width), BF),
            jax.ShapeDtypeStruct((rows, full - width), BF),
        ],
        scratch_shapes=[pltpu.VMEM((1, slots), jnp.int32)],
        name="unpack",
        **params(2 * rows * slots * full, 6 * rows * full),
    )(recv)


def conv_silu(ext, weight, bias, rel, rows):
    total = jnp.zeros((rows, ext.shape[1]), F32) + bias
    taps = weight.shape[0]
    for tap in range(taps):
        lag = taps - 1 - tap
        shifted = ext[HALO - lag : HALO - lag + rows]
        total = total + jnp.where(rel >= lag, weight[tap : tap + 1] * shifted, 0.0)
    return jax.nn.silu(total).astype(BF)


def head_spread(tile, first):
    per = TILE // HD
    return as_bf(iota((128, TILE), 0) == first + per * tile + iota((128, TILE), 1) // HD)


def front_kernel(heads, me_ref, *refs):
    xs, hs, ws, wbs = refs[0:4], refs[4:8], refs[8:12], refs[12:16]
    small_ref, rel_ref, cx_ref, bx_ref, cb_ref, bb_ref = refs[16:22]
    conv_ref, state_ref, mid_ref, in_ref, outmap_ref = refs[22:27]
    xe_ref = refs[27]
    tile = pl.program_id(0)
    rows = xs[0].shape[0]
    rel = rel_ref[...]
    states = in_ref.shape[1]

    def project(weights):
        total = mm(xe_ref[0], weights[0][0])
        for piece in range(1, 4):
            total = total + mm(xe_ref[piece], weights[piece][0])
        return total.astype(BF).astype(F32)

    @pl.when(tile == 0)
    def _():
        for piece in range(4):
            xe_ref[piece, :HALO] = hs[piece][...]
            xe_ref[piece, HALO:] = xs[piece][...]
        both = conv_silu(project(wbs), cb_ref[...], bb_ref[...], rel, rows)
        in_ref[...] = both[:, :states]
        outmap_ref[...] = both[:, states:]
        sums = []
        for block in range(rows // BLK):
            part = small_ref[block * BLK : (block + 1) * BLK]
            last = rel[(block + 1) * BLK - 1 : (block + 1) * BLK]
            total = mm(jnp.ones((8, BLK), BF), part)[0:1]
            sums.append(jnp.where(last > BLK - 1, jnp.exp(total), 0.0))
        reach = sums[0]
        for more in sums[1:]:
            reach = reach * more
        high = reach.astype(BF).astype(F32)
        low = reach - high
        even = iota((128, 128), 0) % 2 == 0
        lane = iota((128, 128), 1)
        keep = (lane >= heads) & (lane < 2 * heads)
        state_ref[:, heads * HD :] = jnp.where(keep, jnp.where(even, high, low), 0.0).astype(BF)

    inner = conv_silu(project(ws), cx_ref[...], bx_ref[...], rel, rows)
    conv_ref[...] = inner
    small = small_ref[...]
    steps = mm(small, head_spread(tile, 0))
    decays = mm(small, head_spread(tile, heads)).astype(BF)
    inject = (inner.astype(F32) * steps).astype(BF).astype(F32)
    ones = lower_ones(BLK)
    carried = None
    for block in range(rows // BLK):
        span = slice(block * BLK, (block + 1) * BLK)
        cumulative = mm(ones, decays[span])
        last = rel[(block + 1) * BLK - 1 : (block + 1) * BLK]
        end = cumulative[BLK - 1 : BLK]
        behind = BLK - 1 - iota((BLK, 1), 0)
        decayed = jnp.where(
            behind <= last, jnp.exp(end - cumulative) * inject[span], 0.0
        ).astype(BF)
        block_state = mm_tn(in_ref[span], decayed)
        carry = jnp.where(last > BLK - 1, jnp.exp(end), 0.0)
        if carried is None:
            carried = block_state
            mid_ref[...] = carried
        else:
            carried = carry * carried + block_state
    state_ref[:, pl.ds(pl.multiple_of(tile * TILE, TILE), TILE)] = carried.astype(BF)


def front(me, xs, hs, w_x, w_bc, small, rel, conv_x, bias_x, conv_bc, bias_bc):
    rows, width = xs[0].shape
    inner = w_x.shape[1]
    heads = inner // HD
    states = w_bc.shape[1] // 2
    tiles = inner // TILE
    w4 = w_x.reshape(4, width, inner)
    wb4 = w_bc.reshape(4, width, 2 * states)

    def whole(shape):
        return pl.BlockSpec(shape, lambda i, m: tuple(0 for _ in shape))

    in_specs = (
        [whole((rows, width))] * 4
        + [whole((HALO, width))] * 4
        + [
            pl.BlockSpec((1, width, TILE), lambda i, m, k=k: ((m[0] + 4 - k) % 4, 0, i))
            for k in range(4)
        ]
        + [
            pl.BlockSpec((1, width, 2 * states), lambda i, m, k=k: ((m[0] + 4 - k) % 4, 0, 0))
            for k in range(4)
        ]
        + [
            whole((rows, 128)),
            whole((rows, 1)),
            pl.BlockSpec((conv_x.shape[0], TILE), lambda i, m: (0, i)),
            pl.BlockSpec((1, TILE), lambda i, m: (0, i)),
            whole(conv_bc.shape),
            whole((1, 2 * states)),
        ]
    )
    out_specs = [
        pl.BlockSpec((rows, TILE), lambda i, m: (0, i)),
        whole((states, inner + 128)),
        pl.BlockSpec((states, TILE), lambda i, m: (0, i)),
        whole((rows, states)),
        whole((rows, states)),
    ]
    return pl.pallas_call(
        functools.partial(front_kernel, heads),
        grid_spec=pltpu.PrefetchScalarGridSpec(
            num_scalar_prefetch=1,
            grid=(tiles,),
            in_specs=in_specs,
            out_specs=out_specs,
            scratch_shapes=[pltpu.VMEM((4, rows + HALO, width), BF)],
        ),
        out_shape=[
            jax.ShapeDtypeStruct((rows, inner), BF),
            jax.ShapeDtypeStruct((states, inner + 128), BF),
            jax.ShapeDtypeStruct((states, inner), F32),
            jax.ShapeDtypeStruct((rows, states), BF),
            jax.ShapeDtypeStruct((rows, states), BF),
        ],
        name="front",
        **params(2 * rows * 4 * width * (inner + 2 * states), 12_000_000),
    )(
        me, *xs, *hs, w4, w4, w4, w4, wb4, wb4, wb4, wb4,
        small, rel, conv_x, bias_x, conv_bc, bias_bc,
    )


def inner_kernel(
    heads, small_ref, rel_ref, in_ref, outmap_ref, conv_ref, mid_ref, skip_ref,
    part_ref, scores_ref, across_ref,
):
    tile = pl.program_id(0)
    rows = conv_ref.shape[0]
    per = TILE // HD
    ones = lower_ones(BLK)

    @pl.when(tile == 0)
    def _():
        for block in range(rows // BLK):
            span = slice(block * BLK, (block + 1) * BLK)
            scores = mm_nt(outmap_ref[span], in_ref[span])
            gap = iota((BLK, BLK), 0) - iota((BLK, BLK), 1)
            keep = (gap >= 0) & (gap <= rel_ref[span])
            scores_ref[block] = jnp.where(keep, scores, 0.0)
            across_ref[block] = mm(ones, small_ref[span]).T

    small = small_ref[...]
    steps = mm(small, head_spread(tile, 0))
    decays = mm(small, head_spread(tile, heads)).astype(BF)
    conv = conv_ref[...].astype(F32)
    inject = (conv * steps).astype(BF)
    lane_head = iota((BLK, TILE), 1) // HD
    for block in range(rows // BLK):
        span = slice(block * BLK, (block + 1) * BLK)
        cumulative = mm(ones, decays[span])
        scores = scores_ref[block]
        total = skip_ref[...] * conv[span]
        if block > 0:
            enter = jnp.where(
                iota((BLK, 1), 0) < rel_ref[span], jnp.exp(cumulative), 0.0
            )
            total = total + enter * mm(outmap_ref[span], mid_ref[...].astype(BF))
        for q in range(per):
            down = cumulative[:, q * HD : q * HD + 1]
            across = across_ref[block, pl.ds(heads + per * tile + q, 1), :]
            weights = (scores * jnp.exp(jnp.minimum(down - across, 0.0))).astype(BF)
            mine = jnp.where(lane_head == q, inject[span], jnp.zeros((), BF))
            total = total + mm(weights, mine)
        part_ref[span] = total


def inner_part(small, rel, input_map, output_map, conv, mid, skip_wide):
    rows, inner = conv.shape
    states = input_map.shape[1]
    heads = inner // HD
    blocks = rows // BLK

    def whole(shape):
        return pl.BlockSpec(shape, lambda i: tuple(0 for _ in shape))

    return pl.pallas_call(
        functools.partial(inner_kernel, heads),
        grid=(inner // TILE,),
        in_specs=[
            whole((rows, 128)),
            whole((rows, 1)),
            whole((rows, states)),
            whole((rows, states)),
            pl.BlockSpec((rows, TILE), lambda i: (0, i)),
            pl.BlockSpec((states, TILE), lambda i: (0, i)),
            pl.BlockSpec((1, TILE), lambda i: (0, i)),
        ],
        out_specs=pl.BlockSpec((rows, TILE), lambda i: (0, i)),
        out_shape=jax.ShapeDtypeStruct((rows, inner), F32),
        scratch_shapes=[
            pltpu.VMEM((blocks, BLK, BLK), F32),
            pltpu.VMEM((blocks, 128, BLK), F32),
        ],
        name="inner_part",
        **params(8 * rows * BLK * inner, 8_000_000),
    )(small, rel, input_map, output_map, conv, mid, skip_wide)


def scan_kernel(heads, recv_ref, out_ref, gain_ref, add_ref, enter_ref):
    count, inner = out_ref.shape
    codes = recv_ref[:, inner:]
    spread = as_bf(iota((128, inner), 0) == heads + iota((128, inner), 1) // HD)
    row, column = iota((count, count), 0), iota((count, count), 1)
    first = row // 2 * 2
    high = mm(as_bf(column == first), codes).astype(BF)
    low = mm(as_bf(column == first + 1), codes).astype(BF)
    gain_ref[...] = mm(high, spread) + mm(low, spread)
    add_ref[...] = recv_ref[:, :inner].astype(F32)

    def body(group, state):
        rows = pl.ds(pl.multiple_of(group * 8, 8), 8)
        gains, adds = gain_ref[rows], add_ref[rows]
        entered = []
        for pair in range(4):
            span = slice(2 * pair, 2 * pair + 2)
            entered.append(state)
            state = gains[span] * state + adds[span]
        enter_ref[rows] = jnp.concatenate(entered, axis=0)
        return state

    lax.fori_loop(0, count // 8, body, jnp.zeros((2, inner), F32))
    out_ref[...] = enter_ref[...].astype(BF)


def scan_shards(recv, heads):
    count, full = recv.shape
    inner = heads * HD
    return pl.pallas_call(
        functools.partial(scan_kernel, heads),
        out_shape=jax.ShapeDtypeStruct((count, inner), BF),
        scratch_shapes=[pltpu.VMEM((count, inner), F32)] * 3,
        name="scan_shards",
        **params(4 * count * 128 * inner, 700_000),
    )(recv)


def final_kernel(heads, small_ref, rel_ref, outmap_ref, part_ref, enter_ref, out_ref):
    tile = pl.program_id(0)
    rows = part_ref.shape[0]
    decays = mm(small_ref[...], head_spread(tile, heads)).astype(BF)
    cumulative = mm(lower_ones(rows), decays)
    gain = jnp.where(iota((rows, 1), 0) < rel_ref[...], jnp.exp(cumulative), 0.0)
    outer = mm(outmap_ref[...], enter_ref[...])
    out_ref[...] = (part_ref[...] + gain * outer).astype(BF)


def final(small, rel, output_map, part, enter):
    rows, inner = part.shape
    states = output_map.shape[1]

    def whole(shape):
        return pl.BlockSpec(shape, lambda i: tuple(0 for _ in shape))

    return pl.pallas_call(
        functools.partial(final_kernel, inner // HD),
        grid=(inner // TILE,),
        in_specs=[
            whole((rows, 128)),
            whole((rows, 1)),
            whole((rows, states)),
            pl.BlockSpec((rows, TILE), lambda i: (0, i)),
            pl.BlockSpec((states, TILE), lambda i: (0, i)),
        ],
        out_specs=pl.BlockSpec((rows, TILE), lambda i: (0, i)),
        out_shape=jax.ShapeDtypeStruct((rows, inner), BF),
        name="final",
        **params(2 * rows * rows * inner, 5_000_000),
    )(small, rel, output_map, part, enter)


def on_device(tokens, dt_decay, dest, lengths, w_x, w_bc, conv_x, conv_bc, bias_x, bias_bc, skip):
    rows, width = tokens.shape
    groups = lax.axis_size("ctx")
    ring = lax.axis_size("head")
    heads = dt_decay.shape[2]
    inner = w_x.shape[1]
    first_pos = lax.axis_index("ctx") * rows

    place = dest % rows + 1
    small = jnp.concatenate(
        [
            dt_decay.reshape(rows, 2 * heads),
            (place // 256).astype(BF)[:, None],
            (place % 256).astype(BF)[:, None],
            jnp.zeros((rows, 128 - 2 * heads - 2), BF),
        ],
        axis=1,
    )
    sent = pack(dest[None, :], tokens, small, groups)
    arrived = lax.all_to_all(
        sent.reshape(groups, CAP, width + 128), "ctx", split_axis=0, concat_axis=0, tiled=True
    ).reshape(groups * CAP, width + 128)
    mine, small = unpack(arrived, width, heads, rows)

    def turned(x, by):
        return lax.ppermute(x, "head", [(i, (i + by) % ring) for i in range(ring)])

    halo = lax.ppermute(
        mine[rows - HALO :], "ctx", [(i, i + 1) for i in range(groups - 1)]
    )
    xs = [mine] + [turned(mine, by) for by in (1, 2, 3)]
    hs = [halo] + [turned(halo, by) for by in (1, 2, 3)]

    starts = jnp.cumsum(lengths) - lengths
    positions = first_pos + jnp.arange(rows, dtype=jnp.int32)
    doc_start = jnp.max(
        jnp.where(starts[None, :] <= positions[:, None], starts[None, :], 0), axis=1
    )
    rel = (positions - doc_start)[:, None]
    me = lax.axis_index("head").astype(jnp.int32)[None]
    conv, state, mid, input_map, output_map = front(
        me, xs, hs, w_x, w_bc, small, rel, conv_x, bias_x[None, :], conv_bc, bias_bc[None, :]
    )
    states = input_map.shape[1]
    share = states // groups
    gathered = lax.all_to_all(
        state.reshape(groups, share, inner + 128), "ctx", split_axis=0, concat_axis=0, tiled=True
    ).reshape(states, inner + 128)
    part = inner_part(
        small, rel, input_map, output_map, conv, mid, jnp.repeat(skip, HD)[None, :]
    )
    entering = scan_shards(gathered, heads)
    enter = lax.all_to_all(
        entering.reshape(groups, share, inner), "ctx", split_axis=0, concat_axis=0, tiled=True
    ).reshape(states, inner)
    return final(small, rel, output_map, part, enter)


def solution(mesh):
    in_specs = (
        P("ctx", "head"),
        P("ctx", None, "head"),
        P("ctx"),
        P(),
        P(None, "head"),
        P(),
        P(None, "head"),
        P(),
        P("head"),
        P(),
        P("head"),
    )
    out_specs = P("ctx", "head")
    return jax.shard_map(
        on_device, mesh=mesh, in_specs=in_specs, out_specs=out_specs, check_vma=False
    )
```

```python
import functools

import jax
import jax.numpy as jnp
from jax import lax
from jax.experimental import pallas as pl
from jax.experimental.pallas import tpu as pltpu
from jax.sharding import PartitionSpec as P

BF = jnp.bfloat16
F32 = jnp.float32
CAP = 16
BLK = 256
HD = 64
TILE = 256
HALO = 16
VMEM_LIMIT = 60 * 1024 * 1024
LANES = 128
ROWS_SENT = 88
HIGH_AT, LOW_AT = 40, 104


def iota(shape, dim):
    return lax.broadcasted_iota(jnp.int32, shape, dim)


def mm(a, b):
    return jnp.dot(a, b, preferred_element_type=F32)


def mm_nt(a, b):
    return lax.dot_general(a, b, (((1,), (1,)), ((), ())), preferred_element_type=F32)


def mm_tn(a, b):
    return lax.dot_general(a, b, (((0,), (0,)), ((), ())), preferred_element_type=F32)


def as_bf(mask):
    return jnp.where(mask, 1.0, 0.0).astype(BF)


def lower_ones(n):
    return as_bf(iota((n, n), 0) >= iota((n, n), 1))


def params(flops=0, bytes_accessed=0):
    return dict(
        compiler_params=pltpu.CompilerParams(vmem_limit_bytes=VMEM_LIMIT),
        cost_estimate=pl.CostEstimate(
            flops=flops, bytes_accessed=bytes_accessed, transcendentals=0
        ),
    )


def pack_kernel(dest_ref, tok_ref, steps_ref, out_ref, slot_ref, code_ref, small_ref):
    step = pl.program_id(0)
    rows, width = tok_ref.shape
    groups = code_ref.shape[0]
    per = out_ref.shape[0]
    slots = per * CAP

    @pl.when(step == 0)
    def _():
        dest = dest_ref[...]
        target = dest // rows
        place = dest % rows + 1
        onehot = iota((groups, rows), 0) == target
        upper = as_bf(iota((rows, rows), 0) <= iota((rows, rows), 1))
        ranks = mm(as_bf(onehot), upper)
        rank = jnp.sum(jnp.where(onehot, ranks, 0.0), axis=0, keepdims=True) - 1.0
        rank = rank.astype(jnp.int32)
        slot_ref[...] = target * CAP + rank
        line = iota((LANES, rows), 0)
        codes = jnp.where(line == HIGH_AT + rank, place // 256, 0)
        codes = codes + jnp.where(line == LOW_AT + rank, place % 256, 0)
        code_ref[...] = mm_nt(as_bf(onehot), codes.astype(F32).astype(BF))
        small_ref[...] = jnp.zeros_like(small_ref)
        small_ref[:, : steps_ref.shape[1]] = steps_ref[...]

    slot = slot_ref[...] - step * slots
    sent = mm(as_bf(iota((slots, rows), 0) == slot), tok_ref[...]).astype(BF)
    for column in range(width // LANES):
        out_ref[:, column * CAP : (column + 1) * CAP, :] = sent[
            :, column * LANES : (column + 1) * LANES
        ].reshape(per, CAP, LANES)
    half = CAP // 2
    line = iota((per * half, rows), 0)
    line = line + line // half * half
    small = small_ref[...]
    pairs = mm(as_bf(line == slot), small)
    pairs = pairs + pltpu.roll(mm(as_bf(line + half == slot), small), LANES // 2, 1)
    pairs = pairs.reshape(per, half, LANES)
    codes = code_ref[pl.ds(pl.multiple_of(step * per, per), per)]
    first = iota((per, half, LANES), 1) == 0
    pairs = pairs + jnp.where(first, codes[:, None, :], 0.0)
    out_ref[:, ROWS_SENT - half :, :] = pairs.astype(BF)


def pack(dest, tokens, steps, groups):
    rows, width = tokens.shape
    count = 8
    per = groups // count
    return pl.pallas_call(
        pack_kernel,
        grid=(count,),
        in_specs=[
            pl.BlockSpec((1, rows), lambda i: (0, 0)),
            pl.BlockSpec((rows, width), lambda i: (0, 0)),
            pl.BlockSpec(steps.shape, lambda i: (0, 0)),
        ],
        out_specs=pl.BlockSpec((per, ROWS_SENT, LANES), lambda i: (i, 0, 0)),
        out_shape=jax.ShapeDtypeStruct((groups, ROWS_SENT, LANES), BF),
        scratch_shapes=[
            pltpu.VMEM((1, rows), jnp.int32),
            pltpu.VMEM((groups, LANES), F32),
            pltpu.VMEM((rows, LANES), BF),
        ],
        name="pack",
        **params(2 * rows * groups * CAP * (width + LANES), 4 * rows * width),
    )(dest, tokens, steps)


def unpack_kernel(
    heads, recv_ref, low_ref, high_ref, small_ref, pos_ref, first_ref, second_ref, mixed_ref
):
    step = pl.program_id(0)
    groups = recv_ref.shape[0]
    half = CAP // 2
    rows, width = low_ref.shape

    def places(row_codes, lane_slot, lane_group, count):
        line = iota((LANES, count), 0)
        table = jnp.where(
            line == HIGH_AT + lane_slot, 256.0, jnp.where(line == LOW_AT + lane_slot, 1.0, 0.0)
        ).astype(BF)
        wide = mm(row_codes, table)
        mine = iota((groups, count), 0) == lane_group
        return jnp.sum(jnp.where(mine, wide, 0.0), axis=0, keepdims=True).astype(jnp.int32)

    @pl.when(step == 0)
    def _():
        small = recv_ref[:, ROWS_SENT - half :, :].astype(F32)
        mixed_ref[...] = small.reshape(groups * half, LANES).astype(BF)
        codes = small[:, 0, :].astype(BF)
        lane = iota((1, groups * CAP), 1)
        pos_ref[...] = places(codes, lane % CAP, lane // CAP, groups * CAP)
        lane = iota((1, groups * half), 1)
        first_ref[...] = places(codes, lane % half, lane // half, groups * half)
        second_ref[...] = places(codes, lane % half + half, lane // half, groups * half)

    def pick(ref):
        count = ref.shape[1]
        return as_bf(iota((rows, count), 0) + (step * rows + 1) == ref[...])

    select = pick(pos_ref)
    taken = []
    for column in range(width // LANES):
        source = recv_ref[:, column * CAP : (column + 1) * CAP, :].reshape(groups * CAP, LANES)
        taken.append(mm(select, source).astype(BF))
    taken = jnp.concatenate(taken, axis=1)

    @pl.when(step == 0)
    def _():
        low_ref[...] = taken

    @pl.when(step == 1)
    def _():
        high_ref[...] = taken

    mixed = mixed_ref[...]
    small = mm(pick(first_ref), mixed)
    turned = pltpu.roll(mm(pick(second_ref), mixed), LANES // 2, 1)
    valid = iota((rows, LANES), 1) < 2 * heads
    small_ref[...] = jnp.where(valid, small + turned, 0.0).astype(BF)


def unpack(recv, width, heads, rows):
    groups = recv.shape[0]
    half_rows = rows // 2
    half_slots = groups * CAP // 2
    return pl.pallas_call(
        functools.partial(unpack_kernel, heads),
        grid=(2,),
        in_specs=[pl.BlockSpec(recv.shape, lambda i: (0, 0, 0))],
        out_specs=[
            pl.BlockSpec((half_rows, width), lambda i: (0, 0)),
            pl.BlockSpec((half_rows, width), lambda i: (0, 0)),
            pl.BlockSpec((half_rows, LANES), lambda i: (i, 0)),
        ],
        out_shape=[
            jax.ShapeDtypeStruct((half_rows, width), BF),
            jax.ShapeDtypeStruct((half_rows, width), BF),
            jax.ShapeDtypeStruct((rows, LANES), BF),
        ],
        scratch_shapes=[
            pltpu.VMEM((1, groups * CAP), jnp.int32),
            pltpu.VMEM((1, half_slots), jnp.int32),
            pltpu.VMEM((1, half_slots), jnp.int32),
            pltpu.VMEM((half_slots, LANES), BF),
        ],
        name="unpack",
        **params(2 * rows * groups * CAP * width, 6 * rows * width),
    )(recv)


def conv_silu(ext, weight, bias, rel, rows):
    total = jnp.zeros((rows, ext.shape[1]), F32) + bias
    taps = weight.shape[0]
    for tap in range(taps):
        lag = taps - 1 - tap
        shifted = ext[HALO - lag : HALO - lag + rows]
        total = total + jnp.where(rel >= lag, weight[tap : tap + 1] * shifted, 0.0)
    return jax.nn.silu(total).astype(BF)


def head_spread(tile, first):
    per = TILE // HD
    return as_bf(iota((128, TILE), 0) == first + per * tile + iota((128, TILE), 1) // HD)


def front_kernel(heads, me_ref, *refs):
    lows, highs, ws, wbs = refs[0:4], refs[4:8], refs[8:12], refs[12:16]
    small_ref, rel_ref, cx_ref, bx_ref, cb_ref, bb_ref = refs[16:22]
    conv_ref, state_ref, mid_ref, in_ref, outmap_ref = refs[22:27]
    xe_ref, acc_ref, sems = refs[27:30]
    step = pl.program_id(0)
    tiles = pl.num_programs(0) - 1
    half = lows[0].shape[0]
    rows = 2 * half
    states = in_ref.shape[1]

    def project(weights):
        total = mm(xe_ref[0], weights[0][0])
        for piece in range(1, 4):
            total = total + mm(xe_ref[piece], weights[piece][0])
        return total

    def begin():
        copies = []
        for piece in range(4):
            xe = xe_ref.at[piece]
            for at, (source, target) in enumerate(
                (
                    (lows[piece], xe.at[pl.ds(HALO, half)]),
                    (highs[piece].at[pl.ds(0, HALO)], xe.at[pl.ds(0, HALO)]),
                    (highs[piece].at[pl.ds(HALO, half)], xe.at[pl.ds(HALO + half, half)]),
                )
            ):
                copy = pltpu.make_async_copy(source, target, sems.at[piece, at])
                copy.start()
                copies.append(copy)
        for copy in copies:
            copy.wait()
        rel = rel_ref[...]
        ext = project(wbs).astype(BF).astype(F32)
        both = conv_silu(ext, cb_ref[...], bb_ref[...], rel, rows)
        in_ref[...] = both[:, :states]
        outmap_ref[...] = both[:, states:]
        sums = []
        for block in range(rows // BLK):
            part = small_ref[block * BLK : (block + 1) * BLK]
            last = rel[(block + 1) * BLK - 1 : (block + 1) * BLK]
            total = mm(jnp.ones((8, BLK), BF), part)[0:1]
            sums.append(jnp.where(last > BLK - 1, jnp.exp(total), 0.0))
        reach = sums[0]
        for more in sums[1:]:
            reach = reach * more
        high = reach.astype(BF).astype(F32)
        low = reach - high
        even = iota((128, 128), 0) % 2 == 0
        lane = iota((128, 128), 1)
        keep = (lane >= heads) & (lane < 2 * heads)
        state_ref[:, heads * HD :] = jnp.where(keep, jnp.where(even, high, low), 0.0).astype(BF)

    def finish():
        tile = step - 1
        rel = rel_ref[...]
        ext = acc_ref[tile % 2].astype(BF).astype(F32)
        inner = conv_silu(ext, cx_ref[...], bx_ref[...], rel, rows)
        conv_ref[...] = inner
        small = small_ref[...]
        steps = mm(small, head_spread(tile, 0))
        decays = mm(small, head_spread(tile, heads)).astype(BF)
        inject = (inner.astype(F32) * steps).astype(BF).astype(F32)
        ones = lower_ones(BLK)
        carried = None
        for block in range(rows // BLK):
            span = slice(block * BLK, (block + 1) * BLK)
            cumulative = mm(ones, decays[span])
            last = rel[(block + 1) * BLK - 1 : (block + 1) * BLK]
            end = cumulative[BLK - 1 : BLK]
            behind = BLK - 1 - iota((BLK, 1), 0)
            decayed = jnp.where(
                behind <= last, jnp.exp(end - cumulative) * inject[span], 0.0
            ).astype(BF)
            block_state = mm_tn(in_ref[span], decayed)
            carry = jnp.where(last > BLK - 1, jnp.exp(end), 0.0)
            if carried is None:
                carried = block_state
                mid_ref[...] = carried
            else:
                carried = carry * carried + block_state
        state_ref[:, pl.ds(pl.multiple_of(tile * TILE, TILE), TILE)] = carried.astype(BF)

    @pl.when(step == 0)
    def _():
        begin()
        acc_ref[0] = project(ws)

    @pl.when((step > 0) & (step < tiles))
    def _():
        finish()
        acc_ref[step % 2] = project(ws)

    @pl.when(step == tiles)
    def _():
        finish()


def front(me, lows, highs, w_x, w_bc, small, rel, conv_x, bias_x, conv_bc, bias_bc):
    half, width = lows[0].shape
    rows = 2 * half
    inner = w_x.shape[1]
    heads = inner // HD
    states = w_bc.shape[1] // 2
    tiles = inner // TILE
    w4 = w_x.reshape(4, width, inner)
    wb4 = w_bc.reshape(4, width, 2 * states)

    def whole(shape):
        return pl.BlockSpec(shape, lambda i, m: tuple(0 for _ in shape))

    def ahead(i):
        return jnp.minimum(i, tiles - 1)

    def behind(i):
        return jnp.maximum(i - 1, 0)

    in_specs = (
        [pl.BlockSpec(memory_space=pltpu.HBM)] * 8
        + [
            pl.BlockSpec(
                (1, width, TILE), lambda i, m, k=k: ((m[0] + 4 - k) % 4, 0, ahead(i))
            )
            for k in range(4)
        ]
        + [
            pl.BlockSpec((1, width, 2 * states), lambda i, m, k=k: ((m[0] + 4 - k) % 4, 0, 0))
            for k in range(4)
        ]
        + [
            whole((rows, 128)),
            whole((rows, 1)),
            pl.BlockSpec((conv_x.shape[0], TILE), lambda i, m: (0, behind(i))),
            pl.BlockSpec((1, TILE), lambda i, m: (0, behind(i))),
            whole(conv_bc.shape),
            whole((1, 2 * states)),
        ]
    )
    out_specs = [
        pl.BlockSpec((rows, TILE), lambda i, m: (0, behind(i))),
        whole((states, inner + 128)),
        pl.BlockSpec((states, TILE), lambda i, m: (0, behind(i))),
        whole((rows, states)),
        whole((rows, states)),
    ]
    return pl.pallas_call(
        functools.partial(front_kernel, heads),
        grid_spec=pltpu.PrefetchScalarGridSpec(
            num_scalar_prefetch=1,
            grid=(tiles + 1,),
            in_specs=in_specs,
            out_specs=out_specs,
            scratch_shapes=[
                pltpu.VMEM((4, rows + HALO, width), BF),
                pltpu.VMEM((2, rows + HALO, TILE), F32),
                pltpu.SemaphoreType.DMA((4, 3)),
            ],
        ),
        out_shape=[
            jax.ShapeDtypeStruct((rows, inner), BF),
            jax.ShapeDtypeStruct((states, inner + 128), BF),
            jax.ShapeDtypeStruct((states, inner), F32),
            jax.ShapeDtypeStruct((rows, states), BF),
            jax.ShapeDtypeStruct((rows, states), BF),
        ],
        name="front",
        **params(2 * rows * 4 * width * (inner + 2 * states), 12_000_000),
    )(
        me, *lows, *highs, w4, w4, w4, w4, wb4, wb4, wb4, wb4,
        small, rel, conv_x, bias_x, conv_bc, bias_bc,
    )


def inner_kernel(
    heads, small_ref, rel_ref, in_ref, outmap_ref, conv_ref, mid_ref, skip_ref,
    part_ref, scores_ref, across_ref,
):
    tile = pl.program_id(0)
    rows = conv_ref.shape[0]
    per = TILE // HD
    ones = lower_ones(BLK)

    @pl.when(tile == 0)
    def _():
        for block in range(rows // BLK):
            span = slice(block * BLK, (block + 1) * BLK)
            scores = mm_nt(outmap_ref[span], in_ref[span])
            gap = iota((BLK, BLK), 0) - iota((BLK, BLK), 1)
            keep = (gap >= 0) & (gap <= rel_ref[span])
            scores_ref[block] = jnp.where(keep, scores, 0.0)
            across_ref[block] = mm(ones, small_ref[span]).T

    small = small_ref[...]
    steps = mm(small, head_spread(tile, 0))
    decays = mm(small, head_spread(tile, heads)).astype(BF)
    conv = conv_ref[...].astype(F32)
    inject = (conv * steps).astype(BF)
    lane_head = iota((BLK, TILE), 1) // HD
    for block in range(rows // BLK):
        span = slice(block * BLK, (block + 1) * BLK)
        cumulative = mm(ones, decays[span])
        scores = scores_ref[block]
        total = skip_ref[...] * conv[span]
        if block > 0:
            enter = jnp.where(
                iota((BLK, 1), 0) < rel_ref[span], jnp.exp(cumulative), 0.0
            )
            total = total + enter * mm(outmap_ref[span], mid_ref[...].astype(BF))
        for q in range(per):
            down = cumulative[:, q * HD : q * HD + 1]
            across = across_ref[block, pl.ds(heads + per * tile + q, 1), :]
            weights = (scores * jnp.exp(jnp.minimum(down - across, 0.0))).astype(BF)
            mine = jnp.where(lane_head == q, inject[span], jnp.zeros((), BF))
            total = total + mm(weights, mine)
        part_ref[span] = total


def inner_part(small, rel, input_map, output_map, conv, mid, skip_wide):
    rows, inner = conv.shape
    states = input_map.shape[1]
    heads = inner // HD
    blocks = rows // BLK

    def whole(shape):
        return pl.BlockSpec(shape, lambda i: tuple(0 for _ in shape))

    return pl.pallas_call(
        functools.partial(inner_kernel, heads),
        grid=(inner // TILE,),
        in_specs=[
            whole((rows, 128)),
            whole((rows, 1)),
            whole((rows, states)),
            whole((rows, states)),
            pl.BlockSpec((rows, TILE), lambda i: (0, i)),
            pl.BlockSpec((states, TILE), lambda i: (0, i)),
            pl.BlockSpec((1, TILE), lambda i: (0, i)),
        ],
        out_specs=pl.BlockSpec((rows, TILE), lambda i: (0, i)),
        out_shape=jax.ShapeDtypeStruct((rows, inner), F32),
        scratch_shapes=[
            pltpu.VMEM((blocks, BLK, BLK), F32),
            pltpu.VMEM((blocks, 128, BLK), F32),
        ],
        name="inner_part",
        **params(8 * rows * BLK * inner, 8_000_000),
    )(small, rel, input_map, output_map, conv, mid, skip_wide)


def scan_kernel(heads, recv_ref, out_ref, gain_ref, add_ref, enter_ref):
    count, inner = out_ref.shape
    codes = recv_ref[:, inner:]
    spread = as_bf(iota((128, inner), 0) == heads + iota((128, inner), 1) // HD)
    row, column = iota((count, count), 0), iota((count, count), 1)
    first = row // 2 * 2
    high = mm(as_bf(column == first), codes).astype(BF)
    low = mm(as_bf(column == first + 1), codes).astype(BF)
    gain_ref[...] = mm(high, spread) + mm(low, spread)
    add_ref[...] = recv_ref[:, :inner].astype(F32)

    def body(group, state):
        rows = pl.ds(pl.multiple_of(group * 8, 8), 8)
        gains, adds = gain_ref[rows], add_ref[rows]
        entered = []
        for pair in range(4):
            span = slice(2 * pair, 2 * pair + 2)
            entered.append(state)
            state = gains[span] * state + adds[span]
        enter_ref[rows] = jnp.concatenate(entered, axis=0)
        return state

    lax.fori_loop(0, count // 8, body, jnp.zeros((2, inner), F32))
    out_ref[...] = enter_ref[...].astype(BF)


def scan_shards(recv, heads):
    count, full = recv.shape
    inner = heads * HD
    return pl.pallas_call(
        functools.partial(scan_kernel, heads),
        out_shape=jax.ShapeDtypeStruct((count, inner), BF),
        scratch_shapes=[pltpu.VMEM((count, inner), F32)] * 3,
        name="scan_shards",
        **params(4 * count * 128 * inner, 700_000),
    )(recv)


def final_kernel(
    heads, small_ref, rel_ref, outmap_ref, part_ref, enter_ref, out_ref, ones_ref
):
    tile = pl.program_id(0)
    rows = part_ref.shape[0]

    @pl.when(tile == 0)
    def _():
        ones_ref[...] = lower_ones(rows)

    decays = mm(small_ref[...], head_spread(tile, heads)).astype(BF)
    cumulative = mm(ones_ref[...], decays)
    gain = jnp.where(iota((rows, 1), 0) < rel_ref[...], jnp.exp(cumulative), 0.0)
    outer = mm(outmap_ref[...], enter_ref[...])
    out_ref[...] = (part_ref[...] + gain * outer).astype(BF)


def final(small, rel, output_map, part, enter):
    rows, inner = part.shape
    states = output_map.shape[1]

    def whole(shape):
        return pl.BlockSpec(shape, lambda i: tuple(0 for _ in shape))

    return pl.pallas_call(
        functools.partial(final_kernel, inner // HD),
        grid=(inner // TILE,),
        in_specs=[
            whole((rows, 128)),
            whole((rows, 1)),
            whole((rows, states)),
            pl.BlockSpec((rows, TILE), lambda i: (0, i)),
            pl.BlockSpec((states, TILE), lambda i: (0, i)),
        ],
        out_specs=pl.BlockSpec((rows, TILE), lambda i: (0, i)),
        out_shape=jax.ShapeDtypeStruct((rows, inner), BF),
        scratch_shapes=[pltpu.VMEM((rows, rows), BF)],
        name="final",
        **params(2 * rows * rows * inner, 5_000_000),
    )(small, rel, output_map, part, enter)


def on_device(tokens, dt_decay, dest, lengths, w_x, w_bc, conv_x, conv_bc, bias_x, bias_bc, skip):
    rows, width = tokens.shape
    groups = lax.axis_size("ctx")
    ring = lax.axis_size("head")
    heads = dt_decay.shape[2]
    inner = w_x.shape[1]
    first_pos = lax.axis_index("ctx") * rows

    sent = pack(dest[None, :], tokens, dt_decay.reshape(rows, 2 * heads), groups)
    arrived = lax.all_to_all(sent, "ctx", split_axis=0, concat_axis=0, tiled=True)
    low, high, small = unpack(arrived, width, heads, rows)

    def turned(x, by):
        return lax.ppermute(x, "head", [(i, (i + by) % ring) for i in range(ring)])

    low_left, low_right = turned(low, 1), turned(low, ring - 1)
    halo = lax.ppermute(
        high[high.shape[0] - HALO :], "ctx", [(i, i + 1) for i in range(groups - 1)]
    )
    high = jnp.concatenate([halo, high], axis=0)
    high_left, high_right = turned(high, 1), turned(high, ring - 1)
    low_far, high_far = turned(low_left, 1), turned(high_right, ring - 1)
    lows = [low, low_left, low_far, low_right]
    highs = [high, high_left, high_far, high_right]

    starts = jnp.cumsum(lengths) - lengths
    positions = first_pos + jnp.arange(rows, dtype=jnp.int32)
    doc_start = jnp.max(
        jnp.where(starts[None, :] <= positions[:, None], starts[None, :], 0), axis=1
    )
    rel = (positions - doc_start)[:, None]
    me = lax.axis_index("head").astype(jnp.int32)[None]
    conv, state, mid, input_map, output_map = front(
        me, lows, highs, w_x, w_bc, small, rel, conv_x, bias_x[None, :], conv_bc, bias_bc[None, :]
    )
    states = input_map.shape[1]
    share = states // groups
    gathered = lax.all_to_all(
        state.reshape(groups, share, inner + 128), "ctx", split_axis=0, concat_axis=0, tiled=True
    ).reshape(states, inner + 128)
    part = inner_part(
        small, rel, input_map, output_map, conv, mid, jnp.repeat(skip, HD)[None, :]
    )
    entering = scan_shards(gathered, heads)
    enter = lax.all_to_all(
        entering.reshape(groups, share, inner), "ctx", split_axis=0, concat_axis=0, tiled=True
    ).reshape(states, inner)
    return final(small, rel, output_map, part, enter)


def solution(mesh):
    in_specs = (
        P("ctx", "head"),
        P("ctx", None, "head"),
        P("ctx"),
        P(),
        P(None, "head"),
        P(),
        P(None, "head"),
        P(),
        P("head"),
        P(),
        P("head"),
    )
    out_specs = P("ctx", "head")
    return jax.shard_map(
        on_device, mesh=mesh, in_specs=in_specs, out_specs=out_specs, check_vma=False
    )
```

```python
import functools

import jax
import jax.numpy as jnp
from jax import lax
from jax.experimental import pallas as pl
from jax.experimental.pallas import tpu as pltpu
from jax.sharding import PartitionSpec as P

BF = jnp.bfloat16
F32 = jnp.float32
CAP = 16
BLK = 256
HD = 64
TILE = 256
HALO = 16
LANES = 128
ROWS_SENT = 88
DECAY_AT = 24
SMALL_END = 44
HIGH_AT, LOW_AT = 44, 108
PIECE = 24


def iota(shape, dim):
    return lax.broadcasted_iota(jnp.int32, shape, dim)


def mm(a, b):
    return jnp.dot(a, b, preferred_element_type=F32)


def mm_nt(a, b):
    return lax.dot_general(a, b, (((1,), (1,)), ((), ())), preferred_element_type=F32)


def mm_tn(a, b):
    return lax.dot_general(a, b, (((0,), (0,)), ((), ())), preferred_element_type=F32)


def as_bf(mask):
    return jnp.where(mask, 1.0, 0.0).astype(BF)


def lower_ones(n):
    return as_bf(iota((n, n), 0) >= iota((n, n), 1))


def params(mib, flops=0, bytes_accessed=0):
    return dict(
        compiler_params=pltpu.CompilerParams(vmem_limit_bytes=mib * 1024 * 1024),
        cost_estimate=pl.CostEstimate(
            flops=flops, bytes_accessed=bytes_accessed, transcendentals=0
        ),
    )


def vmem(count):
    return [pl.BlockSpec(memory_space=pltpu.VMEM)] * count


def near(x):
    return pltpu.with_memory_space_constraint(x, pltpu.VMEM)


def far(x):
    return pltpu.with_memory_space_constraint(x, pltpu.HBM)


def hbm(count):
    return [pl.BlockSpec(memory_space=pltpu.HBM)] * count


def fetch(source, target, sem):
    copy = pltpu.make_async_copy(source, target, sem)
    copy.start()
    return copy


def pack_kernel(
    dest_hbm, steps_hbm, tok_hbm, out_ref,
    dest_ref, steps_ref, tok_ref, slot_ref, code_ref, small_ref, sems,
):
    get_dest = fetch(dest_hbm, dest_ref, sems.at[0])
    get_steps = fetch(steps_hbm, steps_ref, sems.at[1])
    get_tokens = fetch(tok_hbm, tok_ref, sems.at[2])
    rows, width = tok_ref.shape
    groups = code_ref.shape[0]
    heads = steps_ref.shape[0]
    per = 8
    slots = per * CAP
    get_dest.wait()
    dest = dest_ref[...]
    target = dest // rows
    place = dest % rows + 1
    onehot = iota((groups, rows), 0) == target
    upper = as_bf(iota((rows, rows), 0) <= iota((rows, rows), 1))
    ranks = mm(as_bf(onehot), upper)
    rank = jnp.sum(jnp.where(onehot, ranks, 0.0), axis=0, keepdims=True) - 1.0
    rank = rank.astype(jnp.int32)
    slot_ref[...] = target * CAP + rank
    line = iota((LANES, rows), 0)
    codes = jnp.where(line == HIGH_AT + rank, place // 256, 0)
    codes = codes + jnp.where(line == LOW_AT + rank, place % 256, 0)
    code_ref[...] = mm_nt(as_bf(onehot), codes.astype(F32).astype(BF))
    get_steps.wait()
    steps = steps_ref[...].astype(F32)
    small_ref[...] = jnp.zeros_like(small_ref)
    small_ref[:heads] = steps[:, 0, :]
    small_ref[DECAY_AT : DECAY_AT + heads] = steps[:, 1, :]
    get_tokens.wait()

    def body(step, _):
        slot = slot_ref[...] - step * slots
        here = pl.ds(pl.multiple_of(step * per, per), per)
        sent = mm(as_bf(iota((slots, rows), 0) == slot), tok_ref[...]).astype(BF)
        for column in range(width // LANES):
            out_ref[here, column * CAP : (column + 1) * CAP, :] = sent[
                :, column * LANES : (column + 1) * LANES
            ].reshape(per, CAP, LANES)
        half = CAP // 2
        line = iota((per * half, rows), 0)
        line = line + line // half * half
        small = small_ref[...].astype(BF)
        pairs = mm_nt(as_bf(line == slot), small)
        pairs = pairs + pltpu.roll(mm_nt(as_bf(line + half == slot), small), LANES // 2, 1)
        pairs = pairs.reshape(per, half, LANES)
        first = iota((per, half, LANES), 1) == 0
        pairs = pairs + jnp.where(first, code_ref[here][:, None, :], 0.0)
        out_ref[here, ROWS_SENT - half :, :] = pairs.astype(BF)
        return 0

    lax.fori_loop(0, groups // per, body, 0)


def pack(dest, tokens, steps, groups):
    rows, width = tokens.shape
    return pl.pallas_call(
        pack_kernel,
        in_specs=hbm(3),
        out_specs=pl.BlockSpec(memory_space=pltpu.VMEM),
        out_shape=jax.ShapeDtypeStruct((groups, ROWS_SENT, LANES), BF),
        scratch_shapes=[
            pltpu.VMEM((1, rows), jnp.int32),
            pltpu.VMEM(steps.shape, BF),
            pltpu.VMEM((rows, width), BF),
            pltpu.VMEM((1, rows), jnp.int32),
            pltpu.VMEM((groups, LANES), F32),
            pltpu.VMEM((LANES, rows), F32),
            pltpu.SemaphoreType.DMA((3,)),
        ],
        name="pack",
        **params(16, 2 * rows * groups * CAP * (width + LANES), 4 * rows * width),
    )(far(dest), far(steps), far(tokens))


def places(row_codes, groups, lane_slot, lane_group, count):
    line = iota((LANES, count), 0)
    table = jnp.where(
        line == HIGH_AT + lane_slot, 256.0, jnp.where(line == LOW_AT + lane_slot, 1.0, 0.0)
    ).astype(BF)
    wide = mm(row_codes, table)
    mine = iota((groups, count), 0) == lane_group
    return jnp.sum(jnp.where(mine, wide, 0.0), axis=0, keepdims=True).astype(jnp.int32)


def pick(pos, first, rows):
    return as_bf(iota((rows, pos.shape[1]), 0) + (first + 1) == pos)


def take(select, recv_ref, target, first_row):
    groups = recv_ref.shape[0]
    rows = select.shape[0]
    for column in range(target.shape[1] // LANES):
        source = recv_ref[:, column * CAP : (column + 1) * CAP, :]
        target[first_row : first_row + rows, column * LANES : (column + 1) * LANES] = mm(
            select, source.reshape(groups * CAP, LANES)
        ).astype(BF)


def unpack_low_kernel(recv_ref, low_ref, edge_ref, pos_ref):
    groups = recv_ref.shape[0]
    half = CAP // 2
    rows = 2 * low_ref.shape[0]
    codes = recv_ref[:, ROWS_SENT - half :, :].astype(F32)[:, 0, :].astype(BF)
    lane = iota((1, groups * CAP), 1)
    pos = places(codes, groups, lane % CAP, lane // CAP, groups * CAP)
    pos_ref[...] = pos
    take(pick(pos, 0, rows // 2), recv_ref, low_ref, 0)
    take(pick(pos, rows - HALO, HALO), recv_ref, edge_ref, 0)


def unpack_high_kernel(recv_ref, pos_ref, high_ref, small_hbm, small_ref, mixed_ref, sem):
    groups = recv_ref.shape[0]
    half = CAP // 2
    rows = high_ref.shape[0] - HALO
    small = recv_ref[:, ROWS_SENT - half :, :].astype(F32)
    mixed_ref[...] = small.reshape(groups * half, LANES).astype(BF)
    codes = small[:, 0, :].astype(BF)
    lane = iota((1, groups * half), 1)
    first = places(codes, groups, lane % half, lane // half, groups * half)
    second = places(codes, groups, lane % half + half, lane // half, groups * half)
    mixed = mixed_ref[...]
    values = mm(pick(first, 0, 2 * rows), mixed)
    turned = pltpu.roll(mm(pick(second, 0, 2 * rows), mixed), LANES // 2, 1)
    valid = iota((2 * rows, LANES), 1) < SMALL_END
    small_ref[...] = jnp.where(valid, values + turned, 0.0).astype(BF)
    put = fetch(small_ref, small_hbm, sem)
    high_ref[:HALO] = jnp.zeros((HALO, high_ref.shape[1]), BF)
    take(pick(pos_ref[...], rows, rows), recv_ref, high_ref, HALO)
    put.wait()


def unpack(recv, width, rows):
    groups = recv.shape[0]
    slots = groups * CAP
    low, edge, pos = pl.pallas_call(
        unpack_low_kernel,
        in_specs=vmem(1),
        out_specs=vmem(3),
        out_shape=[
            jax.ShapeDtypeStruct((rows // 2, width), BF),
            jax.ShapeDtypeStruct((HALO, width), BF),
            jax.ShapeDtypeStruct((1, slots), jnp.int32),
        ],
        name="unpack_low",
        **params(12, rows * slots * width, 3 * rows * width),
    )(recv)
    high, small = pl.pallas_call(
        unpack_high_kernel,
        in_specs=vmem(2),
        out_specs=vmem(1) + hbm(1),
        out_shape=[
            jax.ShapeDtypeStruct((rows // 2 + HALO, width), BF),
            pltpu.HBM((rows, LANES), BF),
        ],
        scratch_shapes=[
            pltpu.VMEM((rows, LANES), BF),
            pltpu.VMEM((slots // 2, LANES), BF),
            pltpu.SemaphoreType.DMA,
        ],
        name="unpack_high",
        **params(12, rows * slots * width, 3 * rows * width),
    )(recv, pos)
    return low, edge, high, small


def conv_silu(ext, weight, bias, rel, rows):
    total = jnp.zeros((rows, ext.shape[1]), F32) + bias
    taps = weight.shape[0]
    for tap in range(taps):
        lag = taps - 1 - tap
        shifted = ext[HALO - lag : HALO - lag + rows]
        total = total + jnp.where(rel >= lag, weight[tap : tap + 1] * shifted, 0.0)
    return jax.nn.silu(total).astype(BF)


def head_spread(tile, first):
    per = TILE // HD
    return as_bf(iota((128, TILE), 0) == first + per * tile + iota((128, TILE), 1) // HD)


def piece_tiles(dest):
    base = dest // 2 * 5
    first = (base, base + 1) if dest % 2 == 0 else (base + 3, base + 4)
    return first + (base + 2,)


def near_kernel(
    me_ref, low0, low1, low3, high0, high1, high3, w_hbm, wbc_hbm,
    total_ref, far_ref, xe_ref, w_ref, gets,
):
    half, width = low0.shape
    inner = w_hbm.shape[1]
    copies = []
    for at, turn in enumerate((0, 1, 3, 2)):
        owner = lax.rem(me_ref[0] + 4 - turn, 4)
        lines = pl.ds(pl.multiple_of(owner * width, width), width)
        target = w_ref.at[pl.ds(at * width, width)] if at < 3 else far_ref
        copies.append(
            fetch(w_hbm.at[lines], target.at[:, pl.ds(0, inner)], gets.at[at, 0])
        )
        copies.append(
            fetch(
                wbc_hbm.at[lines],
                target.at[:, pl.ds(inner, wbc_hbm.shape[1])],
                gets.at[at, 1],
            )
        )
    for at, (low, high) in enumerate(((low0, high0), (low1, high1), (low3, high3))):
        columns = slice(at * width, (at + 1) * width)
        xe_ref[:HALO, columns] = high[:HALO]
        xe_ref[HALO : HALO + half, columns] = low[...]
        xe_ref[HALO + half :, columns] = high[HALO:]
    for copy in copies:
        copy.wait()

    def body(tile, _):
        columns = pl.ds(pl.multiple_of(tile * TILE, TILE), TILE)
        total_ref[:, columns] = mm(xe_ref[...], w_ref[:, columns])
        return 0

    lax.fori_loop(0, total_ref.shape[1] // TILE, body, 0)


def project_near(me, lows, highs, w_x, w_bc):
    half, width = lows[0].shape
    rows = 2 * half + HALO
    full = w_x.shape[1] + w_bc.shape[1]
    return pl.pallas_call(
        near_kernel,
        in_specs=[pl.BlockSpec(memory_space=pltpu.SMEM)] + vmem(6) + hbm(2),
        out_specs=vmem(2),
        out_shape=[pltpu.VMEM((rows, full), F32), pltpu.VMEM((width, full), BF)],
        scratch_shapes=[
            pltpu.VMEM((rows, 3 * width), BF),
            pltpu.VMEM((3 * width, full), BF),
            pltpu.SemaphoreType.DMA((4, 2)),
        ],
        name="project_near",
        **params(24, 6 * rows * width * full, 8_000_000),
    )(me, *[near(x) for x in (*lows, *highs)], far(w_x), far(w_bc))


def front_kernel(
    low_ref, high_ref, total_ref, w_ref, rel_ref,
    small_hbm, cx_hbm, bx_hbm, cb_hbm, bb_hbm,
    conv_hbm, sent_ref, mid_hbm, in_hbm, outmap_hbm,
    small_ref, cx_ref, bx_ref, cb_ref, bb_ref,
    conv_ref, mid_ref, in_ref, outmap_ref,
    xe_ref, state_ref, gain_ref, gets, puts,
):
    half, width = low_ref.shape
    rows = 2 * half
    states = in_ref.shape[1]
    tiles = conv_ref.shape[0]
    inner = tiles * TILE
    rest = [
        fetch(source, target, gets.at[at])
        for at, (source, target) in enumerate(
            (
                (small_hbm, small_ref), (cx_hbm, cx_ref), (bx_hbm, bx_ref),
                (cb_hbm, cb_ref), (bb_hbm, bb_ref),
            )
        )
    ]
    xe_ref[:HALO] = high_ref[:HALO]
    xe_ref[HALO : HALO + half] = low_ref[...]
    xe_ref[HALO + half :] = high_ref[HALO:]

    def project(columns):
        total = total_ref[:, columns] + mm(xe_ref[...], w_ref[:, columns])
        return total.astype(BF).astype(F32)

    def tile_columns(tile):
        return pl.ds(pl.multiple_of(tile * TILE, TILE), TILE)

    rel = rel_ref[...]
    ext = project(slice(inner, inner + 2 * states))
    for copy in rest:
        copy.wait()
    both = conv_silu(ext, cb_ref[...], bb_ref[...], rel, rows)
    in_ref[...] = both[:, :states]
    outmap_ref[...] = both[:, states:]
    put_maps = [
        fetch(in_ref, in_hbm, puts.at[0]), fetch(outmap_ref, outmap_hbm, puts.at[1])
    ]

    def finish(tile):
        columns = tile_columns(tile)
        rel = rel_ref[...]
        ext = project(columns)
        inner = conv_silu(ext, cx_ref[:, columns], bx_ref[:, columns], rel, rows)
        conv_ref[tile] = inner
        pltpu.make_async_copy(
            conv_ref.at[tile], conv_hbm.at[:, columns], puts.at[2 + tile]
        ).start()
        small = small_ref[...]
        steps = mm(small, head_spread(tile, 0))
        decays = mm(small, head_spread(tile, DECAY_AT)).astype(BF)
        inject = (inner.astype(F32) * steps).astype(BF).astype(F32)
        ones = lower_ones(BLK)
        carried, reach = None, None
        for block in range(rows // BLK):
            span = slice(block * BLK, (block + 1) * BLK)
            cumulative = mm(ones, decays[span])
            last = rel[(block + 1) * BLK - 1 : (block + 1) * BLK]
            end = cumulative[BLK - 1 : BLK]
            behind = BLK - 1 - iota((BLK, 1), 0)
            decayed = jnp.where(
                behind <= last, jnp.exp(end - cumulative) * inject[span], 0.0
            ).astype(BF)
            block_state = mm_tn(in_ref[span], decayed)
            carry = jnp.where(last > BLK - 1, jnp.exp(end), 0.0)
            if carried is None:
                carried, reach = block_state, carry
                mid_ref[:, columns] = carried.astype(BF)
            else:
                carried = carry * carried + block_state
                reach = reach * carry
        state_ref[:, columns] = carried
        gain_ref[:, columns] = jnp.broadcast_to(reach, (8, TILE))

    def body(tile, _):
        finish(tile)
        return 0

    lax.fori_loop(0, tiles, body, 0)
    put_mid = fetch(mid_ref, mid_hbm, puts.at[2 + tiles])

    lines = states // 8

    def tile_of(index):
        column, line = index // lines, index % lines
        return state_ref[line * 8 : line * 8 + 8, column * LANES : (column + 1) * LANES]

    def codes_of(column):
        gain = gain_ref[0:1, column * LANES : (column + 1) * LANES]
        high = gain.astype(BF).astype(F32)
        return high, gain - high

    for dest in range(sent_ref.shape[0]):
        first, second, shared = piece_tiles(dest)
        columns = [index // lines for index in (first, second, shared)]
        middle = tile_of(shared)[4 * (dest % 2) : 4 * (dest % 2) + 4]
        piece = [tile_of(first), tile_of(second), middle]
        piece += [*codes_of(min(columns)), *codes_of(max(columns))]
        sent_ref[dest] = jnp.concatenate(piece, axis=0).astype(BF)
    put_mid.wait()
    for copy in put_maps:
        copy.wait()
    for tile in range(tiles):
        pltpu.make_async_copy(
            conv_ref.at[tile], conv_hbm.at[:, pl.ds(tile * TILE, TILE)], puts.at[2 + tile]
        ).wait()


def front(low, high, total, w_far, small, rel, conv_x, bias_x, conv_bc, bias_bc, groups):
    half, width = low.shape
    rows = 2 * half
    inner = conv_x.shape[1]
    states = conv_bc.shape[1] // 2
    tiles = inner // TILE
    return pl.pallas_call(
        front_kernel,
        in_specs=vmem(5) + hbm(5),
        out_specs=hbm(1) + vmem(1) + hbm(3),
        out_shape=[
            pltpu.HBM((rows, inner), BF),
            jax.ShapeDtypeStruct((groups, PIECE, LANES), BF),
            pltpu.HBM((states, inner), BF),
            pltpu.HBM((rows, states), BF),
            pltpu.HBM((rows, states), BF),
        ],
        scratch_shapes=[
            pltpu.VMEM(small.shape, BF),
            pltpu.VMEM(conv_x.shape, F32),
            pltpu.VMEM(bias_x.shape, F32),
            pltpu.VMEM(conv_bc.shape, F32),
            pltpu.VMEM(bias_bc.shape, F32),
            pltpu.VMEM((tiles, rows, TILE), BF),
            pltpu.VMEM((states, inner), BF),
            pltpu.VMEM((rows, states), BF),
            pltpu.VMEM((rows, states), BF),
            pltpu.VMEM((rows + HALO, width), BF),
            pltpu.VMEM((states, inner), F32),
            pltpu.VMEM((8, inner), F32),
            pltpu.SemaphoreType.DMA((5,)),
            pltpu.SemaphoreType.DMA((tiles + 3,)),
        ],
        name="front",
        **params(20, 2 * rows * width * (inner + 2 * states), 12_000_000),
    )(
        *[near(x) for x in (low, high, total, w_far, rel)],
        *[far(x) for x in (small, conv_x, bias_x, conv_bc, bias_bc)],
    )


def inner_kernel(
    rel_ref, skip_ref, small_hbm, in_hbm, outmap_hbm, conv_hbm, mid_hbm, part_hbm, codes_hbm,
    small_ref, in_ref, outmap_ref, conv_ref, mid_ref, part_ref, codes_ref,
    scores_ref, across_ref, gets, puts,
):
    gets = [
        fetch(source, target, gets.at[at])
        for at, (source, target) in enumerate(
            (
                (small_hbm, small_ref), (in_hbm, in_ref), (outmap_hbm, outmap_ref),
                (conv_hbm, conv_ref), (mid_hbm, mid_ref),
            )
        )
    ]
    for copy in gets:
        copy.wait()
    rows, inner = conv_ref.shape
    tiles = inner // TILE
    per = TILE // HD
    ones = lower_ones(BLK)
    before = None
    for block in range(rows // BLK):
        span = slice(block * BLK, (block + 1) * BLK)
        scores = mm_nt(outmap_ref[span], in_ref[span])
        gap = iota((BLK, BLK), 0) - iota((BLK, BLK), 1)
        keep = (gap >= 0) & (gap <= rel_ref[span])
        scores_ref[block] = jnp.where(keep, scores, 0.0)
        so_far = mm(ones, small_ref[span])
        across_ref[block] = so_far.T
        if block > 0:
            so_far = so_far + before
        before = so_far[BLK - 1 : BLK]
        lane = iota((BLK, LANES), 1)
        reached = (iota((BLK, LANES), 0) + block * BLK < rel_ref[span]) & (
            (lane >= DECAY_AT) & (lane < SMALL_END)
        )
        gain = jnp.where(reached, jnp.exp(jnp.where(reached, so_far, 0.0)), 0.0)
        high = gain.astype(BF)
        codes_ref[0, span] = high
        codes_ref[1, span] = (gain - high.astype(F32)).astype(BF)
    put_codes = fetch(codes_ref, codes_hbm, puts.at[tiles])

    def body(tile, _):
        columns = pl.ds(pl.multiple_of(tile * TILE, TILE), TILE)
        small = small_ref[...]
        steps = mm(small, head_spread(tile, 0))
        decays = mm(small, head_spread(tile, DECAY_AT)).astype(BF)
        conv = conv_ref[:, columns].astype(F32)
        inject = (conv * steps).astype(BF)
        lane_head = iota((BLK, TILE), 1) // HD
        for block in range(rows // BLK):
            span = slice(block * BLK, (block + 1) * BLK)
            cumulative = mm(ones, decays[span])
            scores = scores_ref[block]
            total = skip_ref[:, columns] * conv[span]
            if block > 0:
                enter = jnp.where(
                    iota((BLK, 1), 0) < rel_ref[span], jnp.exp(cumulative), 0.0
                )
                total = total + enter * mm(outmap_ref[span], mid_ref[:, columns])
            for q in range(per):
                down = cumulative[:, q * HD : q * HD + 1]
                across = across_ref[block, pl.ds(DECAY_AT + per * tile + q, 1), :]
                weights = (scores * jnp.exp(jnp.minimum(down - across, 0.0))).astype(BF)
                mine = jnp.where(lane_head == q, inject[span], jnp.zeros((), BF))
                total = total + mm(weights, mine)
            part_ref[tile, span] = total
        pltpu.make_async_copy(
            part_ref.at[tile], part_hbm.at[tile], puts.at[tile]
        ).start()
        return 0

    lax.fori_loop(0, tiles, body, 0)
    put_codes.wait()
    for tile in range(tiles):
        pltpu.make_async_copy(part_ref.at[tile], part_hbm.at[tile], puts.at[tile]).wait()


def inner_part(small, rel, input_map, output_map, conv, mid, skip_wide):
    rows, inner = conv.shape
    blocks = rows // BLK
    tiles = inner // TILE
    return pl.pallas_call(
        inner_kernel,
        in_specs=vmem(2) + hbm(5),
        out_specs=hbm(2),
        out_shape=[
            pltpu.HBM((tiles, rows, TILE), F32),
            pltpu.HBM((2, rows, LANES), BF),
        ],
        scratch_shapes=[
            pltpu.VMEM(small.shape, BF),
            pltpu.VMEM(input_map.shape, BF),
            pltpu.VMEM(output_map.shape, BF),
            pltpu.VMEM(conv.shape, BF),
            pltpu.VMEM(mid.shape, BF),
            pltpu.VMEM((tiles, rows, TILE), F32),
            pltpu.VMEM((2, rows, LANES), BF),
            pltpu.VMEM((blocks, BLK, BLK), F32),
            pltpu.VMEM((blocks, 128, BLK), F32),
            pltpu.SemaphoreType.DMA((5,)),
            pltpu.SemaphoreType.DMA((tiles + 1,)),
        ],
        name="inner_part",
        **params(24, 8 * rows * BLK * inner, 8_000_000),
    )(rel, skip_wide, *[far(x) for x in (small, input_map, output_map, conv, mid)])


def scan_kernel(lines, me_ref, recv_ref, out_ref):
    groups = recv_ref.shape[0]
    me = me_ref[0]
    base = me // 2 * 5
    odd = lax.rem(me, 2)
    columns = [(base + 3 * odd) // lines, (base + 1 + 3 * odd) // lines, (base + 2) // lines]
    least = jnp.minimum(jnp.minimum(columns[0], columns[1]), columns[2])
    near_first = [
        jnp.where(jnp.full((8, LANES), column, jnp.int32) == least, 1.0, 0.0) for column in columns
    ]

    def body(shard, state):
        piece = recv_ref[shard].astype(F32)
        out_ref[shard] = jnp.concatenate(state, axis=0).astype(BF)
        gain_a = piece[20:21] + piece[21:22]
        gain_b = piece[22:23] + piece[23:24]
        return tuple(
            jnp.where(first > 0.5, gain_a, gain_b) * old + piece[8 * at : 8 * at + 8]
            for at, (first, old) in enumerate(zip(near_first, state))
        )

    lax.fori_loop(0, groups, body, (jnp.zeros((8, LANES), F32),) * 3, unroll=4)


def scan_shards(me, recv, lines):
    return pl.pallas_call(
        functools.partial(scan_kernel, lines),
        in_specs=[pl.BlockSpec(memory_space=pltpu.SMEM)] + vmem(1),
        out_specs=pl.BlockSpec(memory_space=pltpu.VMEM),
        out_shape=jax.ShapeDtypeStruct(recv.shape, BF),
        name="scan_shards",
        **params(8, 10_000_000, 800_000),
    )(me, recv)


def final_kernel(
    recv_ref, outmap_hbm, codes_hbm, part_hbm, out_hbm,
    outmap_ref, codes_ref, part_ref, held_ref, gets, puts,
):
    tiles, rows = part_ref.shape[0], part_ref.shape[1]
    states = outmap_ref.shape[1]
    lines = states // 8
    get_map = fetch(outmap_hbm, outmap_ref, gets.at[tiles])
    get_codes = fetch(codes_hbm, codes_ref, gets.at[tiles + 1])
    get_parts = [
        fetch(part_hbm.at[tile], part_ref.at[tile], gets.at[tile]) for tile in range(tiles)
    ]
    where = {}
    for dest in range(recv_ref.shape[0]):
        first, second, shared = piece_tiles(dest)
        where[first] = (dest, 0)
        where[second] = (dest, 1)
        where.setdefault(shared, dest)

    def tile_of(index):
        if isinstance(where[index], tuple):
            dest, at = where[index]
            return recv_ref[dest].astype(F32)[8 * at : 8 * at + 8]
        dest = where[index]
        upper = recv_ref[dest].astype(F32)[16:20]
        lower = recv_ref[dest + 1].astype(F32)[16:20]
        return jnp.concatenate([upper, lower], axis=0)

    def column_of(column):
        parts = [tile_of(column * lines + line) for line in range(lines)]
        return jnp.concatenate(parts, axis=0).astype(BF)

    get_map.wait()
    get_codes.wait()
    copies = []
    for tile in range(tiles):
        per = TILE // LANES
        entering = jnp.concatenate([column_of(tile * per + at) for at in range(per)], axis=1)
        outer = mm(outmap_ref[...], entering)
        spread = head_spread(tile, DECAY_AT)
        gain = mm(codes_ref[0], spread) + mm(codes_ref[1], spread)
        get_parts[tile].wait()
        held_ref[tile] = (part_ref[tile] + gain * outer).astype(BF)
        copies.append(
            fetch(held_ref.at[tile], out_hbm.at[:, pl.ds(tile * TILE, TILE)], puts.at[tile])
        )
    for copy in copies:
        copy.wait()


def final(output_map, part, codes, recv):
    tiles, rows, _ = part.shape
    return pl.pallas_call(
        final_kernel,
        in_specs=vmem(1) + hbm(3),
        out_specs=pl.BlockSpec(memory_space=pltpu.HBM),
        out_shape=jax.ShapeDtypeStruct((rows, tiles * TILE), BF),
        scratch_shapes=[
            pltpu.VMEM(output_map.shape, BF),
            pltpu.VMEM(codes.shape, BF),
            pltpu.VMEM(part.shape, F32),
            pltpu.VMEM((tiles, rows, TILE), BF),
            pltpu.SemaphoreType.DMA((tiles + 2,)),
            pltpu.SemaphoreType.DMA((tiles,)),
        ],
        name="final",
        **params(16, 2 * rows * 128 * tiles * TILE, 5_000_000),
    )(near(recv), far(output_map), far(codes), far(part))


def on_device(tokens, dt_decay, dest, lengths, w_x, w_bc, conv_x, conv_bc, bias_x, bias_bc, skip):
    rows, width = tokens.shape
    groups = lax.axis_size("ctx")
    ring = lax.axis_size("head")
    first_pos = lax.axis_index("ctx") * rows

    sent = pack(dest[None, :], tokens, jnp.transpose(dt_decay, (2, 1, 0)), groups)
    arrived = lax.all_to_all(sent, "ctx", split_axis=0, concat_axis=0, tiled=True)
    low, edge, high, small = unpack(arrived, width, rows)

    def turned(x, by):
        return lax.ppermute(x, "head", [(i, (i + by) % ring) for i in range(ring)])

    low_left, low_right = turned(low, 1), turned(low, ring - 1)
    halo = lax.ppermute(edge, "ctx", [(i, i + 1) for i in range(groups - 1)])
    high = lax.dynamic_update_slice(high, halo, (0, 0))
    high_left, high_right = turned(high, 1), turned(high, ring - 1)
    low_far, high_far = turned(low_left, 1), turned(high_right, ring - 1)

    starts = jnp.cumsum(lengths) - lengths
    positions = first_pos + jnp.arange(rows, dtype=jnp.int32)
    doc_start = jnp.max(
        jnp.where(starts[None, :] <= positions[:, None], starts[None, :], 0), axis=1
    )
    rel = (positions - doc_start)[:, None]
    me = lax.axis_index("head").astype(jnp.int32)[None]
    total, w_far = project_near(
        me, [low, low_left, low_right], [high, high_left, high_right], w_x, w_bc
    )
    conv, state, mid, input_map, output_map = front(
        low_far, high_far, total, w_far, small, rel,
        conv_x, bias_x[None, :], conv_bc, bias_bc[None, :], groups,
    )
    gathered = lax.all_to_all(state, "ctx", split_axis=0, concat_axis=0, tiled=True)
    part, gain = inner_part(
        small, rel, input_map, output_map, conv, mid, jnp.repeat(skip, HD)[None, :]
    )
    gathered, part = lax.optimization_barrier((gathered, part))
    spot = lax.axis_index("ctx").astype(jnp.int32)[None]
    entering = scan_shards(spot, gathered, input_map.shape[1] // 8)
    enter = lax.all_to_all(entering, "ctx", split_axis=0, concat_axis=0, tiled=True)
    return final(output_map, part, gain, enter)


def solution(mesh):
    in_specs = (
        P("ctx", "head"),
        P("ctx", None, "head"),
        P("ctx"),
        P(),
        P(None, "head"),
        P(),
        P(None, "head"),
        P(),
        P("head"),
        P(),
        P("head"),
    )
    out_specs = P("ctx", "head")
    return jax.shard_map(
        on_device, mesh=mesh, in_specs=in_specs, out_specs=out_specs, check_vma=False
    )
```

```python
import functools

import jax
import jax.numpy as jnp
from jax import lax
from jax.experimental import pallas as pl
from jax.experimental.pallas import tpu as pltpu
from jax.sharding import PartitionSpec as P

BF = jnp.bfloat16
F32 = jnp.float32
CAP = 16
BLK = 256
HD = 64
TILE = 256
HALO = 16
LANES = 128
ROWS_SENT = 88
DECAY_AT = 24
SMALL_END = 44
HIGH_AT, LOW_AT = 44, 108
PIECE = 24
TAKEN = 128


def iota(shape, dim):
    return lax.broadcasted_iota(jnp.int32, shape, dim)


def mm(a, b):
    return jnp.dot(a, b, preferred_element_type=F32)


def mm_nt(a, b):
    return lax.dot_general(a, b, (((1,), (1,)), ((), ())), preferred_element_type=F32)


def mm_tn(a, b):
    return lax.dot_general(a, b, (((0,), (0,)), ((), ())), preferred_element_type=F32)


def as_bf(mask):
    return jnp.where(mask, 1.0, 0.0).astype(BF)


def lower_ones(n):
    return as_bf(iota((n, n), 0) >= iota((n, n), 1))


def params(mib, flops=0, bytes_accessed=0):
    return dict(
        compiler_params=pltpu.CompilerParams(vmem_limit_bytes=mib * 1024 * 1024),
        cost_estimate=pl.CostEstimate(
            flops=flops, bytes_accessed=bytes_accessed, transcendentals=0
        ),
    )


def vmem(count):
    return [pl.BlockSpec(memory_space=pltpu.VMEM)] * count


def near(x):
    return pltpu.with_memory_space_constraint(x, pltpu.VMEM)


def far(x):
    return pltpu.with_memory_space_constraint(x, pltpu.HBM)


def hbm(count):
    return [pl.BlockSpec(memory_space=pltpu.HBM)] * count


def fetch(source, target, sem):
    copy = pltpu.make_async_copy(source, target, sem)
    copy.start()
    return copy


def pack_kernel(
    dest_hbm, steps_hbm, tok_hbm, out_ref,
    dest_ref, steps_ref, tok_ref, slot_ref, code_ref, small_ref, turned_ref, upper_ref,
    sems,
):
    get_dest = fetch(dest_hbm, dest_ref, sems.at[0])
    get_steps = fetch(steps_hbm, steps_ref, sems.at[1])
    get_tokens = fetch(tok_hbm, tok_ref, sems.at[2])
    rows, width = tok_ref.shape
    groups = code_ref.shape[0]
    heads = steps_ref.shape[0]
    per = 8
    slots = per * CAP
    upper_ref[...] = as_bf(iota((rows, rows), 0) <= iota((rows, rows), 1))
    small_ref[...] = jnp.zeros_like(small_ref)
    get_dest.wait()
    dest = dest_ref[...]
    target = dest // rows
    place = dest % rows + 1
    onehot = iota((groups, rows), 0) == target
    ranks = mm(as_bf(onehot), upper_ref[...])
    rank = jnp.sum(jnp.where(onehot, ranks, 0.0), axis=0, keepdims=True) - 1.0
    rank = rank.astype(jnp.int32)
    slot_ref[...] = target * CAP + rank
    line = iota((LANES, rows), 0)
    codes = jnp.where(line == HIGH_AT + rank, place // 256, 0)
    codes = codes + jnp.where(line == LOW_AT + rank, place % 256, 0)
    code_ref[...] = mm_nt(as_bf(onehot), codes.astype(F32).astype(BF))
    get_steps.wait()
    steps = steps_ref[...].astype(F32)
    small_ref[:heads] = steps[:, 0, :]
    small_ref[DECAY_AT : DECAY_AT + heads] = steps[:, 1, :]
    turned_ref[...] = small_ref[...].T.astype(BF)
    get_tokens.wait()

    def body(step, _):
        slot = slot_ref[...] - step * slots
        here = pl.ds(pl.multiple_of(step * per, per), per)
        select = as_bf(iota((slots, rows), 0) == slot)
        sent = mm(select, tok_ref[...]).astype(BF)
        for column in range(width // LANES):
            out_ref[here, column * CAP : (column + 1) * CAP, :] = sent[
                :, column * LANES : (column + 1) * LANES
            ].reshape(per, CAP, LANES)
        half = CAP // 2
        small = mm(select, turned_ref[...]).reshape(per, CAP, LANES)
        pairs = small[:, :half, :] + pltpu.roll(small[:, half:, :], LANES // 2, 2)
        first = iota((per, half, LANES), 1) == 0
        pairs = pairs + jnp.where(first, code_ref[here][:, None, :], 0.0)
        out_ref[here, ROWS_SENT - half :, :] = pairs.astype(BF)
        return 0

    lax.fori_loop(0, groups // per, body, 0, unroll=2)


def pack(dest, tokens, steps, groups):
    rows, width = tokens.shape
    return pl.pallas_call(
        pack_kernel,
        in_specs=hbm(3),
        out_specs=pl.BlockSpec(memory_space=pltpu.VMEM),
        out_shape=jax.ShapeDtypeStruct((groups, ROWS_SENT, LANES), BF),
        scratch_shapes=[
            pltpu.VMEM((1, rows), jnp.int32),
            pltpu.VMEM(steps.shape, BF),
            pltpu.VMEM((rows, width), BF),
            pltpu.VMEM((1, rows), jnp.int32),
            pltpu.VMEM((groups, LANES), F32),
            pltpu.VMEM((LANES, rows), F32),
            pltpu.VMEM((rows, LANES), BF),
            pltpu.VMEM((rows, rows), BF),
            pltpu.SemaphoreType.DMA((3,)),
        ],
        name="pack",
        **params(16, 2 * rows * groups * CAP * (width + LANES), 4 * rows * width),
    )(far(dest), far(steps), far(tokens))


def places(row_codes, groups, lane_slot, lane_group, count):
    line = iota((LANES, count), 0)
    table = jnp.where(
        line == HIGH_AT + lane_slot, 256.0, jnp.where(line == LOW_AT + lane_slot, 1.0, 0.0)
    ).astype(BF)
    wide = mm(row_codes, table)
    mine = iota((groups, count), 0) == lane_group
    return jnp.sum(jnp.where(mine, wide, 0.0), axis=0, keepdims=True).astype(jnp.int32)


def pick(pos, first, rows):
    return as_bf(iota((rows, pos.shape[1]), 0) + (first + 1) == pos)


def take(select, recv_ref, target, first_row):
    groups = recv_ref.shape[0]
    rows = select.shape[0]
    for column in range(target.shape[1] // LANES):
        source = recv_ref[:, column * CAP : (column + 1) * CAP, :]
        target[first_row : first_row + rows, column * LANES : (column + 1) * LANES] = mm(
            select, source.reshape(groups * CAP, LANES)
        ).astype(BF)


def paired_rows(recv_ref, rows_ref):
    groups = recv_ref.shape[0]
    half = CAP // 2
    pairs = recv_ref[:, ROWS_SENT - half :, :].astype(F32)
    both = jnp.concatenate([pairs, pltpu.roll(pairs, LANES // 2, 2)], axis=1)
    rows_ref[...] = both.reshape(groups * CAP, LANES).astype(BF)
    return pairs[:, 0, :].astype(BF)


def take_small(select, rows_ref):
    values = mm(select, rows_ref[...])
    valid = iota(values.shape, 1) < SMALL_END
    return jnp.where(valid, values, 0.0).astype(BF)


def unpack_low_kernel(
    recv_ref, low_ref, pos_ref, small_hbm, rows_ref, small_ref, sem
):
    groups = recv_ref.shape[0]
    rows = 2 * low_ref.shape[0]
    codes = paired_rows(recv_ref, rows_ref)
    lane = iota((1, groups * CAP), 1)
    pos = places(codes, groups, lane % CAP, lane // CAP, groups * CAP)
    pos_ref[...] = pos
    select = pick(pos, 0, rows // 2)
    small_ref[...] = take_small(select, rows_ref)
    put = fetch(small_ref, small_hbm, sem)
    take(select, recv_ref, low_ref, 0)
    put.wait()


def unpack_high_kernel(
    recv_ref, pos_ref, high_ref, edge_ref, small_hbm, rows_ref, small_ref, sem
):
    rows = high_ref.shape[0] - HALO
    paired_rows(recv_ref, rows_ref)
    select = pick(pos_ref[...], rows, rows)
    small_ref[...] = take_small(select, rows_ref)
    put = fetch(small_ref, small_hbm, sem)
    high_ref[:HALO] = jnp.zeros((HALO, high_ref.shape[1]), BF)
    take(select, recv_ref, high_ref, HALO)
    edge_ref[...] = high_ref[rows:]
    put.wait()


def unpack(recv, width, rows):
    groups = recv.shape[0]
    slots = groups * CAP
    half = rows // 2
    scratch = [
        pltpu.VMEM((slots, LANES), BF),
        pltpu.VMEM((half, LANES), BF),
        pltpu.SemaphoreType.DMA,
    ]
    low, pos, small_low = pl.pallas_call(
        unpack_low_kernel,
        in_specs=vmem(1),
        out_specs=vmem(2) + hbm(1),
        out_shape=[
            jax.ShapeDtypeStruct((half, width), BF),
            jax.ShapeDtypeStruct((1, slots), jnp.int32),
            pltpu.HBM((half, LANES), BF),
        ],
        scratch_shapes=scratch,
        name="unpack_low",
        **params(12, rows * slots * width, 3 * rows * width),
    )(recv)
    high, edge, small_high = pl.pallas_call(
        unpack_high_kernel,
        in_specs=vmem(2),
        out_specs=vmem(2) + hbm(1),
        out_shape=[
            jax.ShapeDtypeStruct((half + HALO, width), BF),
            jax.ShapeDtypeStruct((HALO, width), BF),
            pltpu.HBM((half, LANES), BF),
        ],
        scratch_shapes=scratch,
        name="unpack_high",
        **params(12, rows * slots * width, 3 * rows * width),
    )(recv, pos)
    return low, edge, high, (small_low, small_high)


def conv_silu(ext_ref, weight, bias, rel, rows):
    taps = weight.shape[0]
    total = bias + weight[taps - 1 : taps] * ext_ref[HALO : HALO + rows]
    for lag in range(1, taps):
        tap = taps - 1 - lag
        shifted = ext_ref[HALO - lag : HALO - lag + rows]
        total = total + jnp.where(rel >= lag, weight[tap : tap + 1] * shifted, 0.0)
    return jax.nn.silu(total).astype(BF)


def head_spread(tile, first):
    per = TILE // HD
    return as_bf(iota((128, TILE), 0) == first + per * tile + iota((128, TILE), 1) // HD)


def piece_tiles(dest):
    base = dest // 2 * 5
    first = (base, base + 1) if dest % 2 == 0 else (base + 3, base + 4)
    return first + (base + 2,)


def decay_kernel(
    rel_ref, low_hbm, high_hbm, steps_hbm, tail_hbm, carry_ref,
    small_ref, steps_ref, tail_ref, gets, puts,
):
    tiles, rows = tail_ref.shape[0], tail_ref.shape[1]
    half = rows // 2
    copies = [
        fetch(low_hbm, small_ref.at[pl.ds(0, half)], gets.at[0]),
        fetch(high_hbm, small_ref.at[pl.ds(half, half)], gets.at[1]),
    ]
    for copy in copies:
        copy.wait()
    ones = lower_ones(BLK)
    rel = rel_ref[...]

    def body(tile, _):
        small = small_ref[...]
        steps_ref[tile] = mm(small, head_spread(tile, 0)).astype(BF)
        decays = mm(small, head_spread(tile, DECAY_AT)).astype(BF)
        reach, lines = None, []
        for block in range(rows // BLK):
            span = slice(block * BLK, (block + 1) * BLK)
            cumulative = mm(ones, decays[span])
            last = rel[(block + 1) * BLK - 1 : (block + 1) * BLK]
            end = cumulative[BLK - 1 : BLK]
            behind = BLK - 1 - iota((BLK, 1), 0)
            tail_ref[tile, span] = jnp.where(behind <= last, jnp.exp(end - cumulative), 0.0)
            carry = jnp.where(last > BLK - 1, jnp.exp(end), 0.0)
            lines.append(carry)
            reach = carry if reach is None else reach * carry
        lines.append(reach)
        lines.append(jnp.zeros((8 - len(lines), TILE), F32))
        carry_ref[tile] = jnp.concatenate(lines, axis=0)
        pltpu.make_async_copy(steps_ref.at[tile], steps_hbm.at[tile], puts.at[tile]).start()
        pltpu.make_async_copy(
            tail_ref.at[tile], tail_hbm.at[tile], puts.at[tiles + tile]
        ).start()
        return 0

    lax.fori_loop(0, tiles, body, 0)
    for tile in range(tiles):
        pltpu.make_async_copy(steps_ref.at[tile], steps_hbm.at[tile], puts.at[tile]).wait()
        pltpu.make_async_copy(
            tail_ref.at[tile], tail_hbm.at[tile], puts.at[tiles + tile]
        ).wait()


def decay_factors(rel, small, inner):
    rows = rel.shape[0]
    tiles = inner // TILE
    return pl.pallas_call(
        decay_kernel,
        in_specs=vmem(1) + hbm(2),
        out_specs=hbm(2) + vmem(1),
        out_shape=[
            pltpu.HBM((tiles, rows, TILE), BF),
            pltpu.HBM((tiles, rows, TILE), F32),
            jax.ShapeDtypeStruct((tiles, 8, TILE), F32),
        ],
        scratch_shapes=[
            pltpu.VMEM((rows, LANES), BF),
            pltpu.VMEM((tiles, rows, TILE), BF),
            pltpu.VMEM((tiles, rows, TILE), F32),
            pltpu.SemaphoreType.DMA((2,)),
            pltpu.SemaphoreType.DMA((2 * tiles,)),
        ],
        name="decay_factors",
        **params(16, 4 * rows * BLK * inner, 7_000_000),
    )(rel, *[far(x) for x in small])


def assemble(xe_ref, low_ref, high_ref, columns):
    half = low_ref.shape[0]
    xe_ref[:HALO, columns] = high_ref[:HALO]
    xe_ref[HALO : HALO + half, columns] = low_ref[...]
    xe_ref[HALO + half :, columns] = high_ref[HALO:]


def own_kernel(
    me_ref, low_ref, high_ref, w_hbm, wbc_hbm,
    total_ref, left_ref, right_ref, far_ref, xe_ref, w_ref, gets,
):
    width = low_ref.shape[1]
    inner, rest = w_hbm.shape[1], wbc_hbm.shape[1]
    copies = []
    for turn, target in enumerate((w_ref, left_ref, far_ref, right_ref)):
        owner = lax.rem(me_ref[0] + 4 - turn, 4)
        lines = pl.ds(pl.multiple_of(owner * width, width), width)
        copies.append(
            (
                fetch(w_hbm.at[lines], target.at[:, pl.ds(0, inner)], gets.at[turn, 0]),
                fetch(wbc_hbm.at[lines], target.at[:, pl.ds(inner, rest)], gets.at[turn, 1]),
            )
        )
    assemble(xe_ref, low_ref, high_ref, slice(None))
    for copy in copies[0]:
        copy.wait()

    def body(tile, _):
        columns = pl.ds(pl.multiple_of(tile * TILE, TILE), TILE)
        total_ref[:, columns] = mm(xe_ref[...], w_ref[:, columns])
        return 0

    lax.fori_loop(0, total_ref.shape[1] // TILE, body, 0)
    for pair in copies[1:]:
        for copy in pair:
            copy.wait()


def project_own(me, low, high, w_x, w_bc):
    half, width = low.shape
    rows = 2 * half + HALO
    full = w_x.shape[1] + w_bc.shape[1]
    return pl.pallas_call(
        own_kernel,
        in_specs=[pl.BlockSpec(memory_space=pltpu.SMEM)] + vmem(2) + hbm(2),
        out_specs=vmem(4),
        out_shape=[pltpu.VMEM((rows, full), F32)] + [pltpu.VMEM((width, full), BF)] * 3,
        scratch_shapes=[
            pltpu.VMEM((rows, width), BF),
            pltpu.VMEM((width, full), BF),
            pltpu.SemaphoreType.DMA((4, 2)),
        ],
        name="project_own",
        **params(8, 2 * rows * width * full, 8_000_000),
    )(me, near(low), near(high), far(w_x), far(w_bc))


def near_kernel(
    low1, high1, low3, high3, left_ref, right_ref, sofar_ref, total_ref, xe_ref
):
    width = low1.shape[1]
    assemble(xe_ref, low1, high1, slice(0, width))
    assemble(xe_ref, low3, high3, slice(width, 2 * width))

    def body(tile, _):
        columns = pl.ds(pl.multiple_of(tile * TILE, TILE), TILE)
        weights = jnp.concatenate([left_ref[:, columns], right_ref[:, columns]], axis=0)
        total_ref[:, columns] = sofar_ref[:, columns] + mm(xe_ref[...], weights)
        return 0

    lax.fori_loop(0, total_ref.shape[1] // TILE, body, 0)


def project_near(left, right, w_left, w_right, total):
    width = left[0].shape[1]
    rows, full = total.shape
    return pl.pallas_call(
        near_kernel,
        in_specs=vmem(7),
        out_specs=vmem(1)[0],
        out_shape=pltpu.VMEM((rows, full), F32),
        scratch_shapes=[pltpu.VMEM((rows, 2 * width), BF)],
        name="project_near",
        **params(6, 4 * rows * width * full, 8_000_000),
    )(*[near(x) for x in (*left, *right, w_left, w_right, total)])


def piece_tiles(dest):
    base = dest // 2 * 5
    first = (base, base + 1) if dest % 2 == 0 else (base + 3, base + 4)
    return first + (base + 2,)


def front_kernel(
    low_ref, high_ref, total_ref, w_ref, rel_ref, carry_ref, cx_ref, bx_ref, cb_ref, bb_ref,
    steps_hbm, tail_hbm,
    conv_hbm, sent_ref, mid_hbm, in_hbm, outmap_hbm,
    steps_ref, tail_ref, conv_ref, mid_ref, in_ref, outmap_ref, across_ref,
    xe_ref, ext_ref, state_ref, gets, puts,
):
    half, width = low_ref.shape
    rows = 2 * half
    states = in_ref.shape[1]
    tiles = conv_ref.shape[0]
    inner = tiles * TILE
    for tile in range(tiles):
        fetch(steps_hbm.at[tile], steps_ref.at[tile], gets.at[0, tile])
        fetch(tail_hbm.at[tile], tail_ref.at[tile], gets.at[1, tile])
    assemble(xe_ref, low_ref, high_ref, slice(None))

    def project(columns):
        total = total_ref[:, columns] + mm(xe_ref[...], w_ref[:, columns])
        ext_ref[...] = total.astype(BF).astype(F32)

    rel = rel_ref[...]
    project(slice(inner, inner + 2 * states))
    both = conv_silu(ext_ref, cb_ref[...], bb_ref[...], rel, rows)
    in_ref[...] = both[:, :states]
    outmap_ref[...] = both[:, states:]
    put_maps = [
        fetch(in_ref, in_hbm, puts.at[0]), fetch(outmap_ref, outmap_hbm, puts.at[1])
    ]
    across_ref[...] = both[:, :states].astype(F32).T.astype(BF)

    def body(tile, _):
        columns = pl.ds(pl.multiple_of(tile * TILE, TILE), TILE)
        project(columns)
        inner_rows = conv_silu(ext_ref, cx_ref[:, columns], bx_ref[:, columns], rel_ref[...], rows)
        conv_ref[tile] = inner_rows
        pltpu.make_async_copy(
            conv_ref.at[tile], conv_hbm.at[:, columns], puts.at[2 + tile]
        ).start()
        for at, (source, target) in enumerate(((steps_hbm, steps_ref), (tail_hbm, tail_ref))):
            pltpu.make_async_copy(source.at[tile], target.at[tile], gets.at[at, tile]).wait()
        inject = (inner_rows.astype(F32) * steps_ref[tile].astype(F32)).astype(BF)
        decayed = (tail_ref[tile] * inject.astype(F32)).astype(BF)
        carried = None
        for block in range(rows // BLK):
            span = slice(block * BLK, (block + 1) * BLK)
            block_state = mm(across_ref[:, span], decayed[span])
            if carried is None:
                carried = block_state
                mid_ref[:, columns] = carried.astype(BF)
            else:
                carried = carry_ref[tile, block : block + 1] * carried + block_state
        state_ref[:, columns] = carried
        return 0

    lax.fori_loop(0, tiles, body, 0)
    put_mid = fetch(mid_ref, mid_hbm, puts.at[2 + tiles])
    lines = states // 8

    def tile_of(index):
        column, line = index // lines, index % lines
        return state_ref[line * 8 : line * 8 + 8, column * LANES : (column + 1) * LANES]

    def codes_of(column):
        per = TILE // LANES
        at = rows // BLK
        lanes = slice(column % per * LANES, (column % per + 1) * LANES)
        gain = carry_ref[column // per, at : at + 1, lanes]
        high = gain.astype(BF).astype(F32)
        return high, gain - high

    for dest in range(sent_ref.shape[0]):
        first, second, shared = piece_tiles(dest)
        columns = [index // lines for index in (first, second, shared)]
        middle = tile_of(shared)[4 * (dest % 2) : 4 * (dest % 2) + 4]
        piece = [tile_of(first), tile_of(second), middle]
        piece += [*codes_of(min(columns)), *codes_of(max(columns))]
        sent_ref[dest] = jnp.concatenate(piece, axis=0).astype(BF)
    put_mid.wait()
    for copy in put_maps:
        copy.wait()
    for tile in range(tiles):
        pltpu.make_async_copy(
            conv_ref.at[tile], conv_hbm.at[:, pl.ds(tile * TILE, TILE)], puts.at[2 + tile]
        ).wait()


def front(piece, total, w_far, rel, carry, steps, tail, conv_x, bias_x, conv_bc, bias_bc, groups):
    half, width = piece[0].shape
    rows = 2 * half
    inner = conv_x.shape[1]
    states = conv_bc.shape[1] // 2
    tiles = inner // TILE
    return pl.pallas_call(
        front_kernel,
        in_specs=vmem(10) + hbm(2),
        out_specs=hbm(1) + vmem(1) + hbm(3),
        out_shape=[
            pltpu.HBM((rows, inner), BF),
            jax.ShapeDtypeStruct((groups, PIECE, LANES), BF),
            pltpu.HBM((states, inner), BF),
            pltpu.HBM((rows, states), BF),
            pltpu.HBM((rows, states), BF),
        ],
        scratch_shapes=[
            pltpu.VMEM(steps.shape, BF),
            pltpu.VMEM(tail.shape, F32),
            pltpu.VMEM((tiles, rows, TILE), BF),
            pltpu.VMEM((states, inner), BF),
            pltpu.VMEM((rows, states), BF),
            pltpu.VMEM((rows, states), BF),
            pltpu.VMEM((states, rows), BF),
            pltpu.VMEM((rows + HALO, width), BF),
            pltpu.VMEM((rows + HALO, TILE), F32),
            pltpu.VMEM((states, inner), F32),
            pltpu.SemaphoreType.DMA((2, tiles)),
            pltpu.SemaphoreType.DMA((tiles + 3,)),
        ],
        name="front",
        **params(20, 2 * rows * width * (inner + 2 * states), 12_000_000),
    )(
        *[near(x) for x in (*piece, total, w_far)], rel, carry,
        conv_x, bias_x, conv_bc, bias_bc, far(steps), far(tail),
    )


def inner_kernel(
    rel_ref, skip_ref, low_hbm, high_hbm, in_hbm, outmap_hbm, conv_hbm, mid_hbm, part_hbm,
    small_ref, in_ref, outmap_ref, conv_ref, mid_ref, part_ref,
    scores_ref, across_ref, gets, puts,
):
    half = low_hbm.shape[0]
    gets = [
        fetch(source, target, gets.at[at])
        for at, (source, target) in enumerate(
            (
                (low_hbm, small_ref.at[pl.ds(0, half)]),
                (high_hbm, small_ref.at[pl.ds(half, half)]),
                (in_hbm, in_ref), (outmap_hbm, outmap_ref),
                (conv_hbm, conv_ref), (mid_hbm, mid_ref),
            )
        )
    ]
    for copy in gets:
        copy.wait()
    rows, inner = conv_ref.shape
    tiles = inner // TILE
    per = TILE // HD
    ones = lower_ones(BLK)
    for block in range(rows // BLK):
        span = slice(block * BLK, (block + 1) * BLK)
        scores = mm_nt(outmap_ref[span], in_ref[span])
        gap = iota((BLK, BLK), 0) - iota((BLK, BLK), 1)
        keep = (gap >= 0) & (gap <= rel_ref[span])
        scores_ref[block] = jnp.where(keep, scores, 0.0)
        across_ref[block] = mm(ones, small_ref[span]).T

    def body(tile, _):
        columns = pl.ds(pl.multiple_of(tile * TILE, TILE), TILE)
        small = small_ref[...]
        steps = mm(small, head_spread(tile, 0))
        decays = mm(small, head_spread(tile, DECAY_AT)).astype(BF)
        conv = conv_ref[:, columns].astype(F32)
        inject = (conv * steps).astype(BF)
        lane_head = iota((BLK, TILE), 1) // HD
        for block in range(rows // BLK):
            span = slice(block * BLK, (block + 1) * BLK)
            cumulative = mm(ones, decays[span])
            scores = scores_ref[block]
            total = skip_ref[:, columns] * conv[span]
            if block > 0:
                enter = jnp.where(
                    iota((BLK, 1), 0) < rel_ref[span], jnp.exp(cumulative), 0.0
                )
                total = total + enter * mm(outmap_ref[span], mid_ref[:, columns])
            for q in range(per):
                down = cumulative[:, q * HD : q * HD + 1]
                across = across_ref[block, pl.ds(DECAY_AT + per * tile + q, 1), :]
                weights = (scores * jnp.exp(jnp.minimum(down - across, 0.0))).astype(BF)
                mine = jnp.where(lane_head == q, inject[span], jnp.zeros((), BF))
                total = total + mm(weights, mine)
            part_ref[span, columns] = total
        pltpu.make_async_copy(
            part_ref.at[:, columns], part_hbm.at[:, columns], puts.at[tile]
        ).start()
        return 0

    lax.fori_loop(0, tiles, body, 0)
    for tile in range(tiles):
        columns = pl.ds(tile * TILE, TILE)
        pltpu.make_async_copy(
            part_ref.at[:, columns], part_hbm.at[:, columns], puts.at[tile]
        ).wait()


def inner_part(small, rel, input_map, output_map, conv, mid, skip_wide):
    rows, inner = conv.shape
    blocks = rows // BLK
    tiles = inner // TILE
    return pl.pallas_call(
        inner_kernel,
        in_specs=vmem(2) + hbm(6),
        out_specs=hbm(1)[0],
        out_shape=pltpu.HBM((rows, inner), F32),
        scratch_shapes=[
            pltpu.VMEM((rows, LANES), BF),
            pltpu.VMEM(input_map.shape, BF),
            pltpu.VMEM(output_map.shape, BF),
            pltpu.VMEM(conv.shape, BF),
            pltpu.VMEM(mid.shape, BF),
            pltpu.VMEM((rows, inner), F32),
            pltpu.VMEM((blocks, BLK, BLK), F32),
            pltpu.VMEM((blocks, 128, BLK), F32),
            pltpu.SemaphoreType.DMA((6,)),
            pltpu.SemaphoreType.DMA((tiles,)),
        ],
        name="inner_part",
        **params(24, 8 * rows * BLK * inner, 8_000_000),
    )(rel, skip_wide, *[far(x) for x in (*small, input_map, output_map, conv, mid)])


def scan_kernel(lines, me_ref, recv_ref, out_ref):
    groups = recv_ref.shape[0]
    me = me_ref[0]
    base = me // 2 * 5
    odd = lax.rem(me, 2)
    columns = [(base + 3 * odd) // lines, (base + 1 + 3 * odd) // lines, (base + 2) // lines]
    least = jnp.minimum(jnp.minimum(columns[0], columns[1]), columns[2])
    near_first = [
        jnp.where(jnp.full((8, LANES), column, jnp.int32) == least, 1.0, 0.0) for column in columns
    ]

    def body(shard, state):
        piece = recv_ref[shard].astype(F32)
        out_ref[shard] = jnp.concatenate(state, axis=0).astype(BF)
        gain_a = piece[20:21] + piece[21:22]
        gain_b = piece[22:23] + piece[23:24]
        return tuple(
            jnp.where(first > 0.5, gain_a, gain_b) * old + piece[8 * at : 8 * at + 8]
            for at, (first, old) in enumerate(zip(near_first, state))
        )

    lax.fori_loop(0, groups, body, (jnp.zeros((8, LANES), F32),) * 3, unroll=4)


def scan_shards(me, recv, lines):
    return pl.pallas_call(
        functools.partial(scan_kernel, lines),
        in_specs=[pl.BlockSpec(memory_space=pltpu.SMEM)] + vmem(1),
        out_specs=pl.BlockSpec(memory_space=pltpu.VMEM),
        out_shape=jax.ShapeDtypeStruct(recv.shape, BF),
        name="scan_shards",
        **params(8, 10_000_000, 800_000),
    )(me, recv)


def prepare_kernel(rel_ref, low_hbm, high_hbm, gain_ref, small_ref, ones_ref, sems):
    rows, inner = gain_ref.shape
    half = rows // 2
    get_small = [
        fetch(low_hbm, small_ref.at[pl.ds(0, half)], sems.at[0]),
        fetch(high_hbm, small_ref.at[pl.ds(half, half)], sems.at[1]),
    ]
    ones_ref[...] = lower_ones(rows)
    reached = iota((rows, 1), 0) < rel_ref[...]
    for copy in get_small:
        copy.wait()

    def body(tile, _):
        decays = mm(small_ref[...], head_spread(tile, DECAY_AT)).astype(BF)
        cumulative = mm(ones_ref[...], decays)
        gain_ref[:, pl.ds(pl.multiple_of(tile * TILE, TILE), TILE)] = jnp.where(
            reached, jnp.exp(cumulative), 0.0
        )
        return 0

    lax.fori_loop(0, inner // TILE, body, 0)


def prepare(rel, small, inner):
    rows = rel.shape[0]
    return pl.pallas_call(
        prepare_kernel,
        in_specs=vmem(1) + hbm(2),
        out_specs=vmem(1)[0],
        out_shape=pltpu.VMEM((rows, inner), F32),
        scratch_shapes=[
            pltpu.VMEM((rows, LANES), BF),
            pltpu.VMEM((rows, rows), BF),
            pltpu.SemaphoreType.DMA((2,)),
        ],
        name="prepare",
        **params(8, 2 * rows * rows * inner, 8_000_000),
    )(rel, *[far(x) for x in small])


def final_kernel(
    recv_ref, gain_ref, outmap_hbm, part_hbm, out_hbm,
    outmap_ref, part_ref, enter_ref, held_ref, gets, puts,
):
    rows, inner = part_ref.shape
    states = outmap_ref.shape[1]
    lines = states // 8
    steps = rows // TAKEN
    spans = [pl.ds(step * TAKEN, TAKEN) for step in range(steps)]
    get_map = fetch(outmap_hbm, outmap_ref, gets.at[steps])
    copies = [
        fetch(part_hbm.at[span], part_ref.at[span], gets.at[step])
        for step, span in enumerate(spans)
    ]
    where = {}
    for dest in range(recv_ref.shape[0]):
        first, second, shared = piece_tiles(dest)
        where[first] = (dest, 0)
        where[second] = (dest, 1)
        where.setdefault(shared, dest)

    def tile_of(index):
        if isinstance(where[index], tuple):
            dest, at = where[index]
            return recv_ref[dest].astype(F32)[8 * at : 8 * at + 8]
        dest = where[index]
        upper = recv_ref[dest].astype(F32)[16:20]
        lower = recv_ref[dest + 1].astype(F32)[16:20]
        return jnp.concatenate([upper, lower], axis=0)

    def column_of(column):
        parts = [tile_of(column * lines + line) for line in range(lines)]
        return jnp.concatenate(parts, axis=0).astype(BF)

    for column in range(inner // LANES):
        enter_ref[:, column * LANES : (column + 1) * LANES] = column_of(column)
    get_map.wait()
    puts_made = []
    for step, span in enumerate(spans):
        outer = mm(outmap_ref[span], enter_ref[...])
        copies[step].wait()
        held_ref[span] = (part_ref[span] + gain_ref[span] * outer).astype(BF)
        puts_made.append(fetch(held_ref.at[span], out_hbm.at[span], puts.at[step]))
    for copy in puts_made:
        copy.wait()


def final(output_map, part, gain, recv):
    rows, inner = part.shape
    states = output_map.shape[1]
    return pl.pallas_call(
        final_kernel,
        in_specs=vmem(2) + hbm(2),
        out_specs=hbm(1)[0],
        out_shape=jax.ShapeDtypeStruct((rows, inner), BF),
        scratch_shapes=[
            pltpu.VMEM((rows, states), BF),
            pltpu.VMEM((rows, inner), F32),
            pltpu.VMEM((states, inner), BF),
            pltpu.VMEM((rows, inner), BF),
            pltpu.SemaphoreType.DMA((rows // TAKEN + 1,)),
            pltpu.SemaphoreType.DMA((rows // TAKEN,)),
        ],
        name="final",
        **params(16, 2 * rows * states * inner, 7_000_000),
    )(near(recv), near(gain), far(output_map), far(part))


def on_device(tokens, dt_decay, dest, lengths, w_x, w_bc, conv_x, conv_bc, bias_x, bias_bc, skip):
    rows, width = tokens.shape
    groups = lax.axis_size("ctx")
    ring = lax.axis_size("head")
    first_pos = lax.axis_index("ctx") * rows

    sent = pack(dest[None, :], tokens, jnp.transpose(dt_decay, (2, 1, 0)), groups)
    arrived = lax.all_to_all(sent, "ctx", split_axis=0, concat_axis=0, tiled=True)
    low, edge, high, small = unpack(arrived, width, rows)

    def turned(x, by):
        return lax.ppermute(x, "head", [(i, (i + by) % ring) for i in range(ring)])

    low_left, low_right = turned(low, 1), turned(low, ring - 1)
    halo = lax.ppermute(edge, "ctx", [(i, i + 1) for i in range(groups - 1)])
    high = lax.dynamic_update_slice(high, halo, (0, 0))
    high_right = turned(high, ring - 1)

    starts = jnp.cumsum(lengths) - lengths
    positions = first_pos + jnp.arange(rows, dtype=jnp.int32)
    doc_start = jnp.max(
        jnp.where(starts[None, :] <= positions[:, None], starts[None, :], 0), axis=1
    )
    rel = (positions - doc_start)[:, None]
    me = lax.axis_index("head").astype(jnp.int32)[None]
    inner = w_x.shape[1]
    steps, tail, carry = decay_factors(rel, small, inner)
    later, carry = lax.optimization_barrier((high, carry))
    high_left = turned(later, 1)
    low_far, high_far = turned(low_left, 1), turned(high_right, ring - 1)
    total, w_left, w_right, w_far = project_own(me, low, high, w_x, w_bc)
    total = project_near(
        (low_left, high_left), (low_right, high_right), w_left, w_right, total
    )
    conv, state, mid, input_map, output_map = front(
        (low_far, high_far), total, w_far, rel, carry, steps, tail,
        conv_x, bias_x[None, :], conv_bc, bias_bc[None, :], groups,
    )
    gathered = lax.all_to_all(state, "ctx", split_axis=0, concat_axis=0, tiled=True)
    part = inner_part(
        small, rel, input_map, output_map, conv, mid, jnp.repeat(skip, HD)[None, :]
    )
    gathered, part = lax.optimization_barrier((gathered, part))
    spot = lax.axis_index("ctx").astype(jnp.int32)[None]
    entering = scan_shards(spot, gathered, input_map.shape[1] // 8)
    entering, rel = lax.optimization_barrier((entering, rel))
    gain = prepare(rel, small, inner)
    enter = lax.all_to_all(entering, "ctx", split_axis=0, concat_axis=0, tiled=True)
    return final(output_map, part, gain, enter)


def solution(mesh):
    in_specs = (
        P("ctx", "head"),
        P("ctx", None, "head"),
        P("ctx"),
        P(),
        P(None, "head"),
        P(),
        P(None, "head"),
        P(),
        P("head"),
        P(),
        P("head"),
    )
    out_specs = P("ctx", "head")
    return jax.shard_map(
        on_device, mesh=mesh, in_specs=in_specs, out_specs=out_specs, check_vma=False
    )
```

```python
import functools

import jax
import jax.numpy as jnp
from jax import lax
from jax.experimental import pallas as pl
from jax.experimental.pallas import tpu as pltpu
from jax.sharding import PartitionSpec as P

BF = jnp.bfloat16
F32 = jnp.float32
CAP = 16
BLK = 256
HD = 64
TILE = 256
HALO = 16
LANES = 128
ROWS_SENT = 88
DECAY_AT = 24
SMALL_END = 44
HIGH_AT, LOW_AT = 44, 108
PIECE = 24
TAKEN = 128


def iota(shape, dim):
    return lax.broadcasted_iota(jnp.int32, shape, dim)


def mm(a, b):
    return jnp.dot(a, b, preferred_element_type=F32)


def mm_nt(a, b):
    return lax.dot_general(a, b, (((1,), (1,)), ((), ())), preferred_element_type=F32)


def mm_tn(a, b):
    return lax.dot_general(a, b, (((0,), (0,)), ((), ())), preferred_element_type=F32)


def as_bf(mask):
    return jnp.where(mask, 1.0, 0.0).astype(BF)


def lower_ones(n):
    return as_bf(iota((n, n), 0) >= iota((n, n), 1))


def params(mib, flops=0, bytes_accessed=0):
    return dict(
        compiler_params=pltpu.CompilerParams(vmem_limit_bytes=mib * 1024 * 1024),
        cost_estimate=pl.CostEstimate(
            flops=flops, bytes_accessed=bytes_accessed, transcendentals=0
        ),
    )


def vmem(count):
    return [pl.BlockSpec(memory_space=pltpu.VMEM)] * count


def near(x):
    return pltpu.with_memory_space_constraint(x, pltpu.VMEM)


def far(x):
    return pltpu.with_memory_space_constraint(x, pltpu.HBM)


def hbm(count):
    return [pl.BlockSpec(memory_space=pltpu.HBM)] * count


def fetch(source, target, sem):
    copy = pltpu.make_async_copy(source, target, sem)
    copy.start()
    return copy


def pack_kernel(
    dest_hbm, steps_hbm, tok_hbm, out_ref,
    dest_ref, steps_ref, tok_ref, slot_ref, code_ref, small_ref, upper_ref,
    sems,
):
    get_dest = fetch(dest_hbm, dest_ref, sems.at[0])
    get_steps = fetch(steps_hbm, steps_ref, sems.at[1])
    rows, width = tok_hbm.shape
    get_tokens = fetch(tok_hbm, tok_ref.at[:, pl.ds(0, width)], sems.at[2])
    groups = code_ref.shape[0]
    heads = steps_ref.shape[0]
    per = 8
    slots = per * CAP
    upper_ref[...] = as_bf(iota((rows, rows), 0) <= iota((rows, rows), 1))
    small_ref[...] = jnp.zeros_like(small_ref)
    get_dest.wait()
    dest = dest_ref[...]
    target = dest // rows
    place = dest % rows + 1
    onehot = iota((groups, rows), 0) == target
    ranks = mm(as_bf(onehot), upper_ref[...])
    rank = jnp.sum(jnp.where(onehot, ranks, 0.0), axis=0, keepdims=True) - 1.0
    rank = rank.astype(jnp.int32)
    slot_ref[...] = target * CAP + rank
    line = iota((LANES, rows), 0)
    codes = jnp.where(line == HIGH_AT + rank, place // 256, 0)
    codes = codes + jnp.where(line == LOW_AT + rank, place % 256, 0)
    code_ref[...] = mm_nt(as_bf(onehot), codes.astype(F32).astype(BF))
    get_steps.wait()
    steps = steps_ref[...].astype(F32)
    small_ref[:heads] = steps[:, 0, :]
    small_ref[DECAY_AT : DECAY_AT + heads] = steps[:, 1, :]
    tok_ref[:, width:] = small_ref[...].T.astype(BF)
    get_tokens.wait()

    def body(step, _):
        slot = slot_ref[...] - step * slots
        here = pl.ds(pl.multiple_of(step * per, per), per)
        select = as_bf(iota((slots, rows), 0) == slot)
        both = mm(select, tok_ref[...])
        sent = both[:, :width].astype(BF)
        for column in range(width // LANES):
            out_ref[here, column * CAP : (column + 1) * CAP, :] = sent[
                :, column * LANES : (column + 1) * LANES
            ].reshape(per, CAP, LANES)
        half = CAP // 2
        small = both[:, width:].reshape(per, CAP, LANES)
        pairs = small[:, :half, :] + pltpu.roll(small[:, half:, :], LANES // 2, 2)
        first = iota((per, half, LANES), 1) == 0
        pairs = pairs + jnp.where(first, code_ref[here][:, None, :], 0.0)
        out_ref[here, ROWS_SENT - half :, :] = pairs.astype(BF)
        return 0

    lax.fori_loop(0, groups // per, body, 0, unroll=8)


def pack(dest, tokens, steps, groups):
    rows, width = tokens.shape
    return pl.pallas_call(
        pack_kernel,
        in_specs=hbm(3),
        out_specs=pl.BlockSpec(memory_space=pltpu.VMEM),
        out_shape=jax.ShapeDtypeStruct((groups, ROWS_SENT, LANES), BF),
        scratch_shapes=[
            pltpu.VMEM((1, rows), jnp.int32),
            pltpu.VMEM(steps.shape, BF),
            pltpu.VMEM((rows, width + LANES), BF),
            pltpu.VMEM((1, rows), jnp.int32),
            pltpu.VMEM((groups, LANES), F32),
            pltpu.VMEM((LANES, rows), F32),
            pltpu.VMEM((rows, rows), BF),
            pltpu.SemaphoreType.DMA((3,)),
        ],
        name="pack",
        **params(16, 2 * rows * groups * CAP * (width + LANES), 4 * rows * width),
    )(far(dest), far(steps), far(tokens))


def places(row_codes, groups, lane_slot, lane_group, count):
    line = iota((LANES, count), 0)
    table = jnp.where(
        line == HIGH_AT + lane_slot, 256.0, jnp.where(line == LOW_AT + lane_slot, 1.0, 0.0)
    ).astype(BF)
    wide = mm(row_codes, table)
    mine = iota((groups, count), 0) == lane_group
    return jnp.sum(jnp.where(mine, wide, 0.0), axis=0, keepdims=True).astype(jnp.int32)


def pick(pos, first, rows):
    return as_bf(iota((rows, pos.shape[1]), 0) + (first + 1) == pos)


def take(select, recv_ref, target, first_row):
    groups = recv_ref.shape[0]
    rows = select.shape[0]
    for column in range(target.shape[1] // LANES):
        source = recv_ref[:, column * CAP : (column + 1) * CAP, :]
        target[first_row : first_row + rows, column * LANES : (column + 1) * LANES] = mm(
            select, source.reshape(groups * CAP, LANES)
        ).astype(BF)


def paired_rows(recv_ref, rows_ref):
    groups = recv_ref.shape[0]
    half = CAP // 2
    pairs = recv_ref[:, ROWS_SENT - half :, :].astype(F32)
    both = jnp.concatenate([pairs, pltpu.roll(pairs, LANES // 2, 2)], axis=1)
    rows_ref[...] = both.reshape(groups * CAP, LANES).astype(BF)
    return pairs[:, 0, :].astype(BF)


def take_small(select, rows_ref):
    values = mm(select, rows_ref[...])
    valid = iota(values.shape, 1) < SMALL_END
    return jnp.where(valid, values, 0.0).astype(BF)


def unpack_low_kernel(
    recv_ref, low_ref, pos_ref, small_hbm, rows_ref, small_ref, sem
):
    groups = recv_ref.shape[0]
    rows = 2 * low_ref.shape[0]
    codes = paired_rows(recv_ref, rows_ref)
    lane = iota((1, groups * CAP), 1)
    pos = places(codes, groups, lane % CAP, lane // CAP, groups * CAP)
    pos_ref[...] = pos
    select = pick(pos, 0, rows // 2)
    small_ref[...] = take_small(select, rows_ref)
    put = fetch(small_ref, small_hbm, sem)
    take(select, recv_ref, low_ref, 0)
    put.wait()


def unpack_high_kernel(
    recv_ref, pos_ref, high_ref, edge_ref, small_hbm, rows_ref, small_ref, sem
):
    rows = high_ref.shape[0] - HALO
    paired_rows(recv_ref, rows_ref)
    select = pick(pos_ref[...], rows, rows)
    small_ref[...] = take_small(select, rows_ref)
    put = fetch(small_ref, small_hbm, sem)
    high_ref[:HALO] = jnp.zeros((HALO, high_ref.shape[1]), BF)
    take(select, recv_ref, high_ref, HALO)
    edge_ref[...] = high_ref[rows:]
    put.wait()


def unpack(recv, width, rows):
    groups = recv.shape[0]
    slots = groups * CAP
    half = rows // 2
    scratch = [
        pltpu.VMEM((slots, LANES), BF),
        pltpu.VMEM((half, LANES), BF),
        pltpu.SemaphoreType.DMA,
    ]
    low, pos, small_low = pl.pallas_call(
        unpack_low_kernel,
        in_specs=vmem(1),
        out_specs=vmem(2) + hbm(1),
        out_shape=[
            jax.ShapeDtypeStruct((half, width), BF),
            jax.ShapeDtypeStruct((1, slots), jnp.int32),
            pltpu.HBM((half, LANES), BF),
        ],
        scratch_shapes=scratch,
        name="unpack_low",
        **params(12, rows * slots * width, 3 * rows * width),
    )(recv)
    high, edge, small_high = pl.pallas_call(
        unpack_high_kernel,
        in_specs=vmem(2),
        out_specs=vmem(2) + hbm(1),
        out_shape=[
            jax.ShapeDtypeStruct((half + HALO, width), BF),
            jax.ShapeDtypeStruct((HALO, width), BF),
            pltpu.HBM((half, LANES), BF),
        ],
        scratch_shapes=scratch,
        name="unpack_high",
        **params(12, rows * slots * width, 3 * rows * width),
    )(recv, pos)
    return low, edge, high, (small_low, small_high)


def conv_silu(ext_ref, weight, bias, rel, rows):
    taps = weight.shape[0]
    total = bias + weight[taps - 1 : taps] * ext_ref[HALO : HALO + rows]
    for lag in range(1, taps):
        tap = taps - 1 - lag
        shifted = ext_ref[HALO - lag : HALO - lag + rows]
        total = total + jnp.where(rel >= lag, weight[tap : tap + 1] * shifted, 0.0)
    return jax.nn.silu(total).astype(BF)


def head_spread(tile, first):
    per = TILE // HD
    return as_bf(iota((128, TILE), 0) == first + per * tile + iota((128, TILE), 1) // HD)


def piece_tiles(dest):
    base = dest // 2 * 5
    first = (base, base + 1) if dest % 2 == 0 else (base + 3, base + 4)
    return first + (base + 2,)


def decay_kernel(
    rel_ref, low_hbm, high_hbm, steps_hbm, tail_hbm, carry_ref,
    small_ref, steps_ref, tail_ref, gets, puts,
):
    tiles, rows = tail_ref.shape[0], tail_ref.shape[1]
    half = rows // 2
    copies = [
        fetch(low_hbm, small_ref.at[pl.ds(0, half)], gets.at[0]),
        fetch(high_hbm, small_ref.at[pl.ds(half, half)], gets.at[1]),
    ]
    for copy in copies:
        copy.wait()
    ones = lower_ones(BLK)
    rel = rel_ref[...]

    def body(tile, _):
        small = small_ref[...]
        steps_ref[tile] = mm(small, head_spread(tile, 0)).astype(BF)
        decays = mm(small, head_spread(tile, DECAY_AT)).astype(BF)
        reach, lines = None, []
        for block in range(rows // BLK):
            span = slice(block * BLK, (block + 1) * BLK)
            cumulative = mm(ones, decays[span])
            last = rel[(block + 1) * BLK - 1 : (block + 1) * BLK]
            end = cumulative[BLK - 1 : BLK]
            behind = BLK - 1 - iota((BLK, 1), 0)
            tail_ref[tile, span] = jnp.where(behind <= last, jnp.exp(end - cumulative), 0.0)
            carry = jnp.where(last > BLK - 1, jnp.exp(end), 0.0)
            lines.append(carry)
            reach = carry if reach is None else reach * carry
        lines.append(reach)
        lines.append(jnp.zeros((8 - len(lines), TILE), F32))
        carry_ref[tile] = jnp.concatenate(lines, axis=0)
        pltpu.make_async_copy(steps_ref.at[tile], steps_hbm.at[tile], puts.at[tile]).start()
        pltpu.make_async_copy(
            tail_ref.at[tile], tail_hbm.at[tile], puts.at[tiles + tile]
        ).start()
        return 0

    lax.fori_loop(0, tiles, body, 0)
    for tile in range(tiles):
        pltpu.make_async_copy(steps_ref.at[tile], steps_hbm.at[tile], puts.at[tile]).wait()
        pltpu.make_async_copy(
            tail_ref.at[tile], tail_hbm.at[tile], puts.at[tiles + tile]
        ).wait()


def decay_factors(rel, small, inner):
    rows = rel.shape[0]
    tiles = inner // TILE
    return pl.pallas_call(
        decay_kernel,
        in_specs=vmem(1) + hbm(2),
        out_specs=hbm(2) + vmem(1),
        out_shape=[
            pltpu.HBM((tiles, rows, TILE), BF),
            pltpu.HBM((tiles, rows, TILE), F32),
            jax.ShapeDtypeStruct((tiles, 8, TILE), F32),
        ],
        scratch_shapes=[
            pltpu.VMEM((rows, LANES), BF),
            pltpu.VMEM((tiles, rows, TILE), BF),
            pltpu.VMEM((tiles, rows, TILE), F32),
            pltpu.SemaphoreType.DMA((2,)),
            pltpu.SemaphoreType.DMA((2 * tiles,)),
        ],
        name="decay_factors",
        **params(16, 4 * rows * BLK * inner, 7_000_000),
    )(rel, *[far(x) for x in small])


def assemble(xe_ref, low_ref, high_ref, columns):
    half = low_ref.shape[0]
    xe_ref[:HALO, columns] = high_ref[:HALO]
    xe_ref[HALO : HALO + half, columns] = low_ref[...]
    xe_ref[HALO + half :, columns] = high_ref[HALO:]


def own_kernel(
    me_ref, low_ref, high_ref, w_hbm, wbc_hbm,
    total_ref, left_ref, right_ref, far_ref, xe_ref, w_ref, gets,
):
    width = low_ref.shape[1]
    inner, rest = w_hbm.shape[1], wbc_hbm.shape[1]
    copies = []
    for turn, target in enumerate((w_ref, left_ref, far_ref, right_ref)):
        owner = lax.rem(me_ref[0] + 4 - turn, 4)
        lines = pl.ds(pl.multiple_of(owner * width, width), width)
        copies.append(
            (
                fetch(w_hbm.at[lines], target.at[:, pl.ds(0, inner)], gets.at[turn, 0]),
                fetch(wbc_hbm.at[lines], target.at[:, pl.ds(inner, rest)], gets.at[turn, 1]),
            )
        )
    assemble(xe_ref, low_ref, high_ref, slice(None))
    for copy in copies[0]:
        copy.wait()

    def body(tile, _):
        columns = pl.ds(pl.multiple_of(tile * TILE, TILE), TILE)
        total_ref[:, columns] = mm(xe_ref[...], w_ref[:, columns])
        return 0

    lax.fori_loop(0, total_ref.shape[1] // TILE, body, 0)
    for pair in copies[1:]:
        for copy in pair:
            copy.wait()


def project_own(me, low, high, w_x, w_bc):
    half, width = low.shape
    rows = 2 * half + HALO
    full = w_x.shape[1] + w_bc.shape[1]
    return pl.pallas_call(
        own_kernel,
        in_specs=[pl.BlockSpec(memory_space=pltpu.SMEM)] + vmem(2) + hbm(2),
        out_specs=vmem(4),
        out_shape=[pltpu.VMEM((rows, full), F32)] + [pltpu.VMEM((width, full), BF)] * 3,
        scratch_shapes=[
            pltpu.VMEM((rows, width), BF),
            pltpu.VMEM((width, full), BF),
            pltpu.SemaphoreType.DMA((4, 2)),
        ],
        name="project_own",
        **params(8, 2 * rows * width * full, 8_000_000),
    )(me, near(low), near(high), far(w_x), far(w_bc))


def near_kernel(
    low1, high1, low3, high3, left_ref, right_ref, sofar_ref, total_ref, xe_ref
):
    width = low1.shape[1]
    assemble(xe_ref, low1, high1, slice(0, width))
    assemble(xe_ref, low3, high3, slice(width, 2 * width))

    def body(tile, _):
        columns = pl.ds(pl.multiple_of(tile * TILE, TILE), TILE)
        weights = jnp.concatenate([left_ref[:, columns], right_ref[:, columns]], axis=0)
        total_ref[:, columns] = sofar_ref[:, columns] + mm(xe_ref[...], weights)
        return 0

    lax.fori_loop(0, total_ref.shape[1] // TILE, body, 0)


def project_near(left, right, w_left, w_right, total):
    width = left[0].shape[1]
    rows, full = total.shape
    return pl.pallas_call(
        near_kernel,
        in_specs=vmem(7),
        out_specs=vmem(1)[0],
        out_shape=pltpu.VMEM((rows, full), F32),
        scratch_shapes=[pltpu.VMEM((rows, 2 * width), BF)],
        name="project_near",
        **params(6, 4 * rows * width * full, 8_000_000),
    )(*[near(x) for x in (*left, *right, w_left, w_right, total)])


def piece_tiles(dest):
    base = dest // 2 * 5
    first = (base, base + 1) if dest % 2 == 0 else (base + 3, base + 4)
    return first + (base + 2,)


def front_kernel(
    low_ref, high_ref, total_ref, w_ref, rel_ref, carry_ref, cx_ref, bx_ref, cb_ref, bb_ref,
    steps_hbm, tail_hbm,
    conv_hbm, mine_ref, mid_hbm, in_hbm, outmap_ref,
    steps_ref, tail_ref, conv_ref, mid_ref, in_ref, across_ref,
    xe_ref, ext_ref, gets, puts,
):
    half, width = low_ref.shape
    rows = 2 * half
    states = in_ref.shape[1]
    tiles = conv_ref.shape[0]
    inner = tiles * TILE
    for tile in range(tiles):
        fetch(steps_hbm.at[tile], steps_ref.at[tile], gets.at[0, tile])
        fetch(tail_hbm.at[tile], tail_ref.at[tile], gets.at[1, tile])
    assemble(xe_ref, low_ref, high_ref, slice(None))

    def project(tile):
        columns = slice(tile * TILE, (tile + 1) * TILE)
        total = total_ref[:, columns] + mm(xe_ref[...], w_ref[:, columns])
        ext_ref[tile] = total.astype(BF).astype(F32)

    rel = rel_ref[...]
    for tile in range(tiles + 1):
        project(tile)
    both = conv_silu(ext_ref.at[tiles], cb_ref[...], bb_ref[...], rel, rows)
    in_ref[...] = both[:, :states]
    outmap_ref[...] = both[:, states:]
    put_map = fetch(in_ref, in_hbm, puts.at[0])
    across_ref[...] = both[:, :states].astype(F32).T.astype(BF)
    for tile in range(tiles):
        columns = slice(tile * TILE, (tile + 1) * TILE)
        inner_rows = conv_silu(ext_ref.at[tile], cx_ref[:, columns], bx_ref[:, columns], rel, rows)
        conv_ref[tile] = inner_rows
        fetch(conv_ref.at[tile], conv_hbm.at[:, pl.ds(tile * TILE, TILE)], puts.at[2 + tile])
        for at, (source, target) in enumerate(((steps_hbm, steps_ref), (tail_hbm, tail_ref))):
            pltpu.make_async_copy(source.at[tile], target.at[tile], gets.at[at, tile]).wait()
        inject = (inner_rows.astype(F32) * steps_ref[tile].astype(F32)).astype(BF)
        decayed = (tail_ref[tile] * inject.astype(F32)).astype(BF)
        carried = None
        for block in range(rows // BLK):
            span = slice(block * BLK, (block + 1) * BLK)
            block_state = mm(across_ref[:, span], decayed[span])
            if carried is None:
                carried = block_state
                mid_ref[:, columns] = carried.astype(BF)
            else:
                carried = carry_ref[tile, block : block + 1] * carried + block_state
        mine_ref[:states, columns] = carried.astype(BF)
        reach = carry_ref[tile, rows // BLK : rows // BLK + 1]
        high = reach.astype(BF).astype(F32)
        line = iota((HALO, TILE), 0)
        codes = jnp.where(line == 0, high, jnp.where(line == 1, reach - high, 0.0))
        mine_ref[states:, columns] = codes.astype(BF)
    put_mid = fetch(mid_ref, mid_hbm, puts.at[2 + tiles])
    put_mid.wait()
    put_map.wait()
    for tile in range(tiles):
        pltpu.make_async_copy(
            conv_ref.at[tile], conv_hbm.at[:, pl.ds(tile * TILE, TILE)], puts.at[2 + tile]
        ).wait()


def front(piece, total, w_far, rel, carry, steps, tail, conv_x, bias_x, conv_bc, bias_bc):
    half, width = piece[0].shape
    rows = 2 * half
    inner = conv_x.shape[1]
    states = conv_bc.shape[1] // 2
    tiles = inner // TILE
    return pl.pallas_call(
        front_kernel,
        in_specs=vmem(10) + hbm(2),
        out_specs=hbm(1) + vmem(1) + hbm(2) + vmem(1),
        out_shape=[
            pltpu.HBM((rows, inner), BF),
            jax.ShapeDtypeStruct((states + HALO, inner), BF),
            pltpu.HBM((states, inner), BF),
            pltpu.HBM((rows, states), BF),
            pltpu.VMEM((rows, states), BF),
        ],
        scratch_shapes=[
            pltpu.VMEM(steps.shape, BF),
            pltpu.VMEM(tail.shape, F32),
            pltpu.VMEM((tiles, rows, TILE), BF),
            pltpu.VMEM((states, inner), BF),
            pltpu.VMEM((rows, states), BF),
            pltpu.VMEM((states, rows), BF),
            pltpu.VMEM((rows + HALO, width), BF),
            pltpu.VMEM((tiles + 1, rows + HALO, TILE), F32),
            pltpu.SemaphoreType.DMA((2, tiles)),
            pltpu.SemaphoreType.DMA((tiles + 3,)),
        ],
        name="front",
        **params(20, 2 * rows * width * (inner + 2 * states), 12_000_000),
    )(
        *[near(x) for x in (*piece, total, w_far)], rel, carry,
        conv_x, bias_x, conv_bc, bias_bc, far(steps), far(tail),
    )


def combine_kernel(
    core_ref, mine_ref, theirs_ref, sent_ref, kept_hbm, chip_ref, gain_ref, kept_ref, sem
):
    half, inner = chip_ref.shape
    states = 2 * half
    lines = half // 8
    first = core_ref[0] == 0
    span = pl.ds(pl.multiple_of(core_ref[0] * half, half), half)
    own, other = mine_ref[span].astype(F32), theirs_ref[span].astype(F32)
    own_codes, other_codes = mine_ref[states:].astype(F32), theirs_ref[states:].astype(F32)
    early = jnp.where(first, own, other)
    early_codes = jnp.where(first, own_codes, other_codes)
    late_codes = jnp.where(first, other_codes, own_codes)
    kept_ref[:half] = early.astype(BF)
    kept_ref[half:] = early_codes.astype(BF)
    put = fetch(kept_ref, kept_hbm, sem)
    early_gain = early_codes[0:1] + early_codes[1:2]
    late_gain = late_codes[0:1] + late_codes[1:2]
    chip_ref[...] = late_gain * early + jnp.where(first, other, own)
    gain_ref[...] = jnp.broadcast_to(early_gain * late_gain, gain_ref.shape)

    def tile_of(index):
        column, line = index // lines, index % lines
        return chip_ref[line * 8 : line * 8 + 8, column * LANES : (column + 1) * LANES]

    def codes_of(column):
        gain = gain_ref[0:1, column * LANES : (column + 1) * LANES]
        high = gain.astype(BF).astype(F32)
        return high, gain - high

    for dest in range(sent_ref.shape[0]):
        one, two, shared = piece_tiles(dest)
        columns = [index // lines for index in (one, two, shared)]
        middle = tile_of(shared)[4 * (dest % 2) : 4 * (dest % 2) + 4]
        piece = [tile_of(one), tile_of(two), middle]
        piece += [*codes_of(min(columns)), *codes_of(max(columns))]
        sent_ref[dest] = jnp.concatenate(piece, axis=0).astype(BF)
    put.wait()


def combine(core, mine, theirs, chips):
    inner = mine.shape[1]
    half = (mine.shape[0] - HALO) // 2
    return pl.pallas_call(
        combine_kernel,
        in_specs=[pl.BlockSpec(memory_space=pltpu.SMEM)] + vmem(2),
        out_specs=vmem(1) + hbm(1),
        out_shape=[
            jax.ShapeDtypeStruct((chips, PIECE, LANES), BF),
            pltpu.HBM((half + HALO, inner), BF),
        ],
        scratch_shapes=[
            pltpu.VMEM((half, inner), F32),
            pltpu.VMEM((8, inner), F32),
            pltpu.VMEM((half + HALO, inner), BF),
            pltpu.SemaphoreType.DMA,
        ],
        name="combine",
        **params(8, 1_000_000, 1_500_000),
    )(core, near(mine), near(theirs))


def entering_kernel(core_ref, recv_ref, kept_hbm, send_ref, keep_ref, kept_ref, enter_ref, sem):
    get = fetch(kept_hbm, kept_ref, sem)
    half, inner = enter_ref.shape
    lines = half // 8
    where = {}
    for dest in range(recv_ref.shape[0]):
        one, two, shared = piece_tiles(dest)
        where[one] = (dest, 0)
        where[two] = (dest, 1)
        where.setdefault(shared, dest)

    def tile_of(index):
        if isinstance(where[index], tuple):
            dest, at = where[index]
            return recv_ref[dest].astype(F32)[8 * at : 8 * at + 8]
        dest = where[index]
        upper = recv_ref[dest].astype(F32)[16:20]
        lower = recv_ref[dest + 1].astype(F32)[16:20]
        return jnp.concatenate([upper, lower], axis=0)

    for index in range(lines * inner // LANES):
        column, line = index // lines, index % lines
        enter_ref[line * 8 : line * 8 + 8, column * LANES : (column + 1) * LANES] = tile_of(index)
    get.wait()
    first = core_ref[0] == 0
    codes = kept_ref[half:].astype(F32)
    early = enter_ref[...]
    late = (codes[0:1] + codes[1:2]) * early + kept_ref[:half].astype(F32)
    send_ref[...] = jnp.where(first, late, early).astype(BF)
    keep_ref[...] = jnp.where(first, early, late).astype(BF)


def entering_halves(core, recv, kept):
    rows, inner = kept.shape
    half = rows - HALO
    return pl.pallas_call(
        entering_kernel,
        in_specs=[pl.BlockSpec(memory_space=pltpu.SMEM)] + vmem(1) + hbm(1),
        out_specs=vmem(2),
        out_shape=[jax.ShapeDtypeStruct((half, inner), BF)] * 2,
        scratch_shapes=[
            pltpu.VMEM((rows, inner), BF),
            pltpu.VMEM((half, inner), F32),
            pltpu.SemaphoreType.DMA,
        ],
        name="entering_halves",
        **params(8, 1_000_000, 1_500_000),
    )(core, near(recv), far(kept))


def inner_kernel(
    rel_ref, skip_ref, outmap_ref, low_hbm, high_hbm, in_hbm, conv_hbm, mid_hbm, part_hbm,
    small_ref, in_ref, conv_ref, mid_ref, part_ref,
    scores_ref, across_ref, gets, puts,
):
    half = low_hbm.shape[0]
    rows, inner = conv_ref.shape
    tiles = inner // TILE
    per = TILE // HD
    first = [
        fetch(source, target, gets.at[tiles + at])
        for at, (source, target) in enumerate(
            (
                (low_hbm, small_ref.at[pl.ds(0, half)]),
                (high_hbm, small_ref.at[pl.ds(half, half)]),
                (in_hbm, in_ref),
            )
        )
    ]
    get_mid = fetch(mid_hbm, mid_ref, gets.at[tiles + 3])
    for tile in range(tiles):
        columns = pl.ds(tile * TILE, TILE)
        fetch(conv_hbm.at[:, columns], conv_ref.at[:, columns], gets.at[tile])
    for copy in first:
        copy.wait()
    ones = lower_ones(BLK)
    for block in range(rows // BLK):
        span = slice(block * BLK, (block + 1) * BLK)
        scores = mm_nt(outmap_ref[span], in_ref[span])
        gap = iota((BLK, BLK), 0) - iota((BLK, BLK), 1)
        keep = (gap >= 0) & (gap <= rel_ref[span])
        scores_ref[block] = jnp.where(keep, scores, 0.0)
        across_ref[block] = mm(ones, small_ref[span]).T

    def body(tile, _):
        columns = pl.ds(pl.multiple_of(tile * TILE, TILE), TILE)
        pltpu.make_async_copy(
            conv_hbm.at[:, columns], conv_ref.at[:, columns], gets.at[tile]
        ).wait()
        small = small_ref[...]
        steps = mm(small, head_spread(tile, 0))
        decays = mm(small, head_spread(tile, DECAY_AT)).astype(BF)
        conv = conv_ref[:, columns].astype(F32)
        inject = (conv * steps).astype(BF)
        lane_head = iota((BLK, TILE), 1) // HD
        for block in range(rows // BLK):
            span = slice(block * BLK, (block + 1) * BLK)
            cumulative = mm(ones, decays[span])
            scores = scores_ref[block]
            total = skip_ref[:, columns] * conv[span]
            if block > 0:
                enter = jnp.where(
                    iota((BLK, 1), 0) < rel_ref[span], jnp.exp(cumulative), 0.0
                )
                total = total + enter * mm(outmap_ref[span], mid_ref[:, columns])
            part = BLK // 2
            pieces = [total[:part], total[part:]]
            for q in range(per):
                down = cumulative[:, q * HD : q * HD + 1]
                across = across_ref[block, pl.ds(DECAY_AT + per * tile + q, 1), :]
                mine = jnp.where(lane_head == q, inject[span], jnp.zeros((), BF))
                for at, seen in ((0, part), (1, BLK)):
                    lines = slice(at * part, (at + 1) * part)
                    gap = jnp.minimum(down[lines] - across[:, :seen], 0.0)
                    weights = (scores[lines, :seen] * jnp.exp(gap)).astype(BF)
                    pieces[at] = pieces[at] + mm(weights, mine[:seen])
            total = jnp.concatenate(pieces, axis=0)
            part_ref[span, columns] = total
        pltpu.make_async_copy(
            part_ref.at[:, columns], part_hbm.at[:, columns], puts.at[tile]
        ).start()
        return 0

    get_mid.wait()
    lax.fori_loop(0, tiles, body, 0)
    for tile in range(tiles):
        columns = pl.ds(tile * TILE, TILE)
        pltpu.make_async_copy(
            part_ref.at[:, columns], part_hbm.at[:, columns], puts.at[tile]
        ).wait()


def inner_part(small, rel, input_map, output_map, conv, mid, skip_wide):
    rows, inner = conv.shape
    blocks = rows // BLK
    tiles = inner // TILE
    return pl.pallas_call(
        inner_kernel,
        in_specs=vmem(3) + hbm(5),
        out_specs=hbm(1)[0],
        out_shape=pltpu.HBM((rows, inner), F32),
        scratch_shapes=[
            pltpu.VMEM((rows, LANES), BF),
            pltpu.VMEM(input_map.shape, BF),
            pltpu.VMEM(conv.shape, BF),
            pltpu.VMEM(mid.shape, BF),
            pltpu.VMEM((rows, inner), F32),
            pltpu.VMEM((blocks, BLK, BLK), F32),
            pltpu.VMEM((blocks, 128, BLK), F32),
            pltpu.SemaphoreType.DMA((tiles + 4,)),
            pltpu.SemaphoreType.DMA((tiles,)),
        ],
        name="inner_part",
        **params(24, 8 * rows * BLK * inner, 8_000_000),
    )(rel, skip_wide, near(output_map), *[far(x) for x in (*small, input_map, conv, mid)])


def scan_kernel(lines, me_ref, recv_ref, out_ref):
    groups = recv_ref.shape[0]
    me = me_ref[0]
    base = me // 2 * 5
    odd = lax.rem(me, 2)
    columns = [(base + 3 * odd) // lines, (base + 1 + 3 * odd) // lines, (base + 2) // lines]
    least = jnp.minimum(jnp.minimum(columns[0], columns[1]), columns[2])
    near_first = [
        jnp.where(jnp.full((8, LANES), column, jnp.int32) == least, 1.0, 0.0) for column in columns
    ]

    def body(shard, state):
        piece = recv_ref[shard].astype(F32)
        out_ref[shard] = jnp.concatenate(state, axis=0).astype(BF)
        gain_a = piece[20:21] + piece[21:22]
        gain_b = piece[22:23] + piece[23:24]
        return tuple(
            jnp.where(first > 0.5, gain_a, gain_b) * old + piece[8 * at : 8 * at + 8]
            for at, (first, old) in enumerate(zip(near_first, state))
        )

    lax.fori_loop(0, groups, body, (jnp.zeros((8, LANES), F32),) * 3, unroll=4)


def scan_shards(me, recv, lines):
    return pl.pallas_call(
        functools.partial(scan_kernel, lines),
        in_specs=[pl.BlockSpec(memory_space=pltpu.SMEM)] + vmem(1),
        out_specs=pl.BlockSpec(memory_space=pltpu.VMEM),
        out_shape=pltpu.VMEM(recv.shape, BF),
        name="scan_shards",
        **params(8, 10_000_000, 800_000),
    )(me, near(recv))


def prepare_kernel(rel_ref, low_hbm, high_hbm, gain_ref, small_ref, ones_ref, sems):
    rows, inner = gain_ref.shape
    half = rows // 2
    get_small = [
        fetch(low_hbm, small_ref.at[pl.ds(0, half)], sems.at[0]),
        fetch(high_hbm, small_ref.at[pl.ds(half, half)], sems.at[1]),
    ]
    ones_ref[...] = lower_ones(rows)
    reached = iota((rows, 1), 0) < rel_ref[...]
    for copy in get_small:
        copy.wait()

    def body(tile, _):
        decays = mm(small_ref[...], head_spread(tile, DECAY_AT)).astype(BF)
        cumulative = mm(ones_ref[...], decays)
        gain_ref[:, pl.ds(pl.multiple_of(tile * TILE, TILE), TILE)] = jnp.where(
            reached, jnp.exp(cumulative), 0.0
        )
        return 0

    lax.fori_loop(0, inner // TILE, body, 0)


def prepare(rel, small, inner):
    rows = rel.shape[0]
    return pl.pallas_call(
        prepare_kernel,
        in_specs=vmem(1) + hbm(2),
        out_specs=vmem(1)[0],
        out_shape=pltpu.VMEM((rows, inner), F32),
        scratch_shapes=[
            pltpu.VMEM((rows, LANES), BF),
            pltpu.VMEM((rows, rows), BF),
            pltpu.SemaphoreType.DMA((2,)),
        ],
        name="prepare",
        **params(8, 2 * rows * rows * inner, 8_000_000),
    )(rel, *[far(x) for x in small])


def final_kernel(
    core_ref, keep_ref, got_ref, gain_ref, outmap_ref, part_hbm, out_hbm,
    part_ref, enter_ref, held_ref, gets, puts,
):
    rows, inner = part_ref.shape
    half = keep_ref.shape[0]
    steps = rows // TAKEN
    spans = [pl.ds(step * TAKEN, TAKEN) for step in range(steps)]
    copies = [
        fetch(part_hbm.at[span], part_ref.at[span], gets.at[step])
        for step, span in enumerate(spans)
    ]
    core = core_ref[0]
    enter_ref[pl.ds(pl.multiple_of(core * half, half), half)] = keep_ref[...]
    enter_ref[pl.ds(pl.multiple_of((1 - core) * half, half), half)] = got_ref[...]
    puts_made = []
    for step, span in enumerate(spans):
        outer = mm(outmap_ref[span], enter_ref[...])
        copies[step].wait()
        held_ref[span] = (part_ref[span] + gain_ref[span] * outer).astype(BF)
        puts_made.append(fetch(held_ref.at[span], out_hbm.at[span], puts.at[step]))
    for copy in puts_made:
        copy.wait()


def final(core, output_map, part, gain, keep, got):
    rows, inner = part.shape
    states = output_map.shape[1]
    return pl.pallas_call(
        final_kernel,
        in_specs=[pl.BlockSpec(memory_space=pltpu.SMEM)] + vmem(4) + hbm(1),
        out_specs=hbm(1)[0],
        out_shape=jax.ShapeDtypeStruct((rows, inner), BF),
        scratch_shapes=[
            pltpu.VMEM((rows, inner), F32),
            pltpu.VMEM((states, inner), BF),
            pltpu.VMEM((rows, inner), BF),
            pltpu.SemaphoreType.DMA((rows // TAKEN,)),
            pltpu.SemaphoreType.DMA((rows // TAKEN,)),
        ],
        name="final",
        **params(16, 2 * rows * states * inner, 7_000_000),
    )(core, near(keep), near(got), near(gain), near(output_map), far(part))


def on_device(tokens, dt_decay, dest, lengths, w_x, w_bc, conv_x, conv_bc, bias_x, bias_bc, skip):
    rows, width = tokens.shape
    groups = lax.axis_size("ctx")
    ring = lax.axis_size("head")
    first_pos = lax.axis_index("ctx") * rows

    sent = pack(dest[None, :], tokens, jnp.transpose(dt_decay, (2, 1, 0)), groups)
    arrived = lax.all_to_all(sent, "ctx", split_axis=0, concat_axis=0, tiled=True)
    low, edge, high, small = unpack(arrived, width, rows)

    def turned(x, by):
        return lax.ppermute(x, "head", [(i, (i + by) % ring) for i in range(ring)])

    low_left, low_right = turned(low, 1), turned(low, ring - 1)
    halo = lax.ppermute(edge, "ctx", [(i, i + 1) for i in range(groups - 1)])
    high = lax.dynamic_update_slice(high, halo, (0, 0))
    high_right = turned(high, ring - 1)

    starts = jnp.cumsum(lengths) - lengths
    positions = first_pos + jnp.arange(rows, dtype=jnp.int32)
    doc_start = jnp.max(
        jnp.where(starts[None, :] <= positions[:, None], starts[None, :], 0), axis=1
    )
    rel = (positions - doc_start)[:, None]
    me = lax.axis_index("head").astype(jnp.int32)[None]
    inner = w_x.shape[1]
    steps, tail, carry = decay_factors(rel, small, inner)
    later, carry = lax.optimization_barrier((high, carry))
    high_left = turned(later, 1)
    low_far, high_far = turned(low_left, 1), turned(high_right, ring - 1)
    total, w_left, w_right, w_far = project_own(me, low, high, w_x, w_bc)
    total = project_near(
        (low_left, high_left), (low_right, high_right), w_left, w_right, total
    )
    conv, mine, mid, input_map, output_map = front(
        (low_far, high_far), total, w_far, rel, carry, steps, tail,
        conv_x, bias_x[None, :], conv_bc, bias_bc[None, :],
    )
    place = lax.axis_index("ctx").astype(jnp.int32)
    core, chip = (place % 2)[None], (place // 2)[None]
    chips = groups // 2
    peers = [[2 * at + half for at in range(chips)] for half in range(2)]
    swap = [(i, i ^ 1) for i in range(groups)]

    def exchange(x):
        return lax.all_to_all(
            x, "ctx", split_axis=0, concat_axis=0, tiled=True, axis_index_groups=peers
        )

    theirs = lax.ppermute(mine, "ctx", swap)
    sent, kept = combine(core, mine, theirs, chips)
    sent, conv = lax.optimization_barrier((sent, conv))
    gathered = exchange(sent)
    part = inner_part(
        small, rel, input_map, output_map, conv, mid, jnp.repeat(skip, HD)[None, :]
    )
    gathered, part = lax.optimization_barrier((gathered, part))
    entering = scan_shards(chip, gathered, input_map.shape[1] // 16)
    entering, rel = lax.optimization_barrier((entering, rel))
    gain = prepare(rel, small, inner)
    arrived, gain = lax.optimization_barrier((exchange(entering), gain))
    send, keep = entering_halves(core, arrived, kept)
    got = lax.ppermute(send, "ctx", swap)
    return final(core, output_map, part, gain, keep, got)


def solution(mesh):
    in_specs = (
        P("ctx", "head"),
        P("ctx", None, "head"),
        P("ctx"),
        P(),
        P(None, "head"),
        P(),
        P(None, "head"),
        P(),
        P("head"),
        P(),
        P("head"),
    )
    out_specs = P("ctx", "head")
    return jax.shard_map(
        on_device, mesh=mesh, in_specs=in_specs, out_specs=out_specs, check_vma=False
    )
```

```python
import functools

import jax
import jax.numpy as jnp
from jax import lax
from jax.experimental import pallas as pl
from jax.experimental.pallas import tpu as pltpu
from jax.sharding import PartitionSpec as P

BF = jnp.bfloat16
F32 = jnp.float32
CAP = 16
BLK = 256
HD = 64
TILE = 256
HALO = 16
LANES = 128
ROWS_SENT = 88
DECAY_AT = 24
SMALL_END = 44
HIGH_AT, LOW_AT = 44, 108
PIECE = 24
TAKEN = 128


def iota(shape, dim):
    return lax.broadcasted_iota(jnp.int32, shape, dim)


def mm(a, b):
    return jnp.dot(a, b, preferred_element_type=F32)


def mm_nt(a, b):
    return lax.dot_general(a, b, (((1,), (1,)), ((), ())), preferred_element_type=F32)


def mm_tn(a, b):
    return lax.dot_general(a, b, (((0,), (0,)), ((), ())), preferred_element_type=F32)


def as_bf(mask):
    return jnp.where(mask, 1.0, 0.0).astype(BF)


def lower_ones(n):
    return as_bf(iota((n, n), 0) >= iota((n, n), 1))


def params(mib, flops=0, bytes_accessed=0):
    return dict(
        compiler_params=pltpu.CompilerParams(vmem_limit_bytes=mib * 1024 * 1024),
        cost_estimate=pl.CostEstimate(
            flops=flops, bytes_accessed=bytes_accessed, transcendentals=0
        ),
    )


def vmem(count):
    return [pl.BlockSpec(memory_space=pltpu.VMEM)] * count


def near(x):
    return pltpu.with_memory_space_constraint(x, pltpu.VMEM)


def far(x):
    return pltpu.with_memory_space_constraint(x, pltpu.HBM)


def hbm(count):
    return [pl.BlockSpec(memory_space=pltpu.HBM)] * count


def fetch(source, target, sem):
    copy = pltpu.make_async_copy(source, target, sem)
    copy.start()
    return copy


def pack_kernel(
    dest_hbm, steps_hbm, tok_hbm, out_ref,
    dest_ref, steps_ref, tok_ref, slot_ref, code_ref, small_ref, upper_ref,
    sems,
):
    get_dest = fetch(dest_hbm, dest_ref, sems.at[0])
    get_steps = fetch(steps_hbm, steps_ref, sems.at[1])
    rows, width = tok_hbm.shape
    get_tokens = fetch(tok_hbm, tok_ref.at[:, pl.ds(0, width)], sems.at[2])
    groups = code_ref.shape[0]
    heads = steps_ref.shape[0]
    per = 8
    slots = per * CAP
    upper_ref[...] = as_bf(iota((rows, rows), 0) <= iota((rows, rows), 1))
    small_ref[...] = jnp.zeros_like(small_ref)
    get_dest.wait()
    dest = dest_ref[...]
    target = dest // rows
    place = dest % rows + 1
    onehot = iota((groups, rows), 0) == target
    ranks = mm(as_bf(onehot), upper_ref[...])
    rank = jnp.sum(jnp.where(onehot, ranks, 0.0), axis=0, keepdims=True) - 1.0
    rank = rank.astype(jnp.int32)
    slot_ref[...] = target * CAP + rank
    line = iota((LANES, rows), 0)
    codes = jnp.where(line == HIGH_AT + rank, place // 256, 0)
    codes = codes + jnp.where(line == LOW_AT + rank, place % 256, 0)
    code_ref[...] = mm_nt(as_bf(onehot), codes.astype(F32).astype(BF))
    get_steps.wait()
    steps = steps_ref[...].astype(F32)
    small_ref[:heads] = steps[:, 0, :]
    small_ref[DECAY_AT : DECAY_AT + heads] = steps[:, 1, :]
    tok_ref[:, width:] = small_ref[...].T.astype(BF)
    get_tokens.wait()

    def body(step, _):
        slot = slot_ref[...] - step * slots
        here = pl.ds(pl.multiple_of(step * per, per), per)
        select = as_bf(iota((slots, rows), 0) == slot)
        both = mm(select, tok_ref[...])
        sent = both[:, :width].astype(BF)
        for column in range(width // LANES):
            out_ref[here, column * CAP : (column + 1) * CAP, :] = sent[
                :, column * LANES : (column + 1) * LANES
            ].reshape(per, CAP, LANES)
        half = CAP // 2
        small = both[:, width:].reshape(per, CAP, LANES)
        pairs = small[:, :half, :] + pltpu.roll(small[:, half:, :], LANES // 2, 2)
        first = iota((per, half, LANES), 1) == 0
        pairs = pairs + jnp.where(first, code_ref[here][:, None, :], 0.0)
        out_ref[here, ROWS_SENT - half :, :] = pairs.astype(BF)
        return 0

    lax.fori_loop(0, groups // per, body, 0, unroll=8)


def pack(dest, tokens, steps, groups):
    rows, width = tokens.shape
    return pl.pallas_call(
        pack_kernel,
        in_specs=hbm(3),
        out_specs=pl.BlockSpec(memory_space=pltpu.VMEM),
        out_shape=jax.ShapeDtypeStruct((groups, ROWS_SENT, LANES), BF),
        scratch_shapes=[
            pltpu.VMEM((1, rows), jnp.int32),
            pltpu.VMEM(steps.shape, BF),
            pltpu.VMEM((rows, width + LANES), BF),
            pltpu.VMEM((1, rows), jnp.int32),
            pltpu.VMEM((groups, LANES), F32),
            pltpu.VMEM((LANES, rows), F32),
            pltpu.VMEM((rows, rows), BF),
            pltpu.SemaphoreType.DMA((3,)),
        ],
        name="pack",
        **params(16, 2 * rows * groups * CAP * (width + LANES), 4 * rows * width),
    )(far(dest), far(steps), far(tokens))


def places(row_codes, groups, lane_slot, lane_group, count):
    line = iota((LANES, count), 0)
    table = jnp.where(
        line == HIGH_AT + lane_slot, 256.0, jnp.where(line == LOW_AT + lane_slot, 1.0, 0.0)
    ).astype(BF)
    wide = mm(row_codes, table)
    mine = iota((groups, count), 0) == lane_group
    return jnp.sum(jnp.where(mine, wide, 0.0), axis=0, keepdims=True).astype(jnp.int32)


def pick(pos, first, rows):
    return as_bf(iota((rows, pos.shape[1]), 0) + (first + 1) == pos)


def take(select, recv_ref, target, first_row):
    groups = recv_ref.shape[0]
    rows = select.shape[0]
    for column in range(target.shape[1] // LANES):
        source = recv_ref[:, column * CAP : (column + 1) * CAP, :]
        target[first_row : first_row + rows, column * LANES : (column + 1) * LANES] = mm(
            select, source.reshape(groups * CAP, LANES)
        ).astype(BF)


def paired_rows(recv_ref, rows_ref):
    groups = recv_ref.shape[0]
    half = CAP // 2
    pairs = recv_ref[:, ROWS_SENT - half :, :].astype(F32)
    both = jnp.concatenate([pairs, pltpu.roll(pairs, LANES // 2, 2)], axis=1)
    rows_ref[...] = both.reshape(groups * CAP, LANES).astype(BF)
    return pairs[:, 0, :].astype(BF)


def take_small(select, rows_ref):
    values = mm(select, rows_ref[...])
    valid = iota(values.shape, 1) < SMALL_END
    return jnp.where(valid, values, 0.0).astype(BF)


def unpack_low_kernel(
    recv_ref, low_ref, pos_ref, small_hbm, rows_ref, small_ref, sem
):
    groups = recv_ref.shape[0]
    rows = 2 * low_ref.shape[0]
    codes = paired_rows(recv_ref, rows_ref)
    lane = iota((1, groups * CAP), 1)
    pos = places(codes, groups, lane % CAP, lane // CAP, groups * CAP)
    pos_ref[...] = pos
    select = pick(pos, 0, rows // 2)
    small_ref[...] = take_small(select, rows_ref)
    put = fetch(small_ref, small_hbm, sem)
    take(select, recv_ref, low_ref, 0)
    put.wait()


def unpack_high_kernel(
    recv_ref, pos_ref, high_ref, edge_ref, small_hbm, rows_ref, small_ref, sem
):
    rows = high_ref.shape[0] - HALO
    paired_rows(recv_ref, rows_ref)
    select = pick(pos_ref[...], rows, rows)
    small_ref[...] = take_small(select, rows_ref)
    put = fetch(small_ref, small_hbm, sem)
    high_ref[:HALO] = jnp.zeros((HALO, high_ref.shape[1]), BF)
    take(select, recv_ref, high_ref, HALO)
    edge_ref[...] = high_ref[rows:]
    put.wait()


def unpack(recv, width, rows):
    groups = recv.shape[0]
    slots = groups * CAP
    half = rows // 2
    scratch = [
        pltpu.VMEM((slots, LANES), BF),
        pltpu.VMEM((half, LANES), BF),
        pltpu.SemaphoreType.DMA,
    ]
    low, pos, small_low = pl.pallas_call(
        unpack_low_kernel,
        in_specs=vmem(1),
        out_specs=vmem(2) + hbm(1),
        out_shape=[
            jax.ShapeDtypeStruct((half, width), BF),
            jax.ShapeDtypeStruct((1, slots), jnp.int32),
            pltpu.HBM((half, LANES), BF),
        ],
        scratch_shapes=scratch,
        name="unpack_low",
        **params(12, rows * slots * width, 3 * rows * width),
    )(recv)
    high, edge, small_high = pl.pallas_call(
        unpack_high_kernel,
        in_specs=vmem(2),
        out_specs=vmem(2) + hbm(1),
        out_shape=[
            jax.ShapeDtypeStruct((half + HALO, width), BF),
            jax.ShapeDtypeStruct((HALO, width), BF),
            pltpu.HBM((half, LANES), BF),
        ],
        scratch_shapes=scratch,
        name="unpack_high",
        **params(12, rows * slots * width, 3 * rows * width),
    )(recv, pos)
    return low, edge, high, (small_low, small_high)


def conv_silu(ext_ref, weight, bias, rel, rows):
    taps = weight.shape[0]
    total = bias + weight[taps - 1 : taps] * ext_ref[HALO : HALO + rows]
    for lag in range(1, taps):
        tap = taps - 1 - lag
        shifted = ext_ref[HALO - lag : HALO - lag + rows]
        total = total + jnp.where(rel >= lag, weight[tap : tap + 1] * shifted, 0.0)
    return jax.nn.silu(total).astype(BF)


def head_spread(tile, first):
    per = TILE // HD
    return as_bf(iota((128, TILE), 0) == first + per * tile + iota((128, TILE), 1) // HD)


def piece_tiles(dest):
    base = dest // 2 * 5
    first = (base, base + 1) if dest % 2 == 0 else (base + 3, base + 4)
    return first + (base + 2,)


def decay_kernel(
    rel_ref, low_hbm, high_hbm, steps_hbm, tail_hbm, carry_ref,
    small_ref, steps_ref, tail_ref, gets, puts,
):
    tiles, rows = tail_ref.shape[0], tail_ref.shape[1]
    half = rows // 2
    copies = [
        fetch(low_hbm, small_ref.at[pl.ds(0, half)], gets.at[0]),
        fetch(high_hbm, small_ref.at[pl.ds(half, half)], gets.at[1]),
    ]
    for copy in copies:
        copy.wait()
    ones = lower_ones(BLK)
    rel = rel_ref[...]

    def body(tile, _):
        small = small_ref[...]
        steps_ref[tile] = mm(small, head_spread(tile, 0)).astype(BF)
        decays = mm(small, head_spread(tile, DECAY_AT)).astype(BF)
        reach, lines = None, []
        for block in range(rows // BLK):
            span = slice(block * BLK, (block + 1) * BLK)
            cumulative = mm(ones, decays[span])
            last = rel[(block + 1) * BLK - 1 : (block + 1) * BLK]
            end = cumulative[BLK - 1 : BLK]
            behind = BLK - 1 - iota((BLK, 1), 0)
            tail_ref[tile, span] = jnp.where(behind <= last, jnp.exp(end - cumulative), 0.0)
            carry = jnp.where(last > BLK - 1, jnp.exp(end), 0.0)
            lines.append(carry)
            reach = carry if reach is None else reach * carry
        lines.append(reach)
        lines.append(jnp.zeros((8 - len(lines), TILE), F32))
        carry_ref[tile] = jnp.concatenate(lines, axis=0)
        pltpu.make_async_copy(steps_ref.at[tile], steps_hbm.at[tile], puts.at[tile]).start()
        pltpu.make_async_copy(
            tail_ref.at[tile], tail_hbm.at[tile], puts.at[tiles + tile]
        ).start()
        return 0

    lax.fori_loop(0, tiles, body, 0)
    for tile in range(tiles):
        pltpu.make_async_copy(steps_ref.at[tile], steps_hbm.at[tile], puts.at[tile]).wait()
        pltpu.make_async_copy(
            tail_ref.at[tile], tail_hbm.at[tile], puts.at[tiles + tile]
        ).wait()


def decay_factors(rel, small, inner):
    rows = rel.shape[0]
    tiles = inner // TILE
    return pl.pallas_call(
        decay_kernel,
        in_specs=vmem(1) + hbm(2),
        out_specs=hbm(2) + vmem(1),
        out_shape=[
            pltpu.HBM((tiles, rows, TILE), BF),
            pltpu.HBM((tiles, rows, TILE), F32),
            jax.ShapeDtypeStruct((tiles, 8, TILE), F32),
        ],
        scratch_shapes=[
            pltpu.VMEM((rows, LANES), BF),
            pltpu.VMEM((tiles, rows, TILE), BF),
            pltpu.VMEM((tiles, rows, TILE), F32),
            pltpu.SemaphoreType.DMA((2,)),
            pltpu.SemaphoreType.DMA((2 * tiles,)),
        ],
        name="decay_factors",
        **params(16, 4 * rows * BLK * inner, 7_000_000),
    )(rel, *[far(x) for x in small])


def assemble(xe_ref, low_ref, high_ref, columns):
    half = low_ref.shape[0]
    xe_ref[:HALO, columns] = high_ref[:HALO]
    xe_ref[HALO : HALO + half, columns] = low_ref[...]
    xe_ref[HALO + half :, columns] = high_ref[HALO:]


def own_kernel(
    me_ref, low_ref, high_ref, w_hbm, wbc_hbm,
    total_ref, left_ref, right_ref, far_ref, xe_ref, w_ref, gets,
):
    width = low_ref.shape[1]
    inner, rest = w_hbm.shape[1], wbc_hbm.shape[1]
    copies = []
    for turn, target in enumerate((w_ref, left_ref, far_ref, right_ref)):
        owner = lax.rem(me_ref[0] + 4 - turn, 4)
        lines = pl.ds(pl.multiple_of(owner * width, width), width)
        copies.append(
            (
                fetch(w_hbm.at[lines], target.at[:, pl.ds(0, inner)], gets.at[turn, 0]),
                fetch(wbc_hbm.at[lines], target.at[:, pl.ds(inner, rest)], gets.at[turn, 1]),
            )
        )
    assemble(xe_ref, low_ref, high_ref, slice(None))
    for copy in copies[0]:
        copy.wait()

    def body(tile, _):
        columns = pl.ds(pl.multiple_of(tile * TILE, TILE), TILE)
        total_ref[:, columns] = mm(xe_ref[...], w_ref[:, columns])
        return 0

    lax.fori_loop(0, total_ref.shape[1] // TILE, body, 0)
    for pair in copies[1:]:
        for copy in pair:
            copy.wait()


def project_own(me, low, high, w_x, w_bc):
    half, width = low.shape
    rows = 2 * half + HALO
    full = w_x.shape[1] + w_bc.shape[1]
    return pl.pallas_call(
        own_kernel,
        in_specs=[pl.BlockSpec(memory_space=pltpu.SMEM)] + vmem(2) + hbm(2),
        out_specs=vmem(4),
        out_shape=[pltpu.VMEM((rows, full), F32)] + [pltpu.VMEM((width, full), BF)] * 3,
        scratch_shapes=[
            pltpu.VMEM((rows, width), BF),
            pltpu.VMEM((width, full), BF),
            pltpu.SemaphoreType.DMA((4, 2)),
        ],
        name="project_own",
        **params(8, 2 * rows * width * full, 8_000_000),
    )(me, near(low), near(high), far(w_x), far(w_bc))


def near_kernel(
    low1, high1, low3, high3, left_ref, right_ref, sofar_ref, total_ref, xe_ref
):
    width = low1.shape[1]
    assemble(xe_ref, low1, high1, slice(0, width))
    assemble(xe_ref, low3, high3, slice(width, 2 * width))

    def body(tile, _):
        columns = pl.ds(pl.multiple_of(tile * TILE, TILE), TILE)
        weights = jnp.concatenate([left_ref[:, columns], right_ref[:, columns]], axis=0)
        total_ref[:, columns] = sofar_ref[:, columns] + mm(xe_ref[...], weights)
        return 0

    lax.fori_loop(0, total_ref.shape[1] // TILE, body, 0)


def project_near(left, right, w_left, w_right, total):
    width = left[0].shape[1]
    rows, full = total.shape
    return pl.pallas_call(
        near_kernel,
        in_specs=vmem(7),
        out_specs=vmem(1)[0],
        out_shape=pltpu.VMEM((rows, full), F32),
        scratch_shapes=[pltpu.VMEM((rows, 2 * width), BF)],
        name="project_near",
        **params(6, 4 * rows * width * full, 8_000_000),
    )(*[near(x) for x in (*left, *right, w_left, w_right, total)])


def piece_tiles(dest):
    base = dest // 2 * 5
    first = (base, base + 1) if dest % 2 == 0 else (base + 3, base + 4)
    return first + (base + 2,)


def front_kernel(
    low_ref, high_ref, total_ref, w_ref, rel_ref, carry_ref, cx_ref, bx_ref, cb_ref, bb_ref,
    steps_hbm, tail_hbm,
    conv_hbm, mine_ref, in_hbm, outmap_ref,
    steps_ref, tail_ref, conv_ref, in_ref, across_ref,
    xe_ref, ext_ref, gets, puts,
):
    half, width = low_ref.shape
    rows = 2 * half
    states = in_ref.shape[1]
    tiles = conv_ref.shape[0]
    inner = tiles * TILE
    for tile in range(tiles):
        fetch(steps_hbm.at[tile], steps_ref.at[tile], gets.at[0, tile])
        fetch(tail_hbm.at[tile], tail_ref.at[tile], gets.at[1, tile])
    assemble(xe_ref, low_ref, high_ref, slice(None))

    def project(tile):
        columns = slice(tile * TILE, (tile + 1) * TILE)
        total = total_ref[:, columns] + mm(xe_ref[...], w_ref[:, columns])
        ext_ref[tile] = total.astype(BF).astype(F32)

    rel = rel_ref[...]
    for tile in range(tiles + 1):
        project(tile)
    both = conv_silu(ext_ref.at[tiles], cb_ref[...], bb_ref[...], rel, rows)
    in_ref[...] = both[:, :states]
    outmap_ref[...] = both[:, states:]
    put_map = fetch(in_ref, in_hbm, puts.at[0])
    across_ref[...] = both[:, :states].astype(F32).T.astype(BF)
    for tile in range(tiles):
        columns = slice(tile * TILE, (tile + 1) * TILE)
        inner_rows = conv_silu(ext_ref.at[tile], cx_ref[:, columns], bx_ref[:, columns], rel, rows)
        conv_ref[tile] = inner_rows
        fetch(conv_ref.at[tile], conv_hbm.at[:, pl.ds(tile * TILE, TILE)], puts.at[2 + tile])
        for at, (source, target) in enumerate(((steps_hbm, steps_ref), (tail_hbm, tail_ref))):
            pltpu.make_async_copy(source.at[tile], target.at[tile], gets.at[at, tile]).wait()
        inject = (inner_rows.astype(F32) * steps_ref[tile].astype(F32)).astype(BF)
        decayed = (tail_ref[tile] * inject.astype(F32)).astype(BF)
        carried = None
        for block in range(rows // BLK):
            span = slice(block * BLK, (block + 1) * BLK)
            block_state = mm(across_ref[:, span], decayed[span])
            if carried is None:
                carried = block_state
            else:
                carried = carry_ref[tile, block : block + 1] * carried + block_state
        mine_ref[:states, columns] = carried.astype(BF)
        reach = carry_ref[tile, rows // BLK : rows // BLK + 1]
        high = reach.astype(BF).astype(F32)
        line = iota((HALO, TILE), 0)
        codes = jnp.where(line == 0, high, jnp.where(line == 1, reach - high, 0.0))
        mine_ref[states:, columns] = codes.astype(BF)
    put_map.wait()
    for tile in range(tiles):
        pltpu.make_async_copy(
            conv_ref.at[tile], conv_hbm.at[:, pl.ds(tile * TILE, TILE)], puts.at[2 + tile]
        ).wait()


def front(piece, total, w_far, rel, carry, steps, tail, conv_x, bias_x, conv_bc, bias_bc):
    half, width = piece[0].shape
    rows = 2 * half
    inner = conv_x.shape[1]
    states = conv_bc.shape[1] // 2
    tiles = inner // TILE
    return pl.pallas_call(
        front_kernel,
        in_specs=vmem(10) + hbm(2),
        out_specs=hbm(1) + vmem(1) + hbm(1) + vmem(1),
        out_shape=[
            pltpu.HBM((rows, inner), BF),
            jax.ShapeDtypeStruct((states + HALO, inner), BF),
            pltpu.HBM((rows, states), BF),
            pltpu.VMEM((rows, states), BF),
        ],
        scratch_shapes=[
            pltpu.VMEM(steps.shape, BF),
            pltpu.VMEM(tail.shape, F32),
            pltpu.VMEM((tiles, rows, TILE), BF),
            pltpu.VMEM((rows, states), BF),
            pltpu.VMEM((states, rows), BF),
            pltpu.VMEM((rows + HALO, width), BF),
            pltpu.VMEM((tiles + 1, rows + HALO, TILE), F32),
            pltpu.SemaphoreType.DMA((2, tiles)),
            pltpu.SemaphoreType.DMA((tiles + 2,)),
        ],
        name="front",
        **params(20, 2 * rows * width * (inner + 2 * states), 12_000_000),
    )(
        *[near(x) for x in (*piece, total, w_far)], rel, carry,
        conv_x, bias_x, conv_bc, bias_bc, far(steps), far(tail),
    )


def combine_kernel(
    core_ref, mine_ref, theirs_ref, sent_ref, kept_hbm, chip_ref, gain_ref, kept_ref, sem
):
    half, inner = chip_ref.shape
    states = 2 * half
    lines = half // 8
    first = core_ref[0] == 0
    span = pl.ds(pl.multiple_of(core_ref[0] * half, half), half)
    own, other = mine_ref[span].astype(F32), theirs_ref[span].astype(F32)
    own_codes, other_codes = mine_ref[states:].astype(F32), theirs_ref[states:].astype(F32)
    early = jnp.where(first, own, other)
    early_codes = jnp.where(first, own_codes, other_codes)
    late_codes = jnp.where(first, other_codes, own_codes)
    kept_ref[:half] = early.astype(BF)
    kept_ref[half:] = early_codes.astype(BF)
    put = fetch(kept_ref, kept_hbm, sem)
    early_gain = early_codes[0:1] + early_codes[1:2]
    late_gain = late_codes[0:1] + late_codes[1:2]
    chip_ref[...] = late_gain * early + jnp.where(first, other, own)
    gain_ref[...] = jnp.broadcast_to(early_gain * late_gain, gain_ref.shape)

    def tile_of(index):
        column, line = index // lines, index % lines
        return chip_ref[line * 8 : line * 8 + 8, column * LANES : (column + 1) * LANES]

    def codes_of(column):
        gain = gain_ref[0:1, column * LANES : (column + 1) * LANES]
        high = gain.astype(BF).astype(F32)
        return high, gain - high

    for dest in range(sent_ref.shape[0]):
        one, two, shared = piece_tiles(dest)
        columns = [index // lines for index in (one, two, shared)]
        middle = tile_of(shared)[4 * (dest % 2) : 4 * (dest % 2) + 4]
        piece = [tile_of(one), tile_of(two), middle]
        piece += [*codes_of(min(columns)), *codes_of(max(columns))]
        sent_ref[dest] = jnp.concatenate(piece, axis=0).astype(BF)
    put.wait()


def combine(core, mine, theirs, chips):
    inner = mine.shape[1]
    half = (mine.shape[0] - HALO) // 2
    return pl.pallas_call(
        combine_kernel,
        in_specs=[pl.BlockSpec(memory_space=pltpu.SMEM)] + vmem(2),
        out_specs=vmem(1) + hbm(1),
        out_shape=[
            jax.ShapeDtypeStruct((chips, PIECE, LANES), BF),
            pltpu.HBM((half + HALO, inner), BF),
        ],
        scratch_shapes=[
            pltpu.VMEM((half, inner), F32),
            pltpu.VMEM((8, inner), F32),
            pltpu.VMEM((half + HALO, inner), BF),
            pltpu.SemaphoreType.DMA,
        ],
        name="combine",
        **params(8, 1_000_000, 1_500_000),
    )(core, near(mine), near(theirs))


def entering_kernel(core_ref, recv_ref, kept_ref, send_ref, keep_ref, enter_ref):
    half, inner = enter_ref.shape
    lines = half // 8
    where = {}
    for dest in range(recv_ref.shape[0]):
        one, two, shared = piece_tiles(dest)
        where[one] = (dest, 0)
        where[two] = (dest, 1)
        where.setdefault(shared, dest)

    def tile_of(index):
        if isinstance(where[index], tuple):
            dest, at = where[index]
            return recv_ref[dest].astype(F32)[8 * at : 8 * at + 8]
        dest = where[index]
        upper = recv_ref[dest].astype(F32)[16:20]
        lower = recv_ref[dest + 1].astype(F32)[16:20]
        return jnp.concatenate([upper, lower], axis=0)

    for index in range(lines * inner // LANES):
        column, line = index // lines, index % lines
        enter_ref[line * 8 : line * 8 + 8, column * LANES : (column + 1) * LANES] = tile_of(index)
    first = core_ref[0] == 0
    codes = kept_ref[half:].astype(F32)
    early = enter_ref[...]
    late = (codes[0:1] + codes[1:2]) * early + kept_ref[:half].astype(F32)
    send_ref[...] = jnp.where(first, late, early).astype(BF)
    keep_ref[...] = jnp.where(first, early, late).astype(BF)


def entering_halves(core, recv, kept):
    rows, inner = kept.shape
    half = rows - HALO
    return pl.pallas_call(
        entering_kernel,
        in_specs=[pl.BlockSpec(memory_space=pltpu.SMEM)] + vmem(2),
        out_specs=vmem(2),
        out_shape=[jax.ShapeDtypeStruct((half, inner), BF)] * 2,
        scratch_shapes=[pltpu.VMEM((half, inner), F32)],
        name="entering_halves",
        **params(8, 1_000_000, 1_500_000),
    )(core, near(recv), near(kept))


def inner_kernel(
    rel_ref, skip_ref, outmap_ref, low_hbm, high_hbm, in_hbm, conv_hbm, part_hbm,
    small_ref, in_ref, conv_ref, part_ref,
    scores_ref, across_ref, turned_ref, gets, puts,
):
    half = low_hbm.shape[0]
    rows, inner = conv_ref.shape
    tiles = inner // TILE
    per = TILE // HD
    first = [
        fetch(source, target, gets.at[tiles + at])
        for at, (source, target) in enumerate(
            (
                (low_hbm, small_ref.at[pl.ds(0, half)]),
                (high_hbm, small_ref.at[pl.ds(half, half)]),
                (in_hbm, in_ref),
            )
        )
    ]
    for tile in range(tiles):
        columns = pl.ds(tile * TILE, TILE)
        fetch(conv_hbm.at[:, columns], conv_ref.at[:, columns], gets.at[tile])
    for copy in first:
        copy.wait()
    ones = lower_ones(BLK)
    for block in range(rows // BLK):
        span = slice(block * BLK, (block + 1) * BLK)
        scores = mm_nt(outmap_ref[span], in_ref[span])
        gap = iota((BLK, BLK), 0) - iota((BLK, BLK), 1)
        keep = (gap >= 0) & (gap <= rel_ref[span])
        scores_ref[block] = jnp.where(keep, scores, 0.0)
        across_ref[block] = mm(ones, small_ref[span]).T
    turned_ref[...] = in_ref[...].astype(F32).T.astype(BF)

    def body(tile, _):
        columns = pl.ds(pl.multiple_of(tile * TILE, TILE), TILE)
        pltpu.make_async_copy(
            conv_hbm.at[:, columns], conv_ref.at[:, columns], gets.at[tile]
        ).wait()
        small = small_ref[...]
        steps = mm(small, head_spread(tile, 0))
        decays = mm(small, head_spread(tile, DECAY_AT)).astype(BF)
        conv = conv_ref[:, columns].astype(F32)
        inject = (conv * steps).astype(BF)
        lane_head = iota((BLK, TILE), 1) // HD
        state = None
        for block in range(rows // BLK):
            span = slice(block * BLK, (block + 1) * BLK)
            cumulative = mm(ones, decays[span])
            scores = scores_ref[block]
            total = skip_ref[:, columns] * conv[span]
            if block > 0:
                enter = jnp.where(
                    iota((BLK, 1), 0) < rel_ref[span], jnp.exp(cumulative), 0.0
                )
                total = total + enter * mm(outmap_ref[span], state.astype(BF))
            if (block + 1) * BLK < rows:
                last = rel_ref[(block + 1) * BLK - 1 : (block + 1) * BLK]
                end = cumulative[BLK - 1 : BLK]
                behind = BLK - 1 - iota((BLK, 1), 0)
                tail = jnp.where(behind <= last, jnp.exp(end - cumulative), 0.0)
                decayed = (tail * inject[span].astype(F32)).astype(BF)
                block_state = mm(turned_ref[:, span], decayed)
                carry = jnp.where(last > BLK - 1, jnp.exp(end), 0.0)
                state = block_state if state is None else carry * state + block_state
            part = BLK // 2
            pieces = [total[:part], total[part:]]
            for q in range(per):
                down = cumulative[:, q * HD : q * HD + 1]
                across = across_ref[block, pl.ds(DECAY_AT + per * tile + q, 1), :]
                mine = jnp.where(lane_head == q, inject[span], jnp.zeros((), BF))
                for at, seen in ((0, part), (1, BLK)):
                    lines = slice(at * part, (at + 1) * part)
                    gap = jnp.minimum(down[lines] - across[:, :seen], 0.0)
                    weights = (scores[lines, :seen] * jnp.exp(gap)).astype(BF)
                    pieces[at] = pieces[at] + mm(weights, mine[:seen])
            total = jnp.concatenate(pieces, axis=0)
            part_ref[span, columns] = total
        pltpu.make_async_copy(
            part_ref.at[:, columns], part_hbm.at[:, columns], puts.at[tile]
        ).start()
        return 0

    lax.fori_loop(0, tiles, body, 0)
    for tile in range(tiles):
        columns = pl.ds(tile * TILE, TILE)
        pltpu.make_async_copy(
            part_ref.at[:, columns], part_hbm.at[:, columns], puts.at[tile]
        ).wait()


def inner_part(small, rel, input_map, output_map, conv, skip_wide):
    rows, inner = conv.shape
    blocks = rows // BLK
    tiles = inner // TILE
    return pl.pallas_call(
        inner_kernel,
        in_specs=vmem(3) + hbm(4),
        out_specs=hbm(1)[0],
        out_shape=pltpu.HBM((rows, inner), F32),
        scratch_shapes=[
            pltpu.VMEM((rows, LANES), BF),
            pltpu.VMEM(input_map.shape, BF),
            pltpu.VMEM(conv.shape, BF),
            pltpu.VMEM((rows, inner), F32),
            pltpu.VMEM((blocks, BLK, BLK), F32),
            pltpu.VMEM((blocks, 128, BLK), F32),
            pltpu.VMEM((input_map.shape[1], rows), BF),
            pltpu.SemaphoreType.DMA((tiles + 3,)),
            pltpu.SemaphoreType.DMA((tiles,)),
        ],
        name="inner_part",
        **params(24, 8 * rows * BLK * inner, 8_000_000),
    )(rel, skip_wide, near(output_map), *[far(x) for x in (*small, input_map, conv)])


def scan_kernel(lines, me_ref, recv_ref, out_ref):
    groups = recv_ref.shape[0]
    me = me_ref[0]
    base = me // 2 * 5
    odd = lax.rem(me, 2)
    columns = [(base + 3 * odd) // lines, (base + 1 + 3 * odd) // lines, (base + 2) // lines]
    least = jnp.minimum(jnp.minimum(columns[0], columns[1]), columns[2])
    near_first = [
        jnp.where(jnp.full((8, LANES), column, jnp.int32) == least, 1.0, 0.0) for column in columns
    ]

    def body(shard, state):
        piece = recv_ref[shard].astype(F32)
        out_ref[shard] = jnp.concatenate(state, axis=0).astype(BF)
        gain_a = piece[20:21] + piece[21:22]
        gain_b = piece[22:23] + piece[23:24]
        return tuple(
            jnp.where(first > 0.5, gain_a, gain_b) * old + piece[8 * at : 8 * at + 8]
            for at, (first, old) in enumerate(zip(near_first, state))
        )

    lax.fori_loop(0, groups, body, (jnp.zeros((8, LANES), F32),) * 3, unroll=4)


def scan_shards(me, recv, lines):
    return pl.pallas_call(
        functools.partial(scan_kernel, lines),
        in_specs=[pl.BlockSpec(memory_space=pltpu.SMEM)] + vmem(1),
        out_specs=pl.BlockSpec(memory_space=pltpu.VMEM),
        out_shape=pltpu.VMEM(recv.shape, BF),
        name="scan_shards",
        **params(8, 10_000_000, 800_000),
    )(me, near(recv))


def prepare_kernel(
    rel_ref, low_hbm, high_hbm, kept_hbm, gain_ref, kept_ref,
    small_ref, ones_ref, sems,
):
    rows, inner = gain_ref.shape
    half = rows // 2
    get_kept = fetch(kept_hbm, kept_ref, sems.at[2])
    get_small = [
        fetch(low_hbm, small_ref.at[pl.ds(0, half)], sems.at[0]),
        fetch(high_hbm, small_ref.at[pl.ds(half, half)], sems.at[1]),
    ]
    ones_ref[...] = lower_ones(rows)
    reached = iota((rows, 1), 0) < rel_ref[...]
    for copy in get_small:
        copy.wait()

    def body(tile, _):
        decays = mm(small_ref[...], head_spread(tile, DECAY_AT)).astype(BF)
        cumulative = mm(ones_ref[...], decays)
        gain_ref[:, pl.ds(pl.multiple_of(tile * TILE, TILE), TILE)] = jnp.where(
            reached, jnp.exp(cumulative), 0.0
        )
        return 0

    lax.fori_loop(0, inner // TILE, body, 0)
    get_kept.wait()


def prepare(rel, small, kept):
    rows, inner = rel.shape[0], kept.shape[1]
    return pl.pallas_call(
        prepare_kernel,
        in_specs=vmem(1) + hbm(3),
        out_specs=vmem(2),
        out_shape=[
            pltpu.VMEM((rows, inner), F32),
            pltpu.VMEM(kept.shape, BF),
        ],
        scratch_shapes=[
            pltpu.VMEM((rows, LANES), BF),
            pltpu.VMEM((rows, rows), BF),
            pltpu.SemaphoreType.DMA((3,)),
        ],
        name="prepare",
        **params(8, 2 * rows * rows * inner, 8_000_000),
    )(rel, *[far(x) for x in (*small, kept)])


def final_kernel(
    core_ref, keep_ref, got_ref, gain_ref, outmap_ref, part_hbm, out_hbm,
    part_ref, enter_ref, held_ref, gets, puts,
):
    rows, inner = part_ref.shape
    half = keep_ref.shape[0]
    steps = rows // TAKEN
    spans = [pl.ds(step * TAKEN, TAKEN) for step in range(steps)]
    copies = [
        fetch(part_hbm.at[span], part_ref.at[span], gets.at[step])
        for step, span in enumerate(spans)
    ]
    core = core_ref[0]
    enter_ref[pl.ds(pl.multiple_of(core * half, half), half)] = keep_ref[...]
    enter_ref[pl.ds(pl.multiple_of((1 - core) * half, half), half)] = got_ref[...]
    puts_made = []
    for step, span in enumerate(spans):
        outer = mm(outmap_ref[span], enter_ref[...])
        copies[step].wait()
        held_ref[span] = (part_ref[span] + gain_ref[span] * outer).astype(BF)
        puts_made.append(fetch(held_ref.at[span], out_hbm.at[span], puts.at[step]))
    for copy in puts_made:
        copy.wait()


def final(core, output_map, part, gain, keep, got):
    rows, inner = part.shape
    states = output_map.shape[1]
    return pl.pallas_call(
        final_kernel,
        in_specs=[pl.BlockSpec(memory_space=pltpu.SMEM)] + vmem(4) + hbm(1),
        out_specs=hbm(1)[0],
        out_shape=jax.ShapeDtypeStruct((rows, inner), BF),
        scratch_shapes=[
            pltpu.VMEM((rows, inner), F32),
            pltpu.VMEM((states, inner), BF),
            pltpu.VMEM((rows, inner), BF),
            pltpu.SemaphoreType.DMA((rows // TAKEN,)),
            pltpu.SemaphoreType.DMA((rows // TAKEN,)),
        ],
        name="final",
        **params(16, 2 * rows * states * inner, 7_000_000),
    )(core, near(keep), near(got), near(gain), near(output_map), far(part))


def on_device(tokens, dt_decay, dest, lengths, w_x, w_bc, conv_x, conv_bc, bias_x, bias_bc, skip):
    rows, width = tokens.shape
    groups = lax.axis_size("ctx")
    ring = lax.axis_size("head")
    first_pos = lax.axis_index("ctx") * rows

    sent = pack(dest[None, :], tokens, jnp.transpose(dt_decay, (2, 1, 0)), groups)
    arrived = lax.all_to_all(sent, "ctx", split_axis=0, concat_axis=0, tiled=True)
    low, edge, high, small = unpack(arrived, width, rows)

    def turned(x, by):
        return lax.ppermute(x, "head", [(i, (i + by) % ring) for i in range(ring)])

    low_left, low_right = turned(low, 1), turned(low, ring - 1)
    halo = lax.ppermute(edge, "ctx", [(i, i + 1) for i in range(groups - 1)])
    high = lax.dynamic_update_slice(high, halo, (0, 0))
    high_right = turned(high, ring - 1)

    starts = jnp.cumsum(lengths) - lengths
    positions = first_pos + jnp.arange(rows, dtype=jnp.int32)
    doc_start = jnp.max(
        jnp.where(starts[None, :] <= positions[:, None], starts[None, :], 0), axis=1
    )
    rel = (positions - doc_start)[:, None]
    me = lax.axis_index("head").astype(jnp.int32)[None]
    inner = w_x.shape[1]
    steps, tail, carry = decay_factors(rel, small, inner)
    later, carry = lax.optimization_barrier((high, carry))
    high_left = turned(later, 1)
    low_far, high_far = turned(low_left, 1), turned(high_right, ring - 1)
    total, w_left, w_right, w_far = project_own(me, low, high, w_x, w_bc)
    total = project_near(
        (low_left, high_left), (low_right, high_right), w_left, w_right, total
    )
    conv, mine, input_map, output_map = front(
        (low_far, high_far), total, w_far, rel, carry, steps, tail,
        conv_x, bias_x[None, :], conv_bc, bias_bc[None, :],
    )
    place = lax.axis_index("ctx").astype(jnp.int32)
    core, chip = (place % 2)[None], (place // 2)[None]
    chips = groups // 2
    peers = [[2 * at + half for at in range(chips)] for half in range(2)]
    swap = [(i, i ^ 1) for i in range(groups)]

    def exchange(x):
        return lax.all_to_all(
            x, "ctx", split_axis=0, concat_axis=0, tiled=True, axis_index_groups=peers
        )

    theirs = lax.ppermute(mine, "ctx", swap)
    sent, kept = combine(core, mine, theirs, chips)
    sent, conv = lax.optimization_barrier((sent, conv))
    gathered = exchange(sent)
    part = inner_part(
        small, rel, input_map, output_map, conv, jnp.repeat(skip, HD)[None, :]
    )
    gathered, part = lax.optimization_barrier((gathered, part))
    entering = scan_shards(chip, gathered, input_map.shape[1] // 16)
    entering, rel = lax.optimization_barrier((entering, rel))
    gain, kept = prepare(rel, small, kept)
    arrived, gain = lax.optimization_barrier((exchange(entering), gain))
    send, keep = entering_halves(core, arrived, kept)
    got = lax.ppermute(send, "ctx", swap)
    return final(core, output_map, part, gain, keep, got)


def solution(mesh):
    in_specs = (
        P("ctx", "head"),
        P("ctx", None, "head"),
        P("ctx"),
        P(),
        P(None, "head"),
        P(),
        P(None, "head"),
        P(),
        P("head"),
        P(),
        P("head"),
    )
    out_specs = P("ctx", "head")
    return jax.shard_map(
        on_device, mesh=mesh, in_specs=in_specs, out_specs=out_specs, check_vma=False
    )
```

```python
import functools

import jax
import jax.numpy as jnp
from jax import lax
from jax.experimental import pallas as pl
from jax.experimental.pallas import tpu as pltpu
from jax.sharding import PartitionSpec as P

BF = jnp.bfloat16
F32 = jnp.float32
CAP = 16
BLK = 256
HD = 64
TILE = 256
HALO = 16
LANES = 128
ROWS_SENT = 88
DECAY_AT = 24
SMALL_END = 44
HIGH_AT, LOW_AT = 44, 108
PIECE = 24
TAKEN = 128


def iota(shape, dim):
    return lax.broadcasted_iota(jnp.int32, shape, dim)


def mm(a, b):
    return jnp.dot(a, b, preferred_element_type=F32)


def mm_nt(a, b):
    return lax.dot_general(a, b, (((1,), (1,)), ((), ())), preferred_element_type=F32)


def mm_tn(a, b):
    return lax.dot_general(a, b, (((0,), (0,)), ((), ())), preferred_element_type=F32)


def as_bf(mask):
    return jnp.where(mask, 1.0, 0.0).astype(BF)


def lower_ones(n):
    return as_bf(iota((n, n), 0) >= iota((n, n), 1))


def params(mib, flops=0, bytes_accessed=0):
    return dict(
        compiler_params=pltpu.CompilerParams(vmem_limit_bytes=mib * 1024 * 1024),
        cost_estimate=pl.CostEstimate(
            flops=flops, bytes_accessed=bytes_accessed, transcendentals=0
        ),
    )


def vmem(count):
    return [pl.BlockSpec(memory_space=pltpu.VMEM)] * count


def near(x):
    return pltpu.with_memory_space_constraint(x, pltpu.VMEM)


def far(x):
    return pltpu.with_memory_space_constraint(x, pltpu.HBM)


def hbm(count):
    return [pl.BlockSpec(memory_space=pltpu.HBM)] * count


def fetch(source, target, sem):
    copy = pltpu.make_async_copy(source, target, sem)
    copy.start()
    return copy


def pack_kernel(
    dest_hbm, steps_hbm, tok_hbm, out_ref,
    dest_ref, steps_ref, tok_ref, slot_ref, code_ref, small_ref, upper_ref,
    sems,
):
    get_dest = fetch(dest_hbm, dest_ref, sems.at[0])
    get_steps = fetch(steps_hbm, steps_ref, sems.at[1])
    rows, width = tok_hbm.shape
    get_tokens = fetch(tok_hbm, tok_ref.at[:, pl.ds(0, width)], sems.at[2])
    groups = code_ref.shape[0]
    heads = steps_ref.shape[0]
    per = 8
    slots = per * CAP
    upper_ref[...] = as_bf(iota((rows, rows), 0) <= iota((rows, rows), 1))
    small_ref[...] = jnp.zeros_like(small_ref)
    get_dest.wait()
    dest = dest_ref[...]
    target = dest // rows
    place = dest % rows + 1
    onehot = iota((groups, rows), 0) == target
    ranks = mm(as_bf(onehot), upper_ref[...])
    rank = jnp.sum(jnp.where(onehot, ranks, 0.0), axis=0, keepdims=True) - 1.0
    rank = rank.astype(jnp.int32)
    slot_ref[...] = target * CAP + rank
    line = iota((LANES, rows), 0)
    codes = jnp.where(line == HIGH_AT + rank, place // 256, 0)
    codes = codes + jnp.where(line == LOW_AT + rank, place % 256, 0)
    code_ref[...] = mm_nt(as_bf(onehot), codes.astype(F32).astype(BF))
    get_steps.wait()
    steps = steps_ref[...].astype(F32)
    small_ref[:heads] = steps[:, 0, :]
    small_ref[DECAY_AT : DECAY_AT + heads] = steps[:, 1, :]
    tok_ref[:, width:] = small_ref[...].T.astype(BF)
    get_tokens.wait()

    def body(step, _):
        slot = slot_ref[...] - step * slots
        here = pl.ds(pl.multiple_of(step * per, per), per)
        select = as_bf(iota((slots, rows), 0) == slot)
        both = mm(select, tok_ref[...])
        sent = both[:, :width].astype(BF)
        for column in range(width // LANES):
            out_ref[here, column * CAP : (column + 1) * CAP, :] = sent[
                :, column * LANES : (column + 1) * LANES
            ].reshape(per, CAP, LANES)
        half = CAP // 2
        small = both[:, width:].reshape(per, CAP, LANES)
        pairs = small[:, :half, :] + pltpu.roll(small[:, half:, :], LANES // 2, 2)
        first = iota((per, half, LANES), 1) == 0
        pairs = pairs + jnp.where(first, code_ref[here][:, None, :], 0.0)
        out_ref[here, ROWS_SENT - half :, :] = pairs.astype(BF)
        return 0

    lax.fori_loop(0, groups // per, body, 0, unroll=8)


def pack(dest, tokens, steps, groups):
    rows, width = tokens.shape
    return pl.pallas_call(
        pack_kernel,
        in_specs=hbm(3),
        out_specs=pl.BlockSpec(memory_space=pltpu.VMEM),
        out_shape=jax.ShapeDtypeStruct((groups, ROWS_SENT, LANES), BF),
        scratch_shapes=[
            pltpu.VMEM((1, rows), jnp.int32),
            pltpu.VMEM(steps.shape, BF),
            pltpu.VMEM((rows, width + LANES), BF),
            pltpu.VMEM((1, rows), jnp.int32),
            pltpu.VMEM((groups, LANES), F32),
            pltpu.VMEM((LANES, rows), F32),
            pltpu.VMEM((rows, rows), BF),
            pltpu.SemaphoreType.DMA((3,)),
        ],
        name="pack",
        **params(16, 2 * rows * groups * CAP * (width + LANES), 4 * rows * width),
    )(far(dest), far(steps), far(tokens))


def places(row_codes, groups, lane_slot, lane_group, count):
    line = iota((LANES, count), 0)
    table = jnp.where(
        line == HIGH_AT + lane_slot, 256.0, jnp.where(line == LOW_AT + lane_slot, 1.0, 0.0)
    ).astype(BF)
    wide = mm(row_codes, table)
    mine = iota((groups, count), 0) == lane_group
    return jnp.sum(jnp.where(mine, wide, 0.0), axis=0, keepdims=True).astype(jnp.int32)


def pick(pos, first, rows):
    return as_bf(iota((rows, pos.shape[1]), 0) + (first + 1) == pos)


def take(select, recv_ref, target, first_row):
    groups = recv_ref.shape[0]
    rows = select.shape[0]
    for column in range(target.shape[1] // LANES):
        source = recv_ref[:, column * CAP : (column + 1) * CAP, :]
        target[first_row : first_row + rows, column * LANES : (column + 1) * LANES] = mm(
            select, source.reshape(groups * CAP, LANES)
        ).astype(BF)


def paired_rows(recv_ref, rows_ref):
    groups = recv_ref.shape[0]
    half = CAP // 2
    pairs = recv_ref[:, ROWS_SENT - half :, :].astype(F32)
    both = jnp.concatenate([pairs, pltpu.roll(pairs, LANES // 2, 2)], axis=1)
    rows_ref[...] = both.reshape(groups * CAP, LANES).astype(BF)
    return pairs[:, 0, :].astype(BF)


def take_small(select, rows_ref):
    values = mm(select, rows_ref[...])
    valid = iota(values.shape, 1) < SMALL_END
    return jnp.where(valid, values, 0.0).astype(BF)


def unpack_low_kernel(
    recv_ref, low_ref, pos_ref, small_hbm, rows_ref, small_ref, sem
):
    groups = recv_ref.shape[0]
    rows = 2 * low_ref.shape[0]
    codes = paired_rows(recv_ref, rows_ref)
    lane = iota((1, groups * CAP), 1)
    pos = places(codes, groups, lane % CAP, lane // CAP, groups * CAP)
    pos_ref[...] = pos
    select = pick(pos, 0, rows // 2)
    small_ref[...] = take_small(select, rows_ref)
    put = fetch(small_ref, small_hbm, sem)
    take(select, recv_ref, low_ref, 0)
    put.wait()


def unpack_high_kernel(
    recv_ref, pos_ref, high_ref, edge_ref, small_hbm, rows_ref, small_ref, sem
):
    rows = high_ref.shape[0] - HALO
    paired_rows(recv_ref, rows_ref)
    select = pick(pos_ref[...], rows, rows)
    small_ref[...] = take_small(select, rows_ref)
    put = fetch(small_ref, small_hbm, sem)
    high_ref[:HALO] = jnp.zeros((HALO, high_ref.shape[1]), BF)
    take(select, recv_ref, high_ref, HALO)
    edge_ref[...] = high_ref[rows:]
    put.wait()


def unpack(recv, width, rows):
    groups = recv.shape[0]
    slots = groups * CAP
    half = rows // 2
    scratch = [
        pltpu.VMEM((slots, LANES), BF),
        pltpu.VMEM((half, LANES), BF),
        pltpu.SemaphoreType.DMA,
    ]
    low, pos, small_low = pl.pallas_call(
        unpack_low_kernel,
        in_specs=vmem(1),
        out_specs=vmem(2) + hbm(1),
        out_shape=[
            jax.ShapeDtypeStruct((half, width), BF),
            jax.ShapeDtypeStruct((1, slots), jnp.int32),
            pltpu.HBM((half, LANES), BF),
        ],
        scratch_shapes=scratch,
        name="unpack_low",
        **params(12, rows * slots * width, 3 * rows * width),
    )(recv)
    high, edge, small_high = pl.pallas_call(
        unpack_high_kernel,
        in_specs=vmem(2),
        out_specs=vmem(2) + hbm(1),
        out_shape=[
            jax.ShapeDtypeStruct((half + HALO, width), BF),
            jax.ShapeDtypeStruct((HALO, width), BF),
            pltpu.HBM((half, LANES), BF),
        ],
        scratch_shapes=scratch,
        name="unpack_high",
        **params(12, rows * slots * width, 3 * rows * width),
    )(recv, pos)
    return low, edge, high, (small_low, small_high)


def conv_silu(ext_ref, weight, bias, rel, rows):
    taps = weight.shape[0]
    total = bias + weight[taps - 1 : taps] * ext_ref[HALO : HALO + rows]
    for lag in range(1, taps):
        tap = taps - 1 - lag
        shifted = ext_ref[HALO - lag : HALO - lag + rows]
        total = total + jnp.where(rel >= lag, weight[tap : tap + 1] * shifted, 0.0)
    return jax.nn.silu(total).astype(BF)


def head_spread(tile, first):
    per = TILE // HD
    return as_bf(iota((128, TILE), 0) == first + per * tile + iota((128, TILE), 1) // HD)


def piece_tiles(dest):
    base = dest // 2 * 5
    first = (base, base + 1) if dest % 2 == 0 else (base + 3, base + 4)
    return first + (base + 2,)


def decay_kernel(
    rel_ref, low_hbm, high_hbm, steps_hbm, tail_hbm, carry_ref,
    small_ref, steps_ref, tail_ref, gets, puts,
):
    tiles, rows = tail_ref.shape[0], tail_ref.shape[1]
    half = rows // 2
    copies = [
        fetch(low_hbm, small_ref.at[pl.ds(0, half)], gets.at[0]),
        fetch(high_hbm, small_ref.at[pl.ds(half, half)], gets.at[1]),
    ]
    for copy in copies:
        copy.wait()
    ones = lower_ones(BLK)
    rel = rel_ref[...]

    def body(tile, _):
        small = small_ref[...]
        steps_ref[tile] = mm(small, head_spread(tile, 0)).astype(BF)
        decays = mm(small, head_spread(tile, DECAY_AT)).astype(BF)
        reach, lines = None, []
        for block in range(rows // BLK):
            span = slice(block * BLK, (block + 1) * BLK)
            cumulative = mm(ones, decays[span])
            last = rel[(block + 1) * BLK - 1 : (block + 1) * BLK]
            end = cumulative[BLK - 1 : BLK]
            behind = BLK - 1 - iota((BLK, 1), 0)
            tail_ref[tile, span] = jnp.where(behind <= last, jnp.exp(end - cumulative), 0.0)
            carry = jnp.where(last > BLK - 1, jnp.exp(end), 0.0)
            lines.append(carry)
            reach = carry if reach is None else reach * carry
        lines.append(reach)
        lines.append(jnp.zeros((8 - len(lines), TILE), F32))
        carry_ref[tile] = jnp.concatenate(lines, axis=0)
        pltpu.make_async_copy(steps_ref.at[tile], steps_hbm.at[tile], puts.at[tile]).start()
        pltpu.make_async_copy(
            tail_ref.at[tile], tail_hbm.at[tile], puts.at[tiles + tile]
        ).start()
        return 0

    lax.fori_loop(0, tiles, body, 0)
    for tile in range(tiles):
        pltpu.make_async_copy(steps_ref.at[tile], steps_hbm.at[tile], puts.at[tile]).wait()
        pltpu.make_async_copy(
            tail_ref.at[tile], tail_hbm.at[tile], puts.at[tiles + tile]
        ).wait()


def decay_factors(rel, small, inner):
    rows = rel.shape[0]
    tiles = inner // TILE
    return pl.pallas_call(
        decay_kernel,
        in_specs=vmem(1) + hbm(2),
        out_specs=hbm(2) + vmem(1),
        out_shape=[
            pltpu.HBM((tiles, rows, TILE), BF),
            pltpu.HBM((tiles, rows, TILE), F32),
            jax.ShapeDtypeStruct((tiles, 8, TILE), F32),
        ],
        scratch_shapes=[
            pltpu.VMEM((rows, LANES), BF),
            pltpu.VMEM((tiles, rows, TILE), BF),
            pltpu.VMEM((tiles, rows, TILE), F32),
            pltpu.SemaphoreType.DMA((2,)),
            pltpu.SemaphoreType.DMA((2 * tiles,)),
        ],
        name="decay_factors",
        **params(16, 4 * rows * BLK * inner, 7_000_000),
    )(rel, *[far(x) for x in small])


def assemble(xe_ref, low_ref, high_ref, columns):
    half = low_ref.shape[0]
    xe_ref[:HALO, columns] = high_ref[:HALO]
    xe_ref[HALO : HALO + half, columns] = low_ref[...]
    xe_ref[HALO + half :, columns] = high_ref[HALO:]


def own_kernel(
    me_ref, low_ref, high_ref, w_hbm, wbc_hbm,
    total_ref, left_ref, right_ref, far_ref, xe_ref, w_ref, gets,
):
    width = low_ref.shape[1]
    inner, rest = w_hbm.shape[1], wbc_hbm.shape[1]
    copies = []
    for turn, target in enumerate((w_ref, left_ref, far_ref, right_ref)):
        owner = lax.rem(me_ref[0] + 4 - turn, 4)
        lines = pl.ds(pl.multiple_of(owner * width, width), width)
        copies.append(
            (
                fetch(w_hbm.at[lines], target.at[:, pl.ds(0, inner)], gets.at[turn, 0]),
                fetch(wbc_hbm.at[lines], target.at[:, pl.ds(inner, rest)], gets.at[turn, 1]),
            )
        )
    assemble(xe_ref, low_ref, high_ref, slice(None))
    for copy in copies[0]:
        copy.wait()

    def body(tile, _):
        columns = pl.ds(pl.multiple_of(tile * TILE, TILE), TILE)
        total_ref[:, columns] = mm(xe_ref[...], w_ref[:, columns])
        return 0

    lax.fori_loop(0, total_ref.shape[1] // TILE, body, 0)
    for pair in copies[1:]:
        for copy in pair:
            copy.wait()


def project_own(me, low, high, w_x, w_bc):
    half, width = low.shape
    rows = 2 * half + HALO
    full = w_x.shape[1] + w_bc.shape[1]
    return pl.pallas_call(
        own_kernel,
        in_specs=[pl.BlockSpec(memory_space=pltpu.SMEM)] + vmem(2) + hbm(2),
        out_specs=vmem(4),
        out_shape=[pltpu.VMEM((rows, full), F32)] + [pltpu.VMEM((width, full), BF)] * 3,
        scratch_shapes=[
            pltpu.VMEM((rows, width), BF),
            pltpu.VMEM((width, full), BF),
            pltpu.SemaphoreType.DMA((4, 2)),
        ],
        name="project_own",
        **params(8, 2 * rows * width * full, 8_000_000),
    )(me, near(low), near(high), far(w_x), far(w_bc))


def near_kernel(
    low1, high1, low3, high3, left_ref, right_ref, sofar_ref, total_ref, xe_ref
):
    width = low1.shape[1]
    assemble(xe_ref, low1, high1, slice(0, width))
    assemble(xe_ref, low3, high3, slice(width, 2 * width))

    def body(tile, _):
        columns = pl.ds(pl.multiple_of(tile * TILE, TILE), TILE)
        weights = jnp.concatenate([left_ref[:, columns], right_ref[:, columns]], axis=0)
        total_ref[:, columns] = sofar_ref[:, columns] + mm(xe_ref[...], weights)
        return 0

    lax.fori_loop(0, total_ref.shape[1] // TILE, body, 0)


def project_near(left, right, w_left, w_right, total):
    width = left[0].shape[1]
    rows, full = total.shape
    return pl.pallas_call(
        near_kernel,
        in_specs=vmem(7),
        out_specs=vmem(1)[0],
        out_shape=pltpu.VMEM((rows, full), F32),
        scratch_shapes=[pltpu.VMEM((rows, 2 * width), BF)],
        name="project_near",
        **params(6, 4 * rows * width * full, 8_000_000),
    )(*[near(x) for x in (*left, *right, w_left, w_right, total)])


def piece_tiles(dest):
    base = dest // 2 * 5
    first = (base, base + 1) if dest % 2 == 0 else (base + 3, base + 4)
    return first + (base + 2,)


def front_kernel(
    low_ref, high_ref, total_ref, w_ref, rel_ref, carry_ref, cx_ref, bx_ref, cb_ref, bb_ref,
    steps_hbm, tail_hbm,
    conv_hbm, mine_ref, in_hbm, outmap_ref,
    steps_ref, tail_ref, conv_ref, in_ref, across_ref,
    xe_ref, ext_ref, gets, puts,
):
    half, width = low_ref.shape
    rows = 2 * half
    states = in_ref.shape[1]
    tiles = conv_ref.shape[0]
    inner = tiles * TILE
    for tile in range(tiles):
        fetch(steps_hbm.at[tile], steps_ref.at[tile], gets.at[0, tile])
        fetch(tail_hbm.at[tile], tail_ref.at[tile], gets.at[1, tile])
    assemble(xe_ref, low_ref, high_ref, slice(None))

    def project(tile):
        columns = slice(tile * TILE, (tile + 1) * TILE)
        total = total_ref[:, columns] + mm(xe_ref[...], w_ref[:, columns])
        ext_ref[tile] = total.astype(BF).astype(F32)

    rel = rel_ref[...]
    for tile in range(tiles + 1):
        project(tile)
    both = conv_silu(ext_ref.at[tiles], cb_ref[...], bb_ref[...], rel, rows)
    in_ref[...] = both[:, :states]
    outmap_ref[...] = both[:, states:]
    put_map = fetch(in_ref, in_hbm, puts.at[0])
    across_ref[...] = both[:, :states].astype(F32).T.astype(BF)
    for tile in range(tiles):
        columns = slice(tile * TILE, (tile + 1) * TILE)
        inner_rows = conv_silu(ext_ref.at[tile], cx_ref[:, columns], bx_ref[:, columns], rel, rows)
        conv_ref[tile] = inner_rows
        fetch(conv_ref.at[tile], conv_hbm.at[:, pl.ds(tile * TILE, TILE)], puts.at[2 + tile])
        for at, (source, target) in enumerate(((steps_hbm, steps_ref), (tail_hbm, tail_ref))):
            pltpu.make_async_copy(source.at[tile], target.at[tile], gets.at[at, tile]).wait()
        inject = (inner_rows.astype(F32) * steps_ref[tile].astype(F32)).astype(BF)
        decayed = (tail_ref[tile] * inject.astype(F32)).astype(BF)
        carried = None
        for block in range(rows // BLK):
            span = slice(block * BLK, (block + 1) * BLK)
            block_state = mm(across_ref[:, span], decayed[span])
            if carried is None:
                carried = block_state
            else:
                carried = carry_ref[tile, block : block + 1] * carried + block_state
        mine_ref[:states, columns] = carried.astype(BF)
        reach = carry_ref[tile, rows // BLK : rows // BLK + 1]
        high = reach.astype(BF).astype(F32)
        line = iota((HALO, TILE), 0)
        codes = jnp.where(line == 0, high, jnp.where(line == 1, reach - high, 0.0))
        mine_ref[states:, columns] = codes.astype(BF)
    put_map.wait()
    for tile in range(tiles):
        pltpu.make_async_copy(
            conv_ref.at[tile], conv_hbm.at[:, pl.ds(tile * TILE, TILE)], puts.at[2 + tile]
        ).wait()


def front(piece, total, w_far, rel, carry, steps, tail, conv_x, bias_x, conv_bc, bias_bc):
    half, width = piece[0].shape
    rows = 2 * half
    inner = conv_x.shape[1]
    states = conv_bc.shape[1] // 2
    tiles = inner // TILE
    return pl.pallas_call(
        front_kernel,
        in_specs=vmem(10) + hbm(2),
        out_specs=hbm(1) + vmem(1) + hbm(1) + vmem(1),
        out_shape=[
            pltpu.HBM((rows, inner), BF),
            jax.ShapeDtypeStruct((states + HALO, inner), BF),
            pltpu.HBM((rows, states), BF),
            pltpu.VMEM((rows, states), BF),
        ],
        scratch_shapes=[
            pltpu.VMEM(steps.shape, BF),
            pltpu.VMEM(tail.shape, F32),
            pltpu.VMEM((tiles, rows, TILE), BF),
            pltpu.VMEM((rows, states), BF),
            pltpu.VMEM((states, rows), BF),
            pltpu.VMEM((rows + HALO, width), BF),
            pltpu.VMEM((tiles + 1, rows + HALO, TILE), F32),
            pltpu.SemaphoreType.DMA((2, tiles)),
            pltpu.SemaphoreType.DMA((tiles + 2,)),
        ],
        name="front",
        **params(20, 2 * rows * width * (inner + 2 * states), 12_000_000),
    )(
        *[near(x) for x in (*piece, total, w_far)], rel, carry,
        conv_x, bias_x, conv_bc, bias_bc, far(steps), far(tail),
    )


def combine_kernel(
    core_ref, mine_ref, theirs_ref, sent_ref, kept_ref, chip_ref, gain_ref
):
    half, inner = chip_ref.shape
    states = 2 * half
    lines = half // 8
    first = core_ref[0] == 0
    span = pl.ds(pl.multiple_of(core_ref[0] * half, half), half)
    own, other = mine_ref[span].astype(F32), theirs_ref[span].astype(F32)
    own_codes, other_codes = mine_ref[states:].astype(F32), theirs_ref[states:].astype(F32)
    early = jnp.where(first, own, other)
    early_codes = jnp.where(first, own_codes, other_codes)
    late_codes = jnp.where(first, other_codes, own_codes)
    kept_ref[:half] = early.astype(BF)
    kept_ref[half:] = early_codes.astype(BF)
    early_gain = early_codes[0:1] + early_codes[1:2]
    late_gain = late_codes[0:1] + late_codes[1:2]
    chip_ref[...] = late_gain * early + jnp.where(first, other, own)
    gain_ref[...] = jnp.broadcast_to(early_gain * late_gain, gain_ref.shape)

    def tile_of(index):
        column, line = index // lines, index % lines
        return chip_ref[line * 8 : line * 8 + 8, column * LANES : (column + 1) * LANES]

    def codes_of(column):
        gain = gain_ref[0:1, column * LANES : (column + 1) * LANES]
        high = gain.astype(BF).astype(F32)
        return high, gain - high

    for dest in range(sent_ref.shape[0]):
        one, two, shared = piece_tiles(dest)
        columns = [index // lines for index in (one, two, shared)]
        middle = tile_of(shared)[4 * (dest % 2) : 4 * (dest % 2) + 4]
        piece = [tile_of(one), tile_of(two), middle]
        piece += [*codes_of(min(columns)), *codes_of(max(columns))]
        sent_ref[dest] = jnp.concatenate(piece, axis=0).astype(BF)


def combine(core, mine, theirs, chips):
    inner = mine.shape[1]
    half = (mine.shape[0] - HALO) // 2
    return pl.pallas_call(
        combine_kernel,
        in_specs=[pl.BlockSpec(memory_space=pltpu.SMEM)] + vmem(2),
        out_specs=vmem(2),
        out_shape=[
            jax.ShapeDtypeStruct((chips, PIECE, LANES), BF),
            pltpu.VMEM((half + HALO, inner), BF),
        ],
        scratch_shapes=[
            pltpu.VMEM((half, inner), F32),
            pltpu.VMEM((8, inner), F32),
        ],
        name="combine",
        **params(8, 1_000_000, 1_500_000),
    )(core, near(mine), near(theirs))


def entering_kernel(core_ref, recv_ref, kept_ref, send_ref, keep_ref, enter_ref):
    half, inner = enter_ref.shape
    lines = half // 8
    where = {}
    for dest in range(recv_ref.shape[0]):
        one, two, shared = piece_tiles(dest)
        where[one] = (dest, 0)
        where[two] = (dest, 1)
        where.setdefault(shared, dest)

    def tile_of(index):
        if isinstance(where[index], tuple):
            dest, at = where[index]
            return recv_ref[dest].astype(F32)[8 * at : 8 * at + 8]
        dest = where[index]
        upper = recv_ref[dest].astype(F32)[16:20]
        lower = recv_ref[dest + 1].astype(F32)[16:20]
        return jnp.concatenate([upper, lower], axis=0)

    for index in range(lines * inner // LANES):
        column, line = index // lines, index % lines
        enter_ref[line * 8 : line * 8 + 8, column * LANES : (column + 1) * LANES] = tile_of(index)
    first = core_ref[0] == 0
    codes = kept_ref[half:].astype(F32)
    early = enter_ref[...]
    late = (codes[0:1] + codes[1:2]) * early + kept_ref[:half].astype(F32)
    send_ref[...] = jnp.where(first, late, early).astype(BF)
    keep_ref[...] = jnp.where(first, early, late).astype(BF)


def entering_halves(core, recv, kept):
    rows, inner = kept.shape
    half = rows - HALO
    return pl.pallas_call(
        entering_kernel,
        in_specs=[pl.BlockSpec(memory_space=pltpu.SMEM)] + vmem(2),
        out_specs=vmem(2),
        out_shape=[jax.ShapeDtypeStruct((half, inner), BF)] * 2,
        scratch_shapes=[pltpu.VMEM((half, inner), F32)],
        name="entering_halves",
        **params(8, 1_000_000, 1_500_000),
    )(core, near(recv), near(kept))


def inner_kernel(
    rel_ref, skip_ref, outmap_ref, low_hbm, high_hbm, in_hbm, conv_hbm, part_hbm,
    small_ref, in_ref, conv_ref, part_ref,
    scores_ref, across_ref, turned_ref, gets, puts,
):
    half = low_hbm.shape[0]
    rows, inner = conv_ref.shape
    tiles = inner // TILE
    per = TILE // HD
    first = [
        fetch(source, target, gets.at[tiles + at])
        for at, (source, target) in enumerate(
            (
                (low_hbm, small_ref.at[pl.ds(0, half)]),
                (high_hbm, small_ref.at[pl.ds(half, half)]),
                (in_hbm, in_ref),
            )
        )
    ]
    for tile in range(tiles):
        columns = pl.ds(tile * TILE, TILE)
        fetch(conv_hbm.at[:, columns], conv_ref.at[:, columns], gets.at[tile])
    for copy in first:
        copy.wait()
    ones = lower_ones(BLK)
    for block in range(rows // BLK):
        span = slice(block * BLK, (block + 1) * BLK)
        scores = mm_nt(outmap_ref[span], in_ref[span])
        gap = iota((BLK, BLK), 0) - iota((BLK, BLK), 1)
        keep = (gap >= 0) & (gap <= rel_ref[span])
        scores_ref[block] = jnp.where(keep, scores, 0.0)
        across_ref[block] = mm(ones, small_ref[span]).T
    turned_ref[...] = in_ref[...].astype(F32).T.astype(BF)

    def body(tile, _):
        columns = pl.ds(pl.multiple_of(tile * TILE, TILE), TILE)
        pltpu.make_async_copy(
            conv_hbm.at[:, columns], conv_ref.at[:, columns], gets.at[tile]
        ).wait()
        small = small_ref[...]
        steps = mm(small, head_spread(tile, 0))
        decays = mm(small, head_spread(tile, DECAY_AT)).astype(BF)
        conv = conv_ref[:, columns].astype(F32)
        inject = (conv * steps).astype(BF)
        lane_head = iota((BLK, TILE), 1) // HD
        state = None
        for block in range(rows // BLK):
            span = slice(block * BLK, (block + 1) * BLK)
            cumulative = mm(ones, decays[span])
            scores = scores_ref[block]
            total = skip_ref[:, columns] * conv[span]
            if block > 0:
                enter = jnp.where(
                    iota((BLK, 1), 0) < rel_ref[span], jnp.exp(cumulative), 0.0
                )
                total = total + enter * mm(outmap_ref[span], state.astype(BF))
            if (block + 1) * BLK < rows:
                last = rel_ref[(block + 1) * BLK - 1 : (block + 1) * BLK]
                end = cumulative[BLK - 1 : BLK]
                behind = BLK - 1 - iota((BLK, 1), 0)
                tail = jnp.where(behind <= last, jnp.exp(end - cumulative), 0.0)
                decayed = (tail * inject[span].astype(F32)).astype(BF)
                block_state = mm(turned_ref[:, span], decayed)
                carry = jnp.where(last > BLK - 1, jnp.exp(end), 0.0)
                state = block_state if state is None else carry * state + block_state
            part = BLK // 2
            pieces = [total[:part], total[part:]]
            for q in range(per):
                down = cumulative[:, q * HD : q * HD + 1]
                across = across_ref[block, pl.ds(DECAY_AT + per * tile + q, 1), :]
                mine = jnp.where(lane_head == q, inject[span], jnp.zeros((), BF))
                for at, seen in ((0, part), (1, BLK)):
                    lines = slice(at * part, (at + 1) * part)
                    gap = jnp.minimum(down[lines] - across[:, :seen], 0.0)
                    weights = (scores[lines, :seen] * jnp.exp(gap)).astype(BF)
                    pieces[at] = pieces[at] + mm(weights, mine[:seen])
            total = jnp.concatenate(pieces, axis=0)
            part_ref[span, columns] = total
        pltpu.make_async_copy(
            part_ref.at[:, columns], part_hbm.at[:, columns], puts.at[tile]
        ).start()
        return 0

    lax.fori_loop(0, tiles, body, 0)
    for tile in range(tiles):
        columns = pl.ds(tile * TILE, TILE)
        pltpu.make_async_copy(
            part_ref.at[:, columns], part_hbm.at[:, columns], puts.at[tile]
        ).wait()


def inner_part(small, rel, input_map, output_map, conv, skip_wide):
    rows, inner = conv.shape
    blocks = rows // BLK
    tiles = inner // TILE
    return pl.pallas_call(
        inner_kernel,
        in_specs=vmem(3) + hbm(4),
        out_specs=hbm(1)[0],
        out_shape=pltpu.HBM((rows, inner), F32),
        scratch_shapes=[
            pltpu.VMEM((rows, LANES), BF),
            pltpu.VMEM(input_map.shape, BF),
            pltpu.VMEM(conv.shape, BF),
            pltpu.VMEM((rows, inner), F32),
            pltpu.VMEM((blocks, BLK, BLK), F32),
            pltpu.VMEM((blocks, 128, BLK), F32),
            pltpu.VMEM((input_map.shape[1], rows), BF),
            pltpu.SemaphoreType.DMA((tiles + 3,)),
            pltpu.SemaphoreType.DMA((tiles,)),
        ],
        name="inner_part",
        **params(24, 8 * rows * BLK * inner, 8_000_000),
    )(rel, skip_wide, near(output_map), *[far(x) for x in (*small, input_map, conv)])


def scan_kernel(lines, me_ref, recv_ref, out_ref):
    groups = recv_ref.shape[0]
    me = me_ref[0]
    base = me // 2 * 5
    odd = lax.rem(me, 2)
    columns = [(base + 3 * odd) // lines, (base + 1 + 3 * odd) // lines, (base + 2) // lines]
    least = jnp.minimum(jnp.minimum(columns[0], columns[1]), columns[2])
    near_first = [
        jnp.where(jnp.full((8, LANES), column, jnp.int32) == least, 1.0, 0.0) for column in columns
    ]

    def body(shard, state):
        piece = recv_ref[shard].astype(F32)
        out_ref[shard] = jnp.concatenate(state, axis=0).astype(BF)
        gain_a = piece[20:21] + piece[21:22]
        gain_b = piece[22:23] + piece[23:24]
        return tuple(
            jnp.where(first > 0.5, gain_a, gain_b) * old + piece[8 * at : 8 * at + 8]
            for at, (first, old) in enumerate(zip(near_first, state))
        )

    lax.fori_loop(0, groups, body, (jnp.zeros((8, LANES), F32),) * 3, unroll=4)


def scan_shards(me, recv, lines):
    return pl.pallas_call(
        functools.partial(scan_kernel, lines),
        in_specs=[pl.BlockSpec(memory_space=pltpu.SMEM)] + vmem(1),
        out_specs=pl.BlockSpec(memory_space=pltpu.VMEM),
        out_shape=pltpu.VMEM(recv.shape, BF),
        name="scan_shards",
        **params(8, 10_000_000, 800_000),
    )(me, near(recv))


def prepare_kernel(
    rel_ref, low_hbm, high_hbm, gain_ref,
    small_ref, ones_ref, sems,
):
    rows, inner = gain_ref.shape
    half = rows // 2
    get_small = [
        fetch(low_hbm, small_ref.at[pl.ds(0, half)], sems.at[0]),
        fetch(high_hbm, small_ref.at[pl.ds(half, half)], sems.at[1]),
    ]
    ones_ref[...] = lower_ones(rows)
    reached = iota((rows, 1), 0) < rel_ref[...]
    for copy in get_small:
        copy.wait()

    def body(tile, _):
        decays = mm(small_ref[...], head_spread(tile, DECAY_AT)).astype(BF)
        cumulative = mm(ones_ref[...], decays)
        gain_ref[:, pl.ds(pl.multiple_of(tile * TILE, TILE), TILE)] = jnp.where(
            reached, jnp.exp(cumulative), 0.0
        )
        return 0

    lax.fori_loop(0, inner // TILE, body, 0)


def prepare(rel, small, inner):
    rows = rel.shape[0]
    return pl.pallas_call(
        prepare_kernel,
        in_specs=vmem(1) + hbm(2),
        out_specs=vmem(1)[0],
        out_shape=pltpu.VMEM((rows, inner), F32),
        scratch_shapes=[
            pltpu.VMEM((rows, LANES), BF),
            pltpu.VMEM((rows, rows), BF),
            pltpu.SemaphoreType.DMA((2,)),
        ],
        name="prepare",
        **params(8, 2 * rows * rows * inner, 8_000_000),
    )(rel, *[far(x) for x in small])


def final_kernel(
    core_ref, keep_ref, got_ref, gain_ref, outmap_ref, part_hbm, out_hbm,
    part_ref, enter_ref, held_ref, gets, puts,
):
    rows, inner = part_ref.shape
    half = keep_ref.shape[0]
    steps = rows // TAKEN
    spans = [pl.ds(step * TAKEN, TAKEN) for step in range(steps)]
    copies = [
        fetch(part_hbm.at[span], part_ref.at[span], gets.at[step])
        for step, span in enumerate(spans)
    ]
    core = core_ref[0]
    enter_ref[pl.ds(pl.multiple_of(core * half, half), half)] = keep_ref[...]
    enter_ref[pl.ds(pl.multiple_of((1 - core) * half, half), half)] = got_ref[...]
    puts_made = []
    for step, span in enumerate(spans):
        outer = mm(outmap_ref[span], enter_ref[...])
        copies[step].wait()
        held_ref[span] = (part_ref[span] + gain_ref[span] * outer).astype(BF)
        puts_made.append(fetch(held_ref.at[span], out_hbm.at[span], puts.at[step]))
    for copy in puts_made:
        copy.wait()


def final(core, output_map, part, gain, keep, got):
    rows, inner = part.shape
    states = output_map.shape[1]
    return pl.pallas_call(
        final_kernel,
        in_specs=[pl.BlockSpec(memory_space=pltpu.SMEM)] + vmem(4) + hbm(1),
        out_specs=hbm(1)[0],
        out_shape=jax.ShapeDtypeStruct((rows, inner), BF),
        scratch_shapes=[
            pltpu.VMEM((rows, inner), F32),
            pltpu.VMEM((states, inner), BF),
            pltpu.VMEM((rows, inner), BF),
            pltpu.SemaphoreType.DMA((rows // TAKEN,)),
            pltpu.SemaphoreType.DMA((rows // TAKEN,)),
        ],
        name="final",
        **params(16, 2 * rows * states * inner, 7_000_000),
    )(core, near(keep), near(got), near(gain), near(output_map), far(part))


def on_device(tokens, dt_decay, dest, lengths, w_x, w_bc, conv_x, conv_bc, bias_x, bias_bc, skip):
    rows, width = tokens.shape
    groups = lax.axis_size("ctx")
    ring = lax.axis_size("head")
    first_pos = lax.axis_index("ctx") * rows

    sent = pack(dest[None, :], tokens, jnp.transpose(dt_decay, (2, 1, 0)), groups)
    arrived = lax.all_to_all(sent, "ctx", split_axis=0, concat_axis=0, tiled=True)
    low, edge, high, small = unpack(arrived, width, rows)

    def turned(x, by):
        return lax.ppermute(x, "head", [(i, (i + by) % ring) for i in range(ring)])

    low_left, low_right = turned(low, 1), turned(low, ring - 1)
    halo = lax.ppermute(edge, "ctx", [(i, i + 1) for i in range(groups - 1)])
    high = lax.dynamic_update_slice(high, halo, (0, 0))
    high_right = turned(high, ring - 1)

    starts = jnp.cumsum(lengths) - lengths
    positions = first_pos + jnp.arange(rows, dtype=jnp.int32)
    doc_start = jnp.max(
        jnp.where(starts[None, :] <= positions[:, None], starts[None, :], 0), axis=1
    )
    rel = (positions - doc_start)[:, None]
    me = lax.axis_index("head").astype(jnp.int32)[None]
    inner = w_x.shape[1]
    steps, tail, carry = decay_factors(rel, small, inner)
    later, carry = lax.optimization_barrier((high, carry))
    high_left = turned(later, 1)
    low_far, high_far = turned(low_left, 1), turned(high_right, ring - 1)
    total, w_left, w_right, w_far = project_own(me, low, high, w_x, w_bc)
    total = project_near(
        (low_left, high_left), (low_right, high_right), w_left, w_right, total
    )
    conv, mine, input_map, output_map = front(
        (low_far, high_far), total, w_far, rel, carry, steps, tail,
        conv_x, bias_x[None, :], conv_bc, bias_bc[None, :],
    )
    place = lax.axis_index("ctx").astype(jnp.int32)
    core, chip = (place % 2)[None], (place // 2)[None]
    chips = groups // 2
    peers = [[2 * at + half for at in range(chips)] for half in range(2)]
    swap = [(i, i ^ 1) for i in range(groups)]

    def exchange(x):
        return lax.all_to_all(
            x, "ctx", split_axis=0, concat_axis=0, tiled=True, axis_index_groups=peers
        )

    theirs = lax.ppermute(mine, "ctx", swap)
    sent, kept = combine(core, mine, theirs, chips)
    sent, conv = lax.optimization_barrier((sent, conv))
    gathered = exchange(sent)
    part = inner_part(
        small, rel, input_map, output_map, conv, jnp.repeat(skip, HD)[None, :]
    )
    gathered, part = lax.optimization_barrier((gathered, part))
    entering = scan_shards(chip, gathered, input_map.shape[1] // 16)
    entering, rel = lax.optimization_barrier((entering, rel))
    gain = prepare(rel, small, inner)
    arrived, gain = lax.optimization_barrier((exchange(entering), gain))
    send, keep = entering_halves(core, arrived, kept)
    got = lax.ppermute(send, "ctx", swap)
    return final(core, output_map, part, gain, keep, got)


def solution(mesh):
    in_specs = (
        P("ctx", "head"),
        P("ctx", None, "head"),
        P("ctx"),
        P(),
        P(None, "head"),
        P(),
        P(None, "head"),
        P(),
        P("head"),
        P(),
        P("head"),
    )
    out_specs = P("ctx", "head")
    return jax.shard_map(
        on_device, mesh=mesh, in_specs=in_specs, out_specs=out_specs, check_vma=False
    )
```

```python
import functools

import jax
import jax.numpy as jnp
from jax import lax
from jax.experimental import pallas as pl
from jax.experimental.pallas import tpu as pltpu
from jax.sharding import PartitionSpec as P

BF = jnp.bfloat16
F32 = jnp.float32
CAP = 16
BLK = 256
HD = 64
TILE = 256
HALO = 16
LANES = 128
ROWS_SENT = 88
DECAY_AT = 24
SMALL_END = 44
HIGH_AT, LOW_AT = 44, 108
PIECE = 24
TAKEN = 128


def iota(shape, dim):
    return lax.broadcasted_iota(jnp.int32, shape, dim)


def mm(a, b):
    return jnp.dot(a, b, preferred_element_type=F32)


def mm_nt(a, b):
    return lax.dot_general(a, b, (((1,), (1,)), ((), ())), preferred_element_type=F32)


def mm_tn(a, b):
    return lax.dot_general(a, b, (((0,), (0,)), ((), ())), preferred_element_type=F32)


def as_bf(mask):
    return jnp.where(mask, 1.0, 0.0).astype(BF)


def lower_ones(n):
    return as_bf(iota((n, n), 0) >= iota((n, n), 1))


def params(mib, flops=0, bytes_accessed=0):
    return dict(
        compiler_params=pltpu.CompilerParams(vmem_limit_bytes=mib * 1024 * 1024),
        cost_estimate=pl.CostEstimate(
            flops=flops, bytes_accessed=bytes_accessed, transcendentals=0
        ),
    )


def vmem(count):
    return [pl.BlockSpec(memory_space=pltpu.VMEM)] * count


def near(x):
    return pltpu.with_memory_space_constraint(x, pltpu.VMEM)


def far(x):
    return pltpu.with_memory_space_constraint(x, pltpu.HBM)


def hbm(count):
    return [pl.BlockSpec(memory_space=pltpu.HBM)] * count


def fetch(source, target, sem):
    copy = pltpu.make_async_copy(source, target, sem)
    copy.start()
    return copy


def pack_kernel(
    dest_hbm, steps_hbm, tok_hbm, out_ref,
    dest_ref, steps_ref, tok_ref, slot_ref, code_ref, small_ref, upper_ref,
    sems,
):
    get_dest = fetch(dest_hbm, dest_ref, sems.at[0])
    get_steps = fetch(steps_hbm, steps_ref, sems.at[1])
    rows, width = tok_hbm.shape
    get_tokens = fetch(tok_hbm, tok_ref.at[:, pl.ds(0, width)], sems.at[2])
    groups = code_ref.shape[0]
    heads = steps_ref.shape[0]
    per = 8
    slots = per * CAP
    upper_ref[...] = as_bf(iota((rows, rows), 0) <= iota((rows, rows), 1))
    small_ref[...] = jnp.zeros_like(small_ref)
    get_dest.wait()
    dest = dest_ref[...]
    target = dest // rows
    place = dest % rows + 1
    onehot = iota((groups, rows), 0) == target
    ranks = mm(as_bf(onehot), upper_ref[...])
    rank = jnp.sum(jnp.where(onehot, ranks, 0.0), axis=0, keepdims=True) - 1.0
    rank = rank.astype(jnp.int32)
    slot_ref[...] = target * CAP + rank
    line = iota((LANES, rows), 0)
    codes = jnp.where(line == HIGH_AT + rank, place // 256, 0)
    codes = codes + jnp.where(line == LOW_AT + rank, place % 256, 0)
    code_ref[...] = mm_nt(as_bf(onehot), codes.astype(F32).astype(BF))
    get_steps.wait()
    steps = steps_ref[...].astype(F32)
    small_ref[:heads] = steps[:, 0, :]
    small_ref[DECAY_AT : DECAY_AT + heads] = steps[:, 1, :]
    tok_ref[:, width:] = small_ref[...].T.astype(BF)
    get_tokens.wait()

    def body(step, _):
        slot = slot_ref[...] - step * slots
        here = pl.ds(pl.multiple_of(step * per, per), per)
        select = as_bf(iota((slots, rows), 0) == slot)
        both = mm(select, tok_ref[...])
        sent = both[:, :width].astype(BF)
        for column in range(width // LANES):
            out_ref[here, column * CAP : (column + 1) * CAP, :] = sent[
                :, column * LANES : (column + 1) * LANES
            ].reshape(per, CAP, LANES)
        half = CAP // 2
        small = both[:, width:].reshape(per, CAP, LANES)
        pairs = small[:, :half, :] + pltpu.roll(small[:, half:, :], LANES // 2, 2)
        first = iota((per, half, LANES), 1) == 0
        pairs = pairs + jnp.where(first, code_ref[here][:, None, :], 0.0)
        out_ref[here, ROWS_SENT - half :, :] = pairs.astype(BF)
        return 0

    lax.fori_loop(0, groups // per, body, 0, unroll=8)


def pack(dest, tokens, steps, groups):
    rows, width = tokens.shape
    return pl.pallas_call(
        pack_kernel,
        in_specs=hbm(3),
        out_specs=pl.BlockSpec(memory_space=pltpu.VMEM),
        out_shape=jax.ShapeDtypeStruct((groups, ROWS_SENT, LANES), BF),
        scratch_shapes=[
            pltpu.VMEM((1, rows), jnp.int32),
            pltpu.VMEM(steps.shape, BF),
            pltpu.VMEM((rows, width + LANES), BF),
            pltpu.VMEM((1, rows), jnp.int32),
            pltpu.VMEM((groups, LANES), F32),
            pltpu.VMEM((LANES, rows), F32),
            pltpu.VMEM((rows, rows), BF),
            pltpu.SemaphoreType.DMA((3,)),
        ],
        name="pack",
        **params(16, 2 * rows * groups * CAP * (width + LANES), 4 * rows * width),
    )(far(dest), far(steps), far(tokens))


def places(row_codes, groups, lane_slot, lane_group, count):
    line = iota((LANES, count), 0)
    table = jnp.where(
        line == HIGH_AT + lane_slot, 256.0, jnp.where(line == LOW_AT + lane_slot, 1.0, 0.0)
    ).astype(BF)
    wide = mm(row_codes, table)
    mine = iota((groups, count), 0) == lane_group
    return jnp.sum(jnp.where(mine, wide, 0.0), axis=0, keepdims=True).astype(jnp.int32)


def pick(pos, first, rows):
    return as_bf(iota((rows, pos.shape[1]), 0) + (first + 1) == pos)


def take(select, recv_ref, target, first_row):
    groups = recv_ref.shape[0]
    rows = select.shape[0]
    for column in range(target.shape[1] // LANES):
        source = recv_ref[:, column * CAP : (column + 1) * CAP, :]
        target[first_row : first_row + rows, column * LANES : (column + 1) * LANES] = mm(
            select, source.reshape(groups * CAP, LANES)
        ).astype(BF)


def paired_rows(recv_ref, rows_ref):
    groups = recv_ref.shape[0]
    half = CAP // 2
    pairs = recv_ref[:, ROWS_SENT - half :, :].astype(F32)
    both = jnp.concatenate([pairs, pltpu.roll(pairs, LANES // 2, 2)], axis=1)
    rows_ref[...] = both.reshape(groups * CAP, LANES).astype(BF)
    return pairs[:, 0, :].astype(BF)


def take_small(select, rows_ref):
    values = mm(select, rows_ref[...])
    valid = iota(values.shape, 1) < SMALL_END
    return jnp.where(valid, values, 0.0).astype(BF)


def unpack_low_kernel(
    recv_ref, low_ref, pos_ref, small_hbm, rows_ref, small_ref, sem
):
    groups = recv_ref.shape[0]
    rows = 2 * low_ref.shape[0]
    codes = paired_rows(recv_ref, rows_ref)
    lane = iota((1, groups * CAP), 1)
    pos = places(codes, groups, lane % CAP, lane // CAP, groups * CAP)
    pos_ref[...] = pos
    select = pick(pos, 0, rows // 2)
    small_ref[...] = take_small(select, rows_ref)
    put = fetch(small_ref, small_hbm, sem)
    take(select, recv_ref, low_ref, 0)
    put.wait()


def unpack_high_kernel(
    recv_ref, pos_ref, high_ref, edge_ref, small_hbm, rows_ref, small_ref, sem
):
    rows = high_ref.shape[0] - HALO
    paired_rows(recv_ref, rows_ref)
    select = pick(pos_ref[...], rows, rows)
    small_ref[...] = take_small(select, rows_ref)
    put = fetch(small_ref, small_hbm, sem)
    high_ref[:HALO] = jnp.zeros((HALO, high_ref.shape[1]), BF)
    take(select, recv_ref, high_ref, HALO)
    edge_ref[...] = high_ref[rows:]
    put.wait()


def unpack(recv, width, rows):
    groups = recv.shape[0]
    slots = groups * CAP
    half = rows // 2
    scratch = [
        pltpu.VMEM((slots, LANES), BF),
        pltpu.VMEM((half, LANES), BF),
        pltpu.SemaphoreType.DMA,
    ]
    low, pos, small_low = pl.pallas_call(
        unpack_low_kernel,
        in_specs=vmem(1),
        out_specs=vmem(2) + hbm(1),
        out_shape=[
            jax.ShapeDtypeStruct((half, width), BF),
            jax.ShapeDtypeStruct((1, slots), jnp.int32),
            pltpu.HBM((half, LANES), BF),
        ],
        scratch_shapes=scratch,
        name="unpack_low",
        **params(12, rows * slots * width, 3 * rows * width),
    )(recv)
    high, edge, small_high = pl.pallas_call(
        unpack_high_kernel,
        in_specs=vmem(2),
        out_specs=vmem(2) + hbm(1),
        out_shape=[
            jax.ShapeDtypeStruct((half + HALO, width), BF),
            jax.ShapeDtypeStruct((HALO, width), BF),
            pltpu.HBM((half, LANES), BF),
        ],
        scratch_shapes=scratch,
        name="unpack_high",
        **params(12, rows * slots * width, 3 * rows * width),
    )(recv, pos)
    return low, edge, high, (small_low, small_high)


def conv_silu(ext_ref, weight, bias, rel, rows):
    taps = weight.shape[0]
    total = bias + weight[taps - 1 : taps] * ext_ref[HALO : HALO + rows]
    for lag in range(1, taps):
        tap = taps - 1 - lag
        shifted = ext_ref[HALO - lag : HALO - lag + rows]
        total = total + jnp.where(rel >= lag, weight[tap : tap + 1] * shifted, 0.0)
    return jax.nn.silu(total).astype(BF)


def head_spread(tile, first):
    per = TILE // HD
    return as_bf(iota((128, TILE), 0) == first + per * tile + iota((128, TILE), 1) // HD)


def piece_tiles(dest):
    base = dest // 2 * 5
    first = (base, base + 1) if dest % 2 == 0 else (base + 3, base + 4)
    return first + (base + 2,)


def decay_kernel(
    rel_ref, low_hbm, high_hbm, steps_hbm, tail_hbm, carry_ref,
    small_ref, steps_ref, tail_ref, gets, puts,
):
    tiles, rows = tail_ref.shape[0], tail_ref.shape[1]
    half = rows // 2
    copies = [
        fetch(low_hbm, small_ref.at[pl.ds(0, half)], gets.at[0]),
        fetch(high_hbm, small_ref.at[pl.ds(half, half)], gets.at[1]),
    ]
    for copy in copies:
        copy.wait()
    ones = lower_ones(BLK)
    rel = rel_ref[...]

    def body(tile, _):
        small = small_ref[...]
        steps_ref[tile] = mm(small, head_spread(tile, 0)).astype(BF)
        decays = mm(small, head_spread(tile, DECAY_AT)).astype(BF)
        reach, lines = None, []
        for block in range(rows // BLK):
            span = slice(block * BLK, (block + 1) * BLK)
            cumulative = mm(ones, decays[span])
            last = rel[(block + 1) * BLK - 1 : (block + 1) * BLK]
            end = cumulative[BLK - 1 : BLK]
            behind = BLK - 1 - iota((BLK, 1), 0)
            tail_ref[tile, span] = jnp.where(behind <= last, jnp.exp(end - cumulative), 0.0)
            carry = jnp.where(last > BLK - 1, jnp.exp(end), 0.0)
            lines.append(carry)
            reach = carry if reach is None else reach * carry
        lines.append(reach)
        lines.append(jnp.zeros((8 - len(lines), TILE), F32))
        carry_ref[tile] = jnp.concatenate(lines, axis=0)
        pltpu.make_async_copy(steps_ref.at[tile], steps_hbm.at[tile], puts.at[tile]).start()
        pltpu.make_async_copy(
            tail_ref.at[tile], tail_hbm.at[tile], puts.at[tiles + tile]
        ).start()
        return 0

    lax.fori_loop(0, tiles, body, 0)
    for tile in range(tiles):
        pltpu.make_async_copy(steps_ref.at[tile], steps_hbm.at[tile], puts.at[tile]).wait()
        pltpu.make_async_copy(
            tail_ref.at[tile], tail_hbm.at[tile], puts.at[tiles + tile]
        ).wait()


def decay_factors(rel, small, inner):
    rows = rel.shape[0]
    tiles = inner // TILE
    return pl.pallas_call(
        decay_kernel,
        in_specs=vmem(1) + hbm(2),
        out_specs=hbm(2) + vmem(1),
        out_shape=[
            pltpu.HBM((tiles, rows, TILE), BF),
            pltpu.HBM((tiles, rows, TILE), F32),
            jax.ShapeDtypeStruct((tiles, 8, TILE), F32),
        ],
        scratch_shapes=[
            pltpu.VMEM((rows, LANES), BF),
            pltpu.VMEM((tiles, rows, TILE), BF),
            pltpu.VMEM((tiles, rows, TILE), F32),
            pltpu.SemaphoreType.DMA((2,)),
            pltpu.SemaphoreType.DMA((2 * tiles,)),
        ],
        name="decay_factors",
        **params(16, 4 * rows * BLK * inner, 7_000_000),
    )(rel, *[far(x) for x in small])


def assemble(xe_ref, low_ref, high_ref, columns):
    half = low_ref.shape[0]
    xe_ref[:HALO, columns] = high_ref[:HALO]
    xe_ref[HALO : HALO + half, columns] = low_ref[...]
    xe_ref[HALO + half :, columns] = high_ref[HALO:]


def own_kernel(
    me_ref, low_ref, high_ref, w_hbm, wbc_hbm,
    total_ref, left_ref, right_ref, far_ref, xe_ref, w_ref, gets,
):
    width = low_ref.shape[1]
    inner, rest = w_hbm.shape[1], wbc_hbm.shape[1]
    copies = []
    for turn, target in enumerate((w_ref, left_ref, far_ref, right_ref)):
        owner = lax.rem(me_ref[0] + 4 - turn, 4)
        lines = pl.ds(pl.multiple_of(owner * width, width), width)
        copies.append(
            (
                fetch(w_hbm.at[lines], target.at[:, pl.ds(0, inner)], gets.at[turn, 0]),
                fetch(wbc_hbm.at[lines], target.at[:, pl.ds(inner, rest)], gets.at[turn, 1]),
            )
        )
    assemble(xe_ref, low_ref, high_ref, slice(None))
    for copy in copies[0]:
        copy.wait()

    def body(tile, _):
        columns = pl.ds(pl.multiple_of(tile * TILE, TILE), TILE)
        total_ref[:, columns] = mm(xe_ref[...], w_ref[:, columns])
        return 0

    lax.fori_loop(0, total_ref.shape[1] // TILE, body, 0)
    for pair in copies[1:]:
        for copy in pair:
            copy.wait()


def project_own(me, low, high, w_x, w_bc):
    half, width = low.shape
    rows = 2 * half + HALO
    full = w_x.shape[1] + w_bc.shape[1]
    return pl.pallas_call(
        own_kernel,
        in_specs=[pl.BlockSpec(memory_space=pltpu.SMEM)] + vmem(2) + hbm(2),
        out_specs=vmem(4),
        out_shape=[pltpu.VMEM((rows, full), F32)] + [pltpu.VMEM((width, full), BF)] * 3,
        scratch_shapes=[
            pltpu.VMEM((rows, width), BF),
            pltpu.VMEM((width, full), BF),
            pltpu.SemaphoreType.DMA((4, 2)),
        ],
        name="project_own",
        **params(8, 2 * rows * width * full, 8_000_000),
    )(me, near(low), near(high), far(w_x), far(w_bc))


def near_kernel(
    low1, high1, low3, high3, left_ref, right_ref, sofar_ref, total_ref, xe_ref
):
    width = low1.shape[1]
    assemble(xe_ref, low1, high1, slice(0, width))
    assemble(xe_ref, low3, high3, slice(width, 2 * width))

    def body(tile, _):
        columns = pl.ds(pl.multiple_of(tile * TILE, TILE), TILE)
        weights = jnp.concatenate([left_ref[:, columns], right_ref[:, columns]], axis=0)
        total_ref[:, columns] = sofar_ref[:, columns] + mm(xe_ref[...], weights)
        return 0

    lax.fori_loop(0, total_ref.shape[1] // TILE, body, 0)


def project_near(left, right, w_left, w_right, total):
    width = left[0].shape[1]
    rows, full = total.shape
    return pl.pallas_call(
        near_kernel,
        in_specs=vmem(7),
        out_specs=vmem(1)[0],
        out_shape=pltpu.VMEM((rows, full), F32),
        scratch_shapes=[pltpu.VMEM((rows, 2 * width), BF)],
        name="project_near",
        **params(6, 4 * rows * width * full, 8_000_000),
    )(*[near(x) for x in (*left, *right, w_left, w_right, total)])


def piece_tiles(dest):
    base = dest // 2 * 5
    first = (base, base + 1) if dest % 2 == 0 else (base + 3, base + 4)
    return first + (base + 2,)


def front_kernel(
    low_ref, high_ref, total_ref, w_ref, rel_ref, carry_ref, cx_ref, bx_ref, cb_ref, bb_ref,
    steps_hbm, tail_hbm,
    conv_hbm, mine_ref, in_ref, outmap_ref,
    steps_ref, tail_ref, conv_ref, across_ref,
    xe_ref, ext_ref, gets, puts,
):
    half, width = low_ref.shape
    rows = 2 * half
    states = in_ref.shape[1]
    tiles = conv_ref.shape[0]
    inner = tiles * TILE
    for tile in range(tiles):
        fetch(steps_hbm.at[tile], steps_ref.at[tile], gets.at[0, tile])
        fetch(tail_hbm.at[tile], tail_ref.at[tile], gets.at[1, tile])
    assemble(xe_ref, low_ref, high_ref, slice(None))

    def project(tile):
        columns = slice(tile * TILE, (tile + 1) * TILE)
        total = total_ref[:, columns] + mm(xe_ref[...], w_ref[:, columns])
        ext_ref[tile] = total.astype(BF).astype(F32)

    rel = rel_ref[...]
    for tile in range(tiles + 1):
        project(tile)
    both = conv_silu(ext_ref.at[tiles], cb_ref[...], bb_ref[...], rel, rows)
    in_ref[...] = both[:, :states]
    outmap_ref[...] = both[:, states:]
    across_ref[...] = both[:, :states].astype(F32).T.astype(BF)
    for tile in range(tiles):
        columns = slice(tile * TILE, (tile + 1) * TILE)
        inner_rows = conv_silu(ext_ref.at[tile], cx_ref[:, columns], bx_ref[:, columns], rel, rows)
        conv_ref[tile] = inner_rows
        fetch(conv_ref.at[tile], conv_hbm.at[:, pl.ds(tile * TILE, TILE)], puts.at[2 + tile])
        for at, (source, target) in enumerate(((steps_hbm, steps_ref), (tail_hbm, tail_ref))):
            pltpu.make_async_copy(source.at[tile], target.at[tile], gets.at[at, tile]).wait()
        inject = (inner_rows.astype(F32) * steps_ref[tile].astype(F32)).astype(BF)
        decayed = (tail_ref[tile] * inject.astype(F32)).astype(BF)
        carried = None
        for block in range(rows // BLK):
            span = slice(block * BLK, (block + 1) * BLK)
            block_state = mm(across_ref[:, span], decayed[span])
            if carried is None:
                carried = block_state
            else:
                carried = carry_ref[tile, block : block + 1] * carried + block_state
        mine_ref[:states, columns] = carried.astype(BF)
        reach = carry_ref[tile, rows // BLK : rows // BLK + 1]
        high = reach.astype(BF).astype(F32)
        line = iota((HALO, TILE), 0)
        codes = jnp.where(line == 0, high, jnp.where(line == 1, reach - high, 0.0))
        mine_ref[states:, columns] = codes.astype(BF)
    for tile in range(tiles):
        pltpu.make_async_copy(
            conv_ref.at[tile], conv_hbm.at[:, pl.ds(tile * TILE, TILE)], puts.at[2 + tile]
        ).wait()


def front(piece, total, w_far, rel, carry, steps, tail, conv_x, bias_x, conv_bc, bias_bc):
    half, width = piece[0].shape
    rows = 2 * half
    inner = conv_x.shape[1]
    states = conv_bc.shape[1] // 2
    tiles = inner // TILE
    return pl.pallas_call(
        front_kernel,
        in_specs=vmem(10) + hbm(2),
        out_specs=hbm(1) + vmem(3),
        out_shape=[
            pltpu.HBM((rows, inner), BF),
            jax.ShapeDtypeStruct((states + HALO, inner), BF),
            pltpu.VMEM((rows, states), BF),
            pltpu.VMEM((rows, states), BF),
        ],
        scratch_shapes=[
            pltpu.VMEM(steps.shape, BF),
            pltpu.VMEM(tail.shape, F32),
            pltpu.VMEM((tiles, rows, TILE), BF),
            pltpu.VMEM((states, rows), BF),
            pltpu.VMEM((rows + HALO, width), BF),
            pltpu.VMEM((tiles + 1, rows + HALO, TILE), F32),
            pltpu.SemaphoreType.DMA((2, tiles)),
            pltpu.SemaphoreType.DMA((tiles + 2,)),
        ],
        name="front",
        **params(20, 2 * rows * width * (inner + 2 * states), 12_000_000),
    )(
        *[near(x) for x in (*piece, total, w_far)], rel, carry,
        conv_x, bias_x, conv_bc, bias_bc, far(steps), far(tail),
    )


def combine_kernel(
    core_ref, mine_ref, theirs_ref, sent_ref, kept_ref, chip_ref, gain_ref
):
    half, inner = chip_ref.shape
    states = 2 * half
    lines = half // 8
    first = core_ref[0] == 0
    span = pl.ds(pl.multiple_of(core_ref[0] * half, half), half)
    own, other = mine_ref[span].astype(F32), theirs_ref[span].astype(F32)
    own_codes, other_codes = mine_ref[states:].astype(F32), theirs_ref[states:].astype(F32)
    early = jnp.where(first, own, other)
    early_codes = jnp.where(first, own_codes, other_codes)
    late_codes = jnp.where(first, other_codes, own_codes)
    kept_ref[:half] = early.astype(BF)
    kept_ref[half:] = early_codes.astype(BF)
    early_gain = early_codes[0:1] + early_codes[1:2]
    late_gain = late_codes[0:1] + late_codes[1:2]
    chip_ref[...] = late_gain * early + jnp.where(first, other, own)
    gain_ref[...] = jnp.broadcast_to(early_gain * late_gain, gain_ref.shape)

    def tile_of(index):
        column, line = index // lines, index % lines
        return chip_ref[line * 8 : line * 8 + 8, column * LANES : (column + 1) * LANES]

    def codes_of(column):
        gain = gain_ref[0:1, column * LANES : (column + 1) * LANES]
        high = gain.astype(BF).astype(F32)
        return high, gain - high

    for dest in range(sent_ref.shape[0]):
        one, two, shared = piece_tiles(dest)
        columns = [index // lines for index in (one, two, shared)]
        middle = tile_of(shared)[4 * (dest % 2) : 4 * (dest % 2) + 4]
        piece = [tile_of(one), tile_of(two), middle]
        piece += [*codes_of(min(columns)), *codes_of(max(columns))]
        sent_ref[dest] = jnp.concatenate(piece, axis=0).astype(BF)


def combine(core, mine, theirs, chips):
    inner = mine.shape[1]
    half = (mine.shape[0] - HALO) // 2
    return pl.pallas_call(
        combine_kernel,
        in_specs=[pl.BlockSpec(memory_space=pltpu.SMEM)] + vmem(2),
        out_specs=vmem(2),
        out_shape=[
            jax.ShapeDtypeStruct((chips, PIECE, LANES), BF),
            pltpu.VMEM((half + HALO, inner), BF),
        ],
        scratch_shapes=[
            pltpu.VMEM((half, inner), F32),
            pltpu.VMEM((8, inner), F32),
        ],
        name="combine",
        **params(8, 1_000_000, 1_500_000),
    )(core, near(mine), near(theirs))


def entering_kernel(core_ref, recv_ref, kept_ref, send_ref, keep_ref, enter_ref):
    half, inner = enter_ref.shape
    lines = half // 8
    where = {}
    for dest in range(recv_ref.shape[0]):
        one, two, shared = piece_tiles(dest)
        where[one] = (dest, 0)
        where[two] = (dest, 1)
        where.setdefault(shared, dest)

    def tile_of(index):
        if isinstance(where[index], tuple):
            dest, at = where[index]
            return recv_ref[dest].astype(F32)[8 * at : 8 * at + 8]
        dest = where[index]
        upper = recv_ref[dest].astype(F32)[16:20]
        lower = recv_ref[dest + 1].astype(F32)[16:20]
        return jnp.concatenate([upper, lower], axis=0)

    for index in range(lines * inner // LANES):
        column, line = index // lines, index % lines
        enter_ref[line * 8 : line * 8 + 8, column * LANES : (column + 1) * LANES] = tile_of(index)
    first = core_ref[0] == 0
    codes = kept_ref[half:].astype(F32)
    early = enter_ref[...]
    late = (codes[0:1] + codes[1:2]) * early + kept_ref[:half].astype(F32)
    send_ref[...] = jnp.where(first, late, early).astype(BF)
    keep_ref[...] = jnp.where(first, early, late).astype(BF)


def entering_halves(core, recv, kept):
    rows, inner = kept.shape
    half = rows - HALO
    return pl.pallas_call(
        entering_kernel,
        in_specs=[pl.BlockSpec(memory_space=pltpu.SMEM)] + vmem(2),
        out_specs=vmem(2),
        out_shape=[jax.ShapeDtypeStruct((half, inner), BF)] * 2,
        scratch_shapes=[pltpu.VMEM((half, inner), F32)],
        name="entering_halves",
        **params(8, 1_000_000, 1_500_000),
    )(core, near(recv), near(kept))


def inner_kernel(
    rel_ref, skip_ref, outmap_ref, in_ref, low_hbm, high_hbm, conv_hbm, part_hbm,
    small_ref, conv_ref, part_ref,
    scores_ref, across_ref, turned_ref, gets, puts,
):
    half = low_hbm.shape[0]
    rows, inner = conv_ref.shape
    tiles = inner // TILE
    per = TILE // HD
    first = [
        fetch(source, target, gets.at[tiles + at])
        for at, (source, target) in enumerate(
            (
                (low_hbm, small_ref.at[pl.ds(0, half)]),
                (high_hbm, small_ref.at[pl.ds(half, half)]),
            )
        )
    ]
    for tile in range(tiles):
        columns = pl.ds(tile * TILE, TILE)
        fetch(conv_hbm.at[:, columns], conv_ref.at[:, columns], gets.at[tile])
    for copy in first:
        copy.wait()
    ones = lower_ones(BLK)
    for block in range(rows // BLK):
        span = slice(block * BLK, (block + 1) * BLK)
        scores = mm_nt(outmap_ref[span], in_ref[span])
        gap = iota((BLK, BLK), 0) - iota((BLK, BLK), 1)
        keep = (gap >= 0) & (gap <= rel_ref[span])
        scores_ref[block] = jnp.where(keep, scores, 0.0)
        across_ref[block] = mm(ones, small_ref[span]).T
    turned_ref[...] = in_ref[...].astype(F32).T.astype(BF)

    def body(tile, _):
        columns = pl.ds(pl.multiple_of(tile * TILE, TILE), TILE)
        pltpu.make_async_copy(
            conv_hbm.at[:, columns], conv_ref.at[:, columns], gets.at[tile]
        ).wait()
        small = small_ref[...]
        steps = mm(small, head_spread(tile, 0))
        decays = mm(small, head_spread(tile, DECAY_AT)).astype(BF)
        conv = conv_ref[:, columns].astype(F32)
        inject = (conv * steps).astype(BF)
        lane_head = iota((BLK, TILE), 1) // HD
        state = None
        for block in range(rows // BLK):
            span = slice(block * BLK, (block + 1) * BLK)
            cumulative = mm(ones, decays[span])
            scores = scores_ref[block]
            total = skip_ref[:, columns] * conv[span]
            if block > 0:
                enter = jnp.where(
                    iota((BLK, 1), 0) < rel_ref[span], jnp.exp(cumulative), 0.0
                )
                total = total + enter * mm(outmap_ref[span], state.astype(BF))
            if (block + 1) * BLK < rows:
                last = rel_ref[(block + 1) * BLK - 1 : (block + 1) * BLK]
                end = cumulative[BLK - 1 : BLK]
                behind = BLK - 1 - iota((BLK, 1), 0)
                tail = jnp.where(behind <= last, jnp.exp(end - cumulative), 0.0)
                decayed = (tail * inject[span].astype(F32)).astype(BF)
                block_state = mm(turned_ref[:, span], decayed)
                carry = jnp.where(last > BLK - 1, jnp.exp(end), 0.0)
                state = block_state if state is None else carry * state + block_state
            part = BLK // 2
            pieces = [total[:part], total[part:]]
            for q in range(per):
                down = cumulative[:, q * HD : q * HD + 1]
                across = across_ref[block, pl.ds(DECAY_AT + per * tile + q, 1), :]
                mine = jnp.where(lane_head == q, inject[span], jnp.zeros((), BF))
                for at, seen in ((0, part), (1, BLK)):
                    lines = slice(at * part, (at + 1) * part)
                    gap = jnp.minimum(down[lines] - across[:, :seen], 0.0)
                    weights = (scores[lines, :seen] * jnp.exp(gap)).astype(BF)
                    pieces[at] = pieces[at] + mm(weights, mine[:seen])
            total = jnp.concatenate(pieces, axis=0)
            part_ref[span, columns] = total
        pltpu.make_async_copy(
            part_ref.at[:, columns], part_hbm.at[:, columns], puts.at[tile]
        ).start()
        return 0

    lax.fori_loop(0, tiles, body, 0)
    for tile in range(tiles):
        columns = pl.ds(tile * TILE, TILE)
        pltpu.make_async_copy(
            part_ref.at[:, columns], part_hbm.at[:, columns], puts.at[tile]
        ).wait()


def inner_part(small, rel, input_map, output_map, conv, skip_wide):
    rows, inner = conv.shape
    blocks = rows // BLK
    tiles = inner // TILE
    return pl.pallas_call(
        inner_kernel,
        in_specs=vmem(4) + hbm(3),
        out_specs=hbm(1)[0],
        out_shape=pltpu.HBM((rows, inner), F32),
        scratch_shapes=[
            pltpu.VMEM((rows, LANES), BF),
            pltpu.VMEM(conv.shape, BF),
            pltpu.VMEM((rows, inner), F32),
            pltpu.VMEM((blocks, BLK, BLK), F32),
            pltpu.VMEM((blocks, 128, BLK), F32),
            pltpu.VMEM((input_map.shape[1], rows), BF),
            pltpu.SemaphoreType.DMA((tiles + 3,)),
            pltpu.SemaphoreType.DMA((tiles,)),
        ],
        name="inner_part",
        **params(24, 8 * rows * BLK * inner, 8_000_000),
    )(rel, skip_wide, near(output_map), near(input_map), *[far(x) for x in (*small, conv)])


def scan_kernel(lines, me_ref, recv_ref, out_ref):
    groups = recv_ref.shape[0]
    me = me_ref[0]
    base = me // 2 * 5
    odd = lax.rem(me, 2)
    columns = [(base + 3 * odd) // lines, (base + 1 + 3 * odd) // lines, (base + 2) // lines]
    least = jnp.minimum(jnp.minimum(columns[0], columns[1]), columns[2])
    near_first = [
        jnp.where(jnp.full((8, LANES), column, jnp.int32) == least, 1.0, 0.0) for column in columns
    ]

    def body(shard, state):
        piece = recv_ref[shard].astype(F32)
        out_ref[shard] = jnp.concatenate(state, axis=0).astype(BF)
        gain_a = piece[20:21] + piece[21:22]
        gain_b = piece[22:23] + piece[23:24]
        return tuple(
            jnp.where(first > 0.5, gain_a, gain_b) * old + piece[8 * at : 8 * at + 8]
            for at, (first, old) in enumerate(zip(near_first, state))
        )

    lax.fori_loop(0, groups, body, (jnp.zeros((8, LANES), F32),) * 3, unroll=4)


def scan_shards(me, recv, lines):
    return pl.pallas_call(
        functools.partial(scan_kernel, lines),
        in_specs=[pl.BlockSpec(memory_space=pltpu.SMEM)] + vmem(1),
        out_specs=pl.BlockSpec(memory_space=pltpu.VMEM),
        out_shape=pltpu.VMEM(recv.shape, BF),
        name="scan_shards",
        **params(8, 10_000_000, 800_000),
    )(me, near(recv))


def prepare_kernel(
    rel_ref, low_hbm, high_hbm, gain_ref,
    small_ref, ones_ref, sems,
):
    rows, inner = gain_ref.shape
    half = rows // 2
    get_small = [
        fetch(low_hbm, small_ref.at[pl.ds(0, half)], sems.at[0]),
        fetch(high_hbm, small_ref.at[pl.ds(half, half)], sems.at[1]),
    ]
    ones_ref[...] = lower_ones(rows)
    reached = iota((rows, 1), 0) < rel_ref[...]
    for copy in get_small:
        copy.wait()

    def body(tile, _):
        decays = mm(small_ref[...], head_spread(tile, DECAY_AT)).astype(BF)
        cumulative = mm(ones_ref[...], decays)
        gain_ref[:, pl.ds(pl.multiple_of(tile * TILE, TILE), TILE)] = jnp.where(
            reached, jnp.exp(cumulative), 0.0
        )
        return 0

    lax.fori_loop(0, inner // TILE, body, 0)


def prepare(rel, small, inner):
    rows = rel.shape[0]
    return pl.pallas_call(
        prepare_kernel,
        in_specs=vmem(1) + hbm(2),
        out_specs=vmem(1)[0],
        out_shape=pltpu.VMEM((rows, inner), F32),
        scratch_shapes=[
            pltpu.VMEM((rows, LANES), BF),
            pltpu.VMEM((rows, rows), BF),
            pltpu.SemaphoreType.DMA((2,)),
        ],
        name="prepare",
        **params(8, 2 * rows * rows * inner, 8_000_000),
    )(rel, *[far(x) for x in small])


def final_kernel(
    core_ref, keep_ref, got_ref, gain_ref, outmap_ref, part_hbm, out_hbm,
    part_ref, enter_ref, held_ref, gets, puts,
):
    rows, inner = part_ref.shape
    half = keep_ref.shape[0]
    steps = rows // TAKEN
    spans = [pl.ds(step * TAKEN, TAKEN) for step in range(steps)]
    copies = [
        fetch(part_hbm.at[span], part_ref.at[span], gets.at[step])
        for step, span in enumerate(spans)
    ]
    core = core_ref[0]
    enter_ref[pl.ds(pl.multiple_of(core * half, half), half)] = keep_ref[...]
    enter_ref[pl.ds(pl.multiple_of((1 - core) * half, half), half)] = got_ref[...]
    puts_made = []
    for step, span in enumerate(spans):
        outer = mm(outmap_ref[span], enter_ref[...])
        copies[step].wait()
        held_ref[span] = (part_ref[span] + gain_ref[span] * outer).astype(BF)
        puts_made.append(fetch(held_ref.at[span], out_hbm.at[span], puts.at[step]))
    for copy in puts_made:
        copy.wait()


def final(core, output_map, part, gain, keep, got):
    rows, inner = part.shape
    states = output_map.shape[1]
    return pl.pallas_call(
        final_kernel,
        in_specs=[pl.BlockSpec(memory_space=pltpu.SMEM)] + vmem(4) + hbm(1),
        out_specs=hbm(1)[0],
        out_shape=jax.ShapeDtypeStruct((rows, inner), BF),
        scratch_shapes=[
            pltpu.VMEM((rows, inner), F32),
            pltpu.VMEM((states, inner), BF),
            pltpu.VMEM((rows, inner), BF),
            pltpu.SemaphoreType.DMA((rows // TAKEN,)),
            pltpu.SemaphoreType.DMA((rows // TAKEN,)),
        ],
        name="final",
        **params(16, 2 * rows * states * inner, 7_000_000),
    )(core, near(keep), near(got), near(gain), near(output_map), far(part))


def on_device(tokens, dt_decay, dest, lengths, w_x, w_bc, conv_x, conv_bc, bias_x, bias_bc, skip):
    rows, width = tokens.shape
    groups = lax.axis_size("ctx")
    ring = lax.axis_size("head")
    first_pos = lax.axis_index("ctx") * rows

    sent = pack(dest[None, :], tokens, jnp.transpose(dt_decay, (2, 1, 0)), groups)
    arrived = lax.all_to_all(sent, "ctx", split_axis=0, concat_axis=0, tiled=True)
    low, edge, high, small = unpack(arrived, width, rows)

    def turned(x, by):
        return lax.ppermute(x, "head", [(i, (i + by) % ring) for i in range(ring)])

    low_left, low_right = turned(low, 1), turned(low, ring - 1)
    halo = lax.ppermute(edge, "ctx", [(i, i + 1) for i in range(groups - 1)])
    high = lax.dynamic_update_slice(high, halo, (0, 0))
    high_right = turned(high, ring - 1)

    starts = jnp.cumsum(lengths) - lengths
    positions = first_pos + jnp.arange(rows, dtype=jnp.int32)
    doc_start = jnp.max(
        jnp.where(starts[None, :] <= positions[:, None], starts[None, :], 0), axis=1
    )
    rel = (positions - doc_start)[:, None]
    me = lax.axis_index("head").astype(jnp.int32)[None]
    inner = w_x.shape[1]
    steps, tail, carry = decay_factors(rel, small, inner)
    later, carry = lax.optimization_barrier((high, carry))
    high_left = turned(later, 1)
    low_far, high_far = turned(low_left, 1), turned(high_right, ring - 1)
    total, w_left, w_right, w_far = project_own(me, low, high, w_x, w_bc)
    total = project_near(
        (low_left, high_left), (low_right, high_right), w_left, w_right, total
    )
    conv, mine, input_map, output_map = front(
        (low_far, high_far), total, w_far, rel, carry, steps, tail,
        conv_x, bias_x[None, :], conv_bc, bias_bc[None, :],
    )
    place = lax.axis_index("ctx").astype(jnp.int32)
    core, chip = (place % 2)[None], (place // 2)[None]
    chips = groups // 2
    peers = [[2 * at + half for at in range(chips)] for half in range(2)]
    swap = [(i, i ^ 1) for i in range(groups)]

    def exchange(x):
        return lax.all_to_all(
            x, "ctx", split_axis=0, concat_axis=0, tiled=True, axis_index_groups=peers
        )

    theirs = lax.ppermute(mine, "ctx", swap)
    sent, kept = combine(core, mine, theirs, chips)
    sent, conv = lax.optimization_barrier((sent, conv))
    gathered = exchange(sent)
    part = inner_part(
        small, rel, input_map, output_map, conv, jnp.repeat(skip, HD)[None, :]
    )
    gathered, part = lax.optimization_barrier((gathered, part))
    entering = scan_shards(chip, gathered, input_map.shape[1] // 16)
    entering, rel = lax.optimization_barrier((entering, rel))
    gain = prepare(rel, small, inner)
    arrived, gain = lax.optimization_barrier((exchange(entering), gain))
    send, keep = entering_halves(core, arrived, kept)
    got = lax.ppermute(send, "ctx", swap)
    return final(core, output_map, part, gain, keep, got)


def solution(mesh):
    in_specs = (
        P("ctx", "head"),
        P("ctx", None, "head"),
        P("ctx"),
        P(),
        P(None, "head"),
        P(),
        P(None, "head"),
        P(),
        P("head"),
        P(),
        P("head"),
    )
    out_specs = P("ctx", "head")
    return jax.shard_map(
        on_device, mesh=mesh, in_specs=in_specs, out_specs=out_specs, check_vma=False
    )
```
